32 devices in a mesh: dp: 4 (over x, core), seq: 8 (over z, y).
Axes of the slice: x: 2, y: 2, z: 4, core: 2. Of those that a mesh axis runs over, the one named last changes fastest.
Arguments:
- tokens: bfloat16 [4, 1024, 1536], P('dp', 'seq'), may hold values from -6 to 6
- upstream: bfloat16 [4, 1024, 1536], P('dp', 'seq'), may hold values from -6 to 6
- conv_value: float32 [3, 1536], replicated, may hold values from -3.5 to 3.5
- conv_gate: float32 [3, 1536], replicated, may hold values from -3.5 to 3.5
- mix_one: bfloat16 [2, 8, 128, 128], P(None, 'seq'), may hold values from -0.375 to 0.375
- mix_two: bfloat16 [2, 128, 8, 8], P(None, 'seq'), may hold values from -1.5 to 1.5
- mix_three: bfloat16 [2, 128, 8, 8], P(None, 'seq'), may hold values from -1.5 to 1.5
- mix_four: bfloat16 [2, 8, 128, 128], P(None, 'seq'), may hold values from -0.375 to 0.375
- filter_log: bfloat16 [128, 8, 1536], P('seq'), may hold values from -2.5 to 2.5
Outputs:
- grad_x: bfloat16 [4, 1024, 1536], P('dp', 'seq')
- grad_conv_value: float32 [3, 1536], replicated
- grad_conv_gate: float32 [3, 1536], replicated
- grad_mix_one: bfloat16 [2, 8, 128, 128], P(None, 'seq')
- grad_mix_two: bfloat16 [2, 128, 8, 8], P(None, 'seq')
- grad_mix_three: bfloat16 [2, 128, 8, 8], P(None, 'seq')
- grad_mix_four: bfloat16 [2, 8, 128, 128], P(None, 'seq')
- grad_filter: bfloat16 [128, 8, 1536], P('seq')
The draws below stay inside these ranges and needn't reach their ends.
All inputs are finite; a program needn't handle non-finite values.
Results may differ from the reference program's by a relative error of at most 0.018.
Values may be sent and summed in bfloat16 or wider, within the bound.
No kernel may reach another device: no remote copies, remote signals or barrier semaphores. Data moves between devices by JAX's collectives and lax.ppermute only.
A program may use at most 64 MiB of HBM per device.

```python
import jax
import jax.numpy as jnp
from jax import lax

C = 1536
BLK = 128
LENGTH = 1024
NBLK = 8
SEQS = 4


def strengthened(values, rng, source, target, parts, factor):
    def block_of(dim):
        return (jnp.arange(values.shape[dim]) // (values.shape[dim] // parts)).reshape((-1,) + (1,) * (values.ndim - 1 - dim))

    first = jax.random.permutation(rng, parts)[block_of(target)]
    second = (block_of(target) + parts // 2) % parts
    return jnp.where((block_of(source) == first) | (block_of(source) == second), factor * values, values)


def block_scale(stream_key, shape, split, least, largest):
    def one(axis_at, shards_of):
        draws = jax.random.uniform(jax.random.fold_in(jax.random.fold_in(stream_key, 6), axis_at), (shards_of,), jnp.float32, least / len(split), largest / len(split))
        return jnp.repeat(jnp.exp(draws), shape[axis_at] // shards_of).reshape((-1,) + (1,) * (len(shape) - axis_at - 1))

    factor_of = one(*split[0])
    for cut in split[1:]:
        factor_of = factor_of * one(*cut)
    return factor_of


def centred(rng, dims, scale, reach, cuts=(), kind=jnp.bfloat16):
    values = scale * jax.random.normal(rng, dims, jnp.float32)
    if cuts:
        values = values * block_scale(rng, dims, cuts, -0.22, 0.18)
    return jnp.clip(values, -reach, reach).astype(kind)


def noise_with(rng, shape, deviation, limit, pieces, heavy, dtype=jnp.bfloat16):
    result = deviation * jax.random.normal(rng, shape, jnp.float32)
    if pieces:
        result = result * block_scale(rng, shape, pieces, -0.22, 0.18)
    return jnp.clip(strengthened(result, jax.random.fold_in(rng, 3), *heavy), -limit, limit).astype(dtype)


def setup_inputs(seed: int = 0) -> dict:
    splits = jax.random.split(jax.random.key(seed), 10)
    return {
        "tokens": centred(splits[0], (SEQS, LENGTH, C), 1.0, 6.0, ((0, 4), (1, 8))),
        "upstream": noise_with(splits[1], (SEQS, LENGTH, C), 1.0, 6.0, ((0, 4), (1, 8)), (1, 2, 8, 2.0)),
        "conv_value": centred(splits[2], (3, C), 3 ** -0.5, 3.5, (), jnp.float32),
        "conv_gate": centred(splits[3], (3, C), 3 ** -0.5, 3.5, (), jnp.float32),
        "mix_one": centred(splits[4], (2, NBLK, BLK, BLK), (2 * BLK) ** -0.5, 0.375, ((1, 8),)),
        "mix_two": centred(splits[5], (2, BLK, NBLK, NBLK), (2 * NBLK) ** -0.5, 1.5, ((1, 8),)),
        "mix_three": centred(splits[6], (2, BLK, NBLK, NBLK), (2 * NBLK) ** -0.5, 1.5, ((1, 8),)),
        "mix_four": centred(splits[7], (2, NBLK, BLK, BLK), (2 * BLK) ** -0.5, 0.375, ((1, 8),)),
        "filter_log": centred(splits[8], (BLK, NBLK, C), 0.5, 2.5, ((0, 8),)),
    }


def settle(array):
    return lax.optimization_barrier(array.astype(jnp.bfloat16)).astype(jnp.float32)

def complex_stack(factor, conjugate):
    real_part = factor[0]
    imag_part = factor[1]
    if conjugate:
        return jnp.stack([jnp.stack([real_part, imag_part]), jnp.stack([-imag_part, real_part])])
    return jnp.stack([jnp.stack([real_part, -imag_part]), jnp.stack([imag_part, real_part])])

def shortconv(padded, weights):
    length = padded.shape[0] - 2
    return weights[0] * padded[0:length] + weights[1] * padded[1:length + 1] + weights[2] * padded[2:length + 2]

def conv_grad(grad, padded):
    length = grad.shape[0]
    return jnp.stack([lax.optimization_barrier(jnp.sum(grad * padded[offset:offset + length], axis=0)) for offset in range(3)])

def transpose_conv(grad, weights):
    edged = jnp.pad(grad, ((1, 1), (0, 0)))
    return weights[0] * edged[2:] + weights[1] * edged[1:-1] + weights[2] * edged[:-2]

def one_sequence(seq_tokens, seq_upstream, conv_value, conv_gate, blocks_one, blocks_two, blocks_three, blocks_four, filt):
    padded = jnp.pad(seq_tokens.astype(jnp.float32), ((1, 1), (0, 0)))
    values = settle(shortconv(padded, conv_value))
    gating = settle(shortconv(padded, conv_gate))
    value_blocks = values.reshape(NBLK, BLK, C)
    stacked_two = complex_stack(blocks_two, False)
    stacked_two_conj = complex_stack(blocks_two, True)
    stacked_three = complex_stack(blocks_three, False)
    stacked_three_conj = complex_stack(blocks_three, True)
    signed_four = jnp.stack([blocks_four[0], -blocks_four[1]])
    first = settle(jnp.einsum('pikj,ijc->pikc', blocks_one, value_blocks))
    second = jnp.einsum('pqkmi,qikc->pkmc', stacked_two, first)
    weighted = settle(filt * second)
    third = settle(jnp.einsum('pqknm,qkmc->pknc', stacked_three, weighted))
    mixed_out = jnp.einsum('pnqk,pknc->nqc', signed_four, third).reshape(LENGTH, C)
    upstream_f = seq_upstream.astype(jnp.float32)
    mix_grad = settle(upstream_f * gating)
    gate_grad = upstream_f * mixed_out
    mix_blocks = mix_grad.reshape(NBLK, BLK, C)
    third_grad = settle(jnp.einsum('pnqk,nqc->pknc', signed_four, mix_blocks))
    products = jnp.einsum('nqc,pknc->pnqk', mix_blocks, third)
    grad_four = jnp.stack([products[0], -products[1]])
    weighted_grad = jnp.einsum('pqknm,qknc->pkmc', stacked_three_conj, third_grad)
    products = jnp.einsum('qknc,pkmc->qpknm', third_grad, weighted)
    grad_three = jnp.stack([products[0, 0] + products[1, 1], products[1, 0] - products[0, 1]])
    filter_term = weighted_grad[0] * second[0] + weighted_grad[1] * second[1]
    second_grad = settle(filt * weighted_grad)
    first_grad = settle(jnp.einsum('pqkmi,qkmc->pikc', stacked_two_conj, second_grad))
    products = jnp.einsum('qkmc,pikc->qpkmi', second_grad, first)
    grad_two = jnp.stack([products[0, 0] + products[1, 1], products[1, 0] - products[0, 1]])
    value_grad = jnp.einsum('pikj,pikc->ijc', blocks_one, first_grad).reshape(LENGTH, C)
    grad_one = jnp.einsum('pikc,ijc->pikj', first_grad, value_blocks)
    token_grad = (transpose_conv(value_grad, conv_value) + transpose_conv(gate_grad, conv_gate)).astype(jnp.bfloat16)
    terms = (grad_one, grad_two, grad_three, grad_four, filter_term, conv_grad(value_grad, padded), conv_grad(gate_grad, padded))
    return (token_grad, terms)

def reference(tokens, upstream, conv_value, conv_gate, mix_one, mix_two, mix_three, mix_four, filter_log):
    filt = jnp.exp(filter_log.astype(jnp.float32))
    blocks_one = mix_one.astype(jnp.float32)
    blocks_two = mix_two.astype(jnp.float32)
    blocks_three = mix_three.astype(jnp.float32)
    blocks_four = mix_four.astype(jnp.float32)

    def advance(carry, pair):
        token_grad, terms = one_sequence(pair[0], pair[1], conv_value, conv_gate, blocks_one, blocks_two, blocks_three, blocks_four, filt)
        return (tuple((total + term for total, term in zip(carry, terms))), token_grad)
    initial = (jnp.zeros((2, NBLK, BLK, BLK), jnp.float32), jnp.zeros((2, BLK, NBLK, NBLK), jnp.float32), jnp.zeros((2, BLK, NBLK, NBLK), jnp.float32), jnp.zeros((2, NBLK, BLK, BLK), jnp.float32), jnp.zeros((BLK, NBLK, C), jnp.float32), jnp.zeros((3, C), jnp.float32), jnp.zeros((3, C), jnp.float32))
    totals, grad_x = lax.scan(advance, initial, (tokens, upstream))
    grad_filter = (filt * totals[4]).astype(jnp.bfloat16)
    return (grad_x, totals[5], totals[6], totals[0].astype(jnp.bfloat16), totals[1].astype(jnp.bfloat16), totals[2].astype(jnp.bfloat16), totals[3].astype(jnp.bfloat16), grad_filter)
```

```python
import functools

import jax
import jax.numpy as jnp
from jax import lax
from jax.experimental import pallas as pl
from jax.experimental.pallas import tpu as pltpu
from jax.sharding import PartitionSpec as P

F32 = jnp.float32
BF16 = jnp.bfloat16
TILE = 16
VMEM = pl.BlockSpec(memory_space=pltpu.VMEM)
SMEM = pl.BlockSpec(memory_space=pltpu.SMEM)
FAR = pl.BlockSpec(memory_space=pl.ANY)


class Plan:
    def __init__(self, dp, seq, tokens, mix_one, mix_two):
        self.dp, self.seq = dp, seq
        self.blk = mix_one.shape[-1]
        self.channels = tokens.shape[-1]
        assert tokens.shape[1] == self.blk and dp % 2 == 0
        self.nblk = seq
        self.kloc = mix_two.shape[1]
        half_dp = dp // 2
        self.fold = max(
            f
            for f in range(1, half_dp + 1)
            if half_dp % f == 0 and self.channels % (seq * f * TILE) == 0
        )
        self.groups = half_dp // self.fold
        self.members = self.fold * seq
        self.width = self.channels // self.members
        assert self.width <= 128
        self.cols = self.fold * self.width
        self.length = self.nblk * self.blk
        self.pairs = self.nblk * self.nblk
        self.yrows = self.kloc * 2 * self.pairs // self.blk
        self.direct = self.yrows == self.kloc
        self.streamed = self.nblk * TILE > self.blk
        self.kgroups = self.blk // TILE
        self.dim = self.nblk * TILE
        unit = TILE * self.fold
        self.half = -(-(2 * self.blk + self.yrows) // unit) * unit
        self.mrows = self.half // self.fold
        self.cores_share = self.width % (2 * TILE) == 0
        self.frows = self.width // 2 if self.cores_share else self.width
        self.full = -(-(self.width + TILE) // (2 * unit)) * 2 * unit
        self.orows = self.full // (2 * self.fold)
        self.share = self.mrows + self.orows
        self.group_lists = [
            [
                ((g * self.fold + h) * 2 + core) * seq + s
                for h in range(self.fold)
                for s in range(seq)
            ]
            for g in range(self.groups)
            for core in range(2)
        ]

    def across_cores(self):
        return [(d, d ^ 1) for d in range(self.dp)]

    def across_fold(self, step):
        moves = []
        for g in range(self.groups):
            for h in range(self.fold):
                for core in range(2):
                    source = (g * self.fold + h) * 2 + core
                    moves.append((source, (g * self.fold + (h + step) % self.fold) * 2 + core))
        return moves

    def across_groups(self, step):
        block = 2 * self.fold
        return [(d, (d + step * block) % self.dp) for d in range(self.dp)]


def each(count, body):
    if count <= 8:
        for i in range(count):
            body(i)
    else:
        lax.fori_loop(0, count, lambda i, c: (body(i), c)[1], 0)


def rows_at(start, size):
    return pl.ds(start if isinstance(start, int) else pl.multiple_of(start, TILE), size)


def dot(a, b, ca, cb):
    return lax.dot_general(a, b, (((ca,), (cb,)), ((), ())), preferred_element_type=F32)


def call(kernel, out_shape, *args, scratch=(), smem=(), far=(), limit=16, name=None):
    single = not isinstance(out_shape, (list, tuple))
    return pl.pallas_call(
        kernel,
        out_shape=out_shape,
        in_specs=[SMEM if i in smem else FAR if i in far else VMEM for i in range(len(args))],
        out_specs=VMEM if single else [VMEM] * len(out_shape),
        scratch_shapes=list(scratch),
        compiler_params=pltpu.CompilerParams(vmem_limit_bytes=limit * 2**20),
        name=name,
    )(*args)


def shape(*dims, dtype=BF16):
    return jax.ShapeDtypeStruct(dims, dtype)


def factor_message_kernel(p, place, *refs):
    count = 5 if p.direct else 4
    far, out, near, rows, turned, done = refs[:count], refs[count], refs[count + 1 : -3], *refs[-3:]
    copies = [pltpu.make_async_copy(f, n, done.at[i]) for i, (f, n) in enumerate(zip(far, near))]
    for copy in copies:
        copy.start()
    h, core = place[0], place[1]
    filt, one, four = near[:3]
    for copy in copies[1:]:
        copy.wait()
    for part in range(2):
        base = part * p.half
        rows[base : base + p.blk] = one[part]
        rows[base + p.blk : base + 2 * p.blk] = four[part]
        if p.direct:
            small = jnp.concatenate([near[3][part], near[4][part]], axis=0).T
        else:
            small = near[3][part]
        rows[base + 2 * p.blk : base + 2 * p.blk + p.yrows] = small
        pad = p.half - 2 * p.blk - p.yrows
        if pad:
            rows[base + p.half - pad : base + p.half] = jnp.zeros((pad, p.blk), BF16)
    mine = rows[rows_at(core * p.half + h * p.mrows, p.mrows)]
    copies[0].wait()
    turned[...] = filt[...].T

    def one_target(s):
        out[s, 0 : p.mrows] = mine
        start = (h * p.seq + s) * p.width
        if p.cores_share:
            start = start + core * p.frows
        out[s, p.mrows :] = turned[rows_at(start, p.frows)]

    each(p.seq, one_target)


def token_message_kernel(p, tokens, upstream, out):
    w = p.width
    token_rows = tokens[...].T
    upstream_rows = upstream[...].T
    for q in range(p.members):
        out[q, 0:w] = token_rows[q * w : (q + 1) * w]
        out[q, w : 2 * w] = upstream_rows[q * w : (q + 1) * w]


def prepare_kernel(p, place, *refs):
    pieces, (one, four, small, filt, rows, turned) = refs[: 2 * p.fold], refs[2 * p.fold :]
    h, core = place[0], place[1]
    for side in range(2):
        c = core if side == 0 else 1 - core
        for step in range(p.fold):
            piece = pieces[side * p.fold + step]
            owner = h - step
            owner = jnp.where(owner < 0, owner + p.fold, owner)
            rows[:, rows_at(c * p.half + owner * p.mrows, p.mrows), :] = piece[:, 0 : p.mrows, :]
            if step == 0 and (p.cores_share or side == 0):
                start = c * p.frows if p.cores_share else 0
                turned[:, rows_at(start, p.frows), :] = piece[:, p.mrows :, :]

    def one_block(i):
        for part in range(2):
            base = part * p.half
            one[i, part * p.blk : (part + 1) * p.blk] = rows[i, base : base + p.blk]
            factor = rows[i, base + p.blk : base + 2 * p.blk]
            four[i, :, part * p.blk : (part + 1) * p.blk] = factor if part == 0 else -factor
            small[part, i] = rows[i, base + 2 * p.blk : base + 2 * p.blk + p.yrows]
        logs = turned[i]
        if p.fold > 1:
            logs = jnp.concatenate([logs] * p.fold, axis=0)
        filt[i] = jnp.exp(logs.T.astype(F32))

    each(p.nblk, one_block)


def iota(dims, axis):
    return lax.broadcasted_iota(jnp.int32, dims, axis)


def block_masks(p):
    d, nb, pairs = p.dim, p.nblk, p.pairs
    same = iota((d, d), 0) % TILE == iota((d, d), 1) // nb
    lane = iota((d, 2 * pairs), 1)
    block = iota((d, 2 * pairs), 0) // TILE
    keep_two = (lane < pairs) & (lane % nb == block)
    keep_three = (lane >= pairs) & ((lane - pairs) // nb == block)
    return same, keep_two, keep_three


def selectors(p, turned):
    d, nb, pairs = p.dim, p.nblk, p.pairs
    dims = (d, 2 * pairs) if turned else (2 * pairs, d)
    lane = iota(dims, 1 if turned else 0)
    block = iota(dims, 0 if turned else 1) % nb
    two = (lane < pairs) & (lane // nb == block)
    three = (lane >= pairs) & ((lane - pairs) % nb == block)
    return two.astype(BF16), three.astype(BF16)


def block_factor_kernel(p, small, two, three):
    same, keep_two, keep_three = block_masks(p)
    pick_two, pick_three = selectors(p, False)
    d = p.dim

    def one_group(g):
        parts = {}
        for part in range(2):
            entries = small[part, rows_at(g * TILE, TILE)]
            tiled = jnp.concatenate([entries] * p.nblk, axis=0)
            zero = jnp.zeros_like(tiled)
            for name, keep, pick in (("two", keep_two, pick_two), ("three", keep_three, pick_three)):
                spread = dot(jnp.where(keep, tiled, zero), pick, 1, 0)
                parts[name, part] = jnp.where(same, spread, 0.0).astype(BF16)
        two[g, :d, :d] = parts["two", 0]
        two[g, d:, d:] = parts["two", 0]
        two[g, :d, d:] = parts["two", 1]
        two[g, d:, :d] = -parts["two", 1]
        three[g, :d, :d] = parts["three", 0]
        three[g, d:, d:] = parts["three", 0]
        three[g, :d, d:] = -parts["three", 1]
        three[g, d:, :d] = parts["three", 1]

    each(p.kgroups, one_group)


def mixer_kernel(
    p, place, tokens_in, taps, one, four, two_far, three_far, filt,
    grad_x, keep, send, small_keep, small_send,
    tok, ups, val, mix, groups_a, groups_b, second, time_a, gate, grad_v, filter_grad, halves, fulls, small, *near,
):
    core = place[1]

    def factor(far, at, g):
        if not p.streamed:
            return far[g]
        pltpu.sync_copy(far.at[g], near[at])
        return near[at][...]

    blk, nb, d, w, cols = p.blk, p.nblk, p.dim, p.width, p.cols
    edge = 8

    def taps_of(branch, offset):
        return taps[3 * branch + offset : 3 * branch + offset + 1, :]

    zero_edge = jnp.zeros((edge, cols), F32)
    for ref in (tok, gate, grad_v):
        ref[0:edge] = zero_edge
        ref[edge + p.length : 2 * edge + p.length] = zero_edge

    def load(i):
        both = [tokens_in[h * nb + i] for h in range(p.fold)]
        t = jnp.concatenate([b[0:w] for b in both], axis=0) if p.fold > 1 else both[0][0:w]
        u = jnp.concatenate([b[w:] for b in both], axis=0) if p.fold > 1 else both[0][w:]
        tok[rows_at(edge + i * blk, blk) if isinstance(i, int) else pl.ds(pl.multiple_of(edge + i * blk, 8), blk)] = t.T.astype(F32)
        ups[rows_at(i * blk, blk)] = u.T

    each(nb, load)

    def window(ref, i, offset):
        return ref[pl.ds(edge + i * blk + offset, blk)]

    def spread(ref, i, value):
        for part in range(2):
            for g in range(p.kgroups):
                row = part * blk + g * TILE
                ref[g, rows_at((part * nb + i) * TILE, TILE)] = value[row : row + TILE]

    def first_stage(i):
        before, here, after = (window(tok, i, o) for o in (-1, 0, 1))
        values = taps_of(0, 0) * before + taps_of(0, 1) * here + taps_of(0, 2) * after
        gating = taps_of(1, 0) * before + taps_of(1, 1) * here + taps_of(1, 2) * after
        values = values.astype(BF16)
        val[rows_at(i * blk, blk)] = values
        up = ups[rows_at(i * blk, blk)].astype(F32)
        mix[rows_at(i * blk, blk)] = (up * gating.astype(BF16).astype(F32)).astype(BF16)
        spread(groups_a, i, dot(one[i], values, 1, 0).astype(BF16))

    each(nb, first_stage)

    def filter_of(g):
        f = filt[rows_at(g * d, d)]
        return f

    def forward_middle(g):
        f = filter_of(g)
        f2 = jnp.concatenate([f, f], axis=0)
        sec = dot(factor(two_far, 0, g), groups_a[g], 0, 0)
        second[g] = sec
        weighted = (f2 * sec).astype(BF16)
        groups_b[g] = weighted
        third = dot(factor(three_far, 1, g), weighted, 1, 0).astype(BF16)
        for part in range(2):
            for n in range(nb):
                row = (part * nb + n) * TILE
                time_a[n, rows_at(part * blk + g * TILE, TILE)] = third[row : row + TILE]

    each(p.kgroups, forward_middle)

    def last_factor(n):
        third = time_a[n]
        last = four[n]
        mixed = dot(last, third, 1, 0)
        at = rows_at(n * blk, blk)
        gate[pl.ds(edge + n * blk, blk)] = ups[at].astype(F32) * mixed
        grads = mix[at]
        back = dot(last, grads, 0, 0).astype(BF16)
        for part in range(2):
            for g in range(p.kgroups):
                row = part * blk + g * TILE
                groups_b[p.kgroups + g, rows_at((part * nb + n) * TILE, TILE)] = back[row : row + TILE]
        products = dot(grads, third, 1, 1)
        halves[0, n, blk : 2 * blk] = products[:, 0:blk].astype(BF16)
        halves[1, n, blk : 2 * blk] = (-products[:, blk:]).astype(BF16)

    each(nb, last_factor)

    same, keep_two, keep_three = block_masks(p)
    pick_two, pick_three = selectors(p, True)

    def folded(real, imag, pick, kept):
        out = []
        for value in (real, imag):
            value = jnp.where(same, value, 0.0).astype(BF16)
            wide = dot(value, pick, 1, 0)
            wide = jnp.where(kept, wide, 0.0)
            out.append(jnp.sum(wide.reshape(nb, TILE, 2 * p.pairs), axis=0))
        return out

    def backward_middle(g):
        f = filter_of(g)
        f2 = jnp.concatenate([f, f], axis=0)
        third_grad = groups_b[p.kgroups + g]
        weighted_grad = dot(factor(three_far, 1, g), third_grad, 0, 0)
        term = weighted_grad * second[g]
        filter_grad[rows_at(g * d, d)] = f * (term[:d] + term[d:])
        products = dot(third_grad, groups_b[g], 1, 1)
        three_real, three_imag = folded(
            products[:d, :d] + products[d:, d:], products[d:, :d] - products[:d, d:], pick_three, keep_three
        )
        second_grad = (f2 * weighted_grad).astype(BF16)
        products = dot(groups_a[g], second_grad, 1, 1)
        two_real, two_imag = folded(
            products[:d, :d] + products[d:, d:], products[:d, d:] - products[d:, :d], pick_two, keep_two
        )
        at = rows_at(g * TILE, TILE)
        small[0, at] = (two_real + three_real).astype(BF16)
        small[1, at] = (two_imag + three_imag).astype(BF16)
        back = dot(factor(two_far, 0, g), second_grad, 1, 0).astype(BF16)
        for part in range(2):
            for i in range(nb):
                row = (part * nb + i) * TILE
                time_a[i, rows_at(part * blk + g * TILE, TILE)] = back[row : row + TILE]

    each(p.kgroups, backward_middle)

    def first_factor(i):
        first_grad = time_a[i]
        grad_v[pl.ds(edge + i * blk, blk)] = dot(one[i], first_grad, 0, 0)
        products = dot(first_grad, val[rows_at(i * blk, blk)], 1, 1)
        for part in range(2):
            halves[part, i, 0:blk] = products[part * blk : (part + 1) * blk].astype(BF16)
        if p.half > 2 * blk:
            rest = jnp.zeros((p.half - 2 * blk, blk), BF16)
            for part in range(2):
                halves[part, i, 2 * blk :] = rest

    each(nb, first_factor)

    sums = [jnp.zeros((8, cols), F32) for _ in range(6)]

    def last_stage(i, sums):
        total = jnp.zeros((blk, cols), F32)
        sums = list(sums)
        for branch, ref in ((0, grad_v), (1, gate)):
            before, here, after = (window(ref, i, o) for o in (-1, 0, 1))
            total += taps_of(branch, 0) * after + taps_of(branch, 1) * here + taps_of(branch, 2) * before
            for offset in range(3):
                product = here * window(tok, i, offset - 1)
                sums[3 * branch + offset] += jnp.sum(product.reshape(blk // 8, 8, cols), axis=0)
        turned = total.astype(BF16).T
        terms = filter_grad[rows_at(i * blk, blk)].T
        term = terms[0:w]
        for h in range(1, p.fold):
            term = term + terms[h * w : (h + 1) * w]
        fulls[i, 0:w] = term.astype(BF16)
        if p.full > w + TILE:
            fulls[i, w + TILE :] = jnp.zeros((p.full - w - TILE, blk), BF16)
        for h in range(p.fold):
            grad_x[h * nb + i] = turned[h * w : (h + 1) * w]
        return tuple(sums)

    if nb <= 8:
        for i in range(nb):
            sums = last_stage(i, sums)
    else:
        sums = lax.fori_loop(0, nb, last_stage, tuple(sums))

    conv = jnp.concatenate([jnp.sum(s, axis=0, keepdims=True) for s in sums] + [jnp.zeros((2, cols), F32)], axis=0)
    term = conv[:, 0:w]
    for h in range(1, p.fold):
        term = term + conv[:, h * w : (h + 1) * w]
    if w < blk:
        term = jnp.concatenate([term, jnp.zeros((8, blk - w), F32)], axis=1)
    high = term.astype(BF16).astype(F32)
    conv_rows = jnp.concatenate([high, term - high], axis=0).astype(BF16)

    def hand_out(s):
        fulls[s, w : w + TILE] = conv_rows
        for ref, c in ((keep, core), (send, 1 - core)):
            for h in range(p.fold):
                ref[h, s, 0 : p.mrows] = halves[c, s, h * p.mrows : (h + 1) * p.mrows]
                ref[h, s, p.mrows :] = fulls[s, rows_at((c * p.fold + h) * p.orows, p.orows)]

    each(nb, hand_out)
    small_keep[...] = small[core]
    small_send[...] = small[1 - core]


def add_kernel(p, grad_x, keep, got, small_keep, small_got, out):
    w = p.width

    def one_target(s):
        extra = (small_keep[s].astype(F32) + small_got[s].astype(F32)).astype(BF16)
        for h in range(p.fold):
            q = h * p.seq + s
            out[q, 0:w] = grad_x[q]
            out[q, w:] = (keep[h, s].astype(F32) + got[h, s].astype(F32)).astype(BF16)
            first, last = 2 * p.blk - h * p.mrows, 2 * p.blk + p.yrows - h * p.mrows
            lo, hi = max(first, 0), min(last, p.mrows)
            if lo < hi:
                out[q, w + lo : w + hi] = extra[lo - first : hi - first]

    each(p.seq, one_target)


def sum_kernel(p, got, out):
    w = p.width
    total = got[0, w : w + p.mrows].astype(F32)
    for q in range(1, p.members):
        total += got[q, w : w + p.mrows].astype(F32)
    out[0 : p.mrows] = total.astype(BF16)
    for q in range(p.members):
        at = p.mrows + q * p.orows
        out[at : at + p.orows] = got[q, w + p.mrows :]


def grad_x_kernel(p, got, out):
    rows = jnp.concatenate([got[q, 0 : p.width] for q in range(p.members)], axis=0)
    out[...] = rows.T


def finish_kernel(p, place, *refs):
    pieces, outs, (rows, fulls) = refs[: 2 * p.fold], refs[2 * p.fold : -2], refs[-2:]
    one, four, filt, conv_value, conv_gate, *small = outs
    h, core = place[0], place[1]
    for side in range(2):
        c = core if side == 0 else 1 - core
        for step in range(p.fold):
            piece = pieces[side * p.fold + step]
            owner = h - step
            owner = jnp.where(owner < 0, owner + p.fold, owner)
            rows[rows_at(c * p.half + owner * p.mrows, p.mrows)] = piece[0 : p.mrows]
            at = rows_at((c * p.fold + owner) * p.orows, p.orows)
            for q in range(p.members):
                fulls[q, at] = piece[p.mrows + q * p.orows : p.mrows + (q + 1) * p.orows]
    for part in range(2):
        base = part * p.half
        one[part] = rows[base : base + p.blk]
        four[part] = rows[base + p.blk : base + 2 * p.blk]
        entries = rows[base + 2 * p.blk : base + 2 * p.blk + p.yrows]
        if p.direct:
            entries = entries.T
            small[0][part] = entries[: p.pairs]
            small[1][part] = entries[p.pairs :]
        else:
            small[0][part] = entries
    turned = jnp.concatenate([fulls[q, 0 : p.width] for q in range(p.members)], axis=0)
    filt[...] = turned.T
    sums = fulls[:, p.width : p.width + TILE].astype(F32)
    sums = sums[:, :8] + sums[:, 8:]
    sums = jnp.concatenate([sums[q].T[: p.width] for q in range(p.members)], axis=0).T
    conv_value[...] = sums[0:3]
    conv_gate[...] = sums[3:6]


def shards(
    tokens, upstream, conv_value, conv_gate, mix_one, mix_two, mix_three, mix_four, filter_log
):
    p = Plan(lax.axis_size("dp"), lax.axis_size("seq"), tokens, mix_one, mix_two)
    dp_at, seq_at = lax.axis_index("dp"), lax.axis_index("seq")
    h_at = (dp_at // 2) % p.fold
    place = jnp.stack([h_at, dp_at % 2]).astype(jnp.int32)
    blk, pairs = p.blk, p.pairs

    def shuffle(array):
        return lax.all_to_all(
            array, ("dp", "seq"), 0, 0, tiled=True, axis_index_groups=p.group_lists
        )

    def swap(array):
        return lax.ppermute(array, "dp", p.across_cores())

    def gathered(array, rows):
        pieces = [array]
        for step in range(1, p.fold):
            pieces.append(lax.ppermute(rows(array), "dp", p.across_fold(step)))
        return pieces + [swap(piece) for piece in pieces]

    if p.direct:
        small = [f.transpose(0, 2, 3, 1).reshape(2, pairs, p.kloc) for f in (mix_two, mix_three)]
    else:
        small = [f.reshape(2, p.kloc, pairs) for f in (mix_two, mix_three)]
        small = [jnp.concatenate(small, axis=2).reshape(2, p.yrows, blk)]
    far = [
        filter_log.reshape(blk, p.channels),
        mix_one.reshape(2, blk, blk),
        mix_four.reshape(2, blk, blk),
        *small,
    ]
    message = call(
        functools.partial(factor_message_kernel, p),
        shape(p.seq, p.mrows + p.frows, blk),
        place,
        *far,
        scratch=[pltpu.VMEM(f.shape, BF16) for f in far]
        + [
            pltpu.VMEM((2 * p.half, blk), BF16),
            pltpu.VMEM((p.channels, blk), BF16),
            pltpu.SemaphoreType.DMA((len(far),)),
        ],
        smem=(0,),
        far=range(1, 1 + len(far)),
        name="factor_message",
    )
    factors = lax.all_to_all(message, "seq", 0, 0, tiled=True)
    pieces = gathered(factors, lambda a: a[:, : p.mrows])
    one, four, small, filt = call(
        functools.partial(prepare_kernel, p),
        [
            shape(p.nblk, 2 * blk, blk),
            shape(p.nblk, blk, 2 * blk),
            shape(2, p.nblk, p.yrows, blk),
            shape(p.nblk, blk, p.cols, dtype=F32),
        ],
        place,
        *pieces,
        scratch=[
            pltpu.VMEM((p.nblk, 2 * p.half, blk), BF16),
            pltpu.VMEM((p.nblk, p.width, blk), BF16),
        ],
        smem=(0,),
        name="prepare",
    )
    two, three = call(
        functools.partial(block_factor_kernel, p),
        [shape(p.kgroups, 2 * p.dim, 2 * p.dim)] * 2,
        small.reshape(2, blk, 2 * pairs),
        limit=48 if p.streamed else 16,
        name="block_factors",
    )

    message = call(
        functools.partial(token_message_kernel, p),
        shape(p.members, 2 * p.width, blk),
        tokens[0],
        upstream[0],
        name="token_message",
    )
    received = shuffle(message)
    start = (h_at * p.seq + seq_at) * p.width
    taps = jnp.concatenate([conv_value, conv_gate], axis=0)
    taps = lax.dynamic_slice_in_dim(taps, start, p.width, 1)
    taps = jnp.concatenate([taps] * p.fold, axis=1)

    padded = p.length + 16
    grad_x, keep, send, small_keep, small_send = call(
        functools.partial(mixer_kernel, p),
        [
            shape(p.members, p.width, blk),
            shape(p.fold, p.seq, p.share, blk),
            shape(p.fold, p.seq, p.share, blk),
            shape(blk, 2 * pairs),
            shape(blk, 2 * pairs),
        ],
        place,
        received,
        taps,
        one,
        four,
        two,
        three,
        filt.reshape(p.length, p.cols),
        scratch=[
            pltpu.VMEM((padded, p.cols), F32),
            pltpu.VMEM((p.length, p.cols), BF16),
            pltpu.VMEM((p.length, p.cols), BF16),
            pltpu.VMEM((p.length, p.cols), BF16),
            pltpu.VMEM((p.kgroups, 2 * p.dim, p.cols), BF16),
            pltpu.VMEM((2 * p.kgroups, 2 * p.dim, p.cols), BF16),
            pltpu.VMEM((p.kgroups, 2 * p.dim, p.cols), F32),
            pltpu.VMEM((p.nblk, 2 * blk, p.cols), BF16),
            pltpu.VMEM((padded, p.cols), F32),
            pltpu.VMEM((padded, p.cols), F32),
            pltpu.VMEM((p.length, p.cols), F32),
            pltpu.VMEM((2, p.nblk, p.half, blk), BF16),
            pltpu.VMEM((p.nblk, p.full, blk), BF16),
            pltpu.VMEM((2, blk, 2 * pairs), BF16),
        ]
        + [pltpu.VMEM((2 * p.dim, 2 * p.dim), BF16)] * (2 if p.streamed else 0),
        smem=(0,),
        far=(5, 6) if p.streamed else (),
        limit=60 if p.streamed else 20,
        name="mixer",
    )

    message = call(
        functools.partial(add_kernel, p),
        shape(p.members, p.width + p.share, blk),
        grad_x,
        keep,
        swap(send),
        small_keep.reshape(p.seq, p.yrows, blk),
        swap(small_send).reshape(p.seq, p.yrows, blk),
        name="add_cores",
    )
    received = shuffle(message)
    sums = call(
        functools.partial(sum_kernel, p),
        shape(p.mrows + p.members * p.orows, blk),
        received,
        name="sum_sources",
    )
    if p.groups > 1:
        total = sums.astype(F32)
        for step in range(1, p.groups):
            total += lax.ppermute(sums, "dp", p.across_groups(step)).astype(F32)
        sums = total.astype(BF16)
    pieces = gathered(sums, lambda a: a)
    token_grad = call(
        functools.partial(grad_x_kernel, p), shape(blk, p.channels), received, name="token_grad"
    )
    grad_one, grad_four, grad_filter, sum_value, sum_gate, *small = call(
        functools.partial(finish_kernel, p),
        [
            shape(2, blk, blk),
            shape(2, blk, blk),
            shape(blk, p.channels),
            shape(3, p.channels, dtype=F32),
            shape(3, p.channels, dtype=F32),
        ]
        + ([shape(2, pairs, p.kloc)] * 2 if p.direct else [shape(2, p.yrows, blk)]),
        place,
        *pieces,
        scratch=[
            pltpu.VMEM((2 * p.half, blk), BF16),
            pltpu.VMEM((p.members, p.full, blk), BF16),
        ],
        smem=(0,),
        name="finish",
    )
    if p.direct:
        small = [f.reshape(2, p.nblk, p.nblk, p.kloc).transpose(0, 3, 1, 2) for f in small]
    else:
        small = small[0].reshape(2, p.kloc, 2, p.nblk, p.nblk)
        small = [small[:, :, 0], small[:, :, 1]]
    return (
        token_grad[None],
        sum_value,
        sum_gate,
        grad_one.reshape(mix_one.shape),
        *small,
        grad_four.reshape(mix_four.shape),
        grad_filter.reshape(filter_log.shape),
    )


def solution(mesh):
    return jax.shard_map(
        shards,
        mesh=mesh,
        in_specs=(
            P("dp", "seq", None),
            P("dp", "seq", None),
            P(),
            P(),
            P(None, "seq", None, None),
            P(None, "seq", None, None),
            P(None, "seq", None, None),
            P(None, "seq", None, None),
            P("seq", None, None),
        ),
        out_specs=(
            P("dp", "seq", None),
            P(),
            P(),
            P(None, "seq", None, None),
            P(None, "seq", None, None),
            P(None, "seq", None, None),
            P(None, "seq", None, None),
            P("seq", None, None),
        ),
        check_vma=False,
    )
```

```python
import functools

import jax
import jax.numpy as jnp
from jax import lax
from jax.experimental import pallas as pl
from jax.experimental.pallas import tpu as pltpu
from jax.sharding import PartitionSpec as P

F32 = jnp.float32
BF16 = jnp.bfloat16
TILE = 16
VMEM = pl.BlockSpec(memory_space=pltpu.VMEM)
SMEM = pl.BlockSpec(memory_space=pltpu.SMEM)
FAR = pl.BlockSpec(memory_space=pl.ANY)


class Plan:
    def __init__(self, dp, seq, tokens, mix_one, mix_two):
        self.dp, self.seq = dp, seq
        self.blk = mix_one.shape[-1]
        self.channels = tokens.shape[-1]
        assert tokens.shape[1] == self.blk and dp % 2 == 0
        self.nblk = seq
        self.kloc = mix_two.shape[1]
        half_dp = dp // 2
        self.fold = max(
            f
            for f in range(1, half_dp + 1)
            if half_dp % f == 0 and self.channels % (seq * f * TILE) == 0
        )
        self.groups = half_dp // self.fold
        self.members = self.fold * seq
        self.width = self.channels // self.members
        assert self.width <= 128
        self.cols = self.fold * self.width
        self.length = self.nblk * self.blk
        self.pairs = self.nblk * self.nblk
        self.yrows = self.kloc * 2 * self.pairs // self.blk
        self.direct = self.yrows == self.kloc
        self.streamed = self.nblk * TILE > self.blk
        self.kgroups = self.blk // TILE
        self.dim = self.nblk * TILE
        unit = TILE * self.fold
        self.half = -(-(2 * self.blk + self.yrows) // unit) * unit
        self.mrows = self.half // self.fold
        self.cores_share = self.width % (2 * TILE) == 0
        self.frows = self.width // 2 if self.cores_share else self.width
        self.full = -(-(self.width + TILE) // (2 * unit)) * 2 * unit
        self.orows = self.full // (2 * self.fold)
        self.share = self.mrows + self.orows
        self.group_lists = [
            [
                ((g * self.fold + h) * 2 + core) * seq + s
                for h in range(self.fold)
                for s in range(seq)
            ]
            for g in range(self.groups)
            for core in range(2)
        ]

    def across_cores(self):
        return [(d, d ^ 1) for d in range(self.dp)]

    def across_fold(self, step):
        moves = []
        for g in range(self.groups):
            for h in range(self.fold):
                for core in range(2):
                    source = (g * self.fold + h) * 2 + core
                    moves.append((source, (g * self.fold + (h + step) % self.fold) * 2 + core))
        return moves

    def across_groups(self, step):
        block = 2 * self.fold
        return [(d, (d + step * block) % self.dp) for d in range(self.dp)]


def each(count, body):
    if count <= 8:
        for i in range(count):
            body(i)
    else:
        lax.fori_loop(0, count, lambda i, c: (body(i), c)[1], 0)


def rows_at(start, size):
    return pl.ds(start if isinstance(start, int) else pl.multiple_of(start, TILE), size)


def dot(a, b, ca, cb):
    return lax.dot_general(a, b, (((ca,), (cb,)), ((), ())), preferred_element_type=F32)


def call(kernel, out_shape, *args, scratch=(), smem=(), far=(), limit=20, name=None):
    single = not isinstance(out_shape, (list, tuple))
    return pl.pallas_call(
        kernel,
        out_shape=out_shape,
        in_specs=[SMEM if i in smem else FAR if i in far else VMEM for i in range(len(args))],
        out_specs=VMEM if single else [VMEM] * len(out_shape),
        scratch_shapes=list(scratch),
        compiler_params=pltpu.CompilerParams(vmem_limit_bytes=limit * 2**20),
        name=name,
    )(*args)


def shape(*dims, dtype=BF16):
    return jax.ShapeDtypeStruct(dims, dtype)


def factor_message_kernel(p, place, *refs):
    count = 5 if p.direct else 4
    far, out, near, rows, turned, done = refs[:count], refs[count], refs[count + 1 : -3], *refs[-3:]
    copies = [pltpu.make_async_copy(f, n, done.at[i]) for i, (f, n) in enumerate(zip(far, near))]
    for copy in copies:
        copy.start()
    h, core = place[0], place[1]
    filt, one, four = near[:3]
    for copy in copies[1:]:
        copy.wait()
    for part in range(2):
        base = part * p.half
        rows[base : base + p.blk] = one[part]
        rows[base + p.blk : base + 2 * p.blk] = four[part]
        if p.direct:
            small = jnp.concatenate([near[3][part], near[4][part]], axis=0).T
        else:
            small = near[3][part]
        rows[base + 2 * p.blk : base + 2 * p.blk + p.yrows] = small
        pad = p.half - 2 * p.blk - p.yrows
        if pad:
            rows[base + p.half - pad : base + p.half] = jnp.zeros((pad, p.blk), BF16)
    mine = rows[rows_at(core * p.half + h * p.mrows, p.mrows)]
    copies[0].wait()
    turned[...] = filt[...].T

    def one_target(s):
        out[s, 0 : p.mrows] = mine
        start = (h * p.seq + s) * p.width
        if p.cores_share:
            start = start + core * p.frows
        out[s, p.mrows :] = turned[rows_at(start, p.frows)]

    each(p.seq, one_target)


def token_message_kernel(p, tokens, upstream, out):
    w = p.width
    token_rows = tokens[...].T
    upstream_rows = upstream[...].T
    for q in range(p.members):
        out[q, 0:w] = token_rows[q * w : (q + 1) * w]
        out[q, w : 2 * w] = upstream_rows[q * w : (q + 1) * w]


def prepare_kernel(p, place, *refs):
    pieces, (one, four, small, filt, rows, turned) = refs[: 2 * p.fold], refs[2 * p.fold :]
    h, core = place[0], place[1]
    for side in range(2):
        c = core if side == 0 else 1 - core
        for step in range(p.fold):
            piece = pieces[side * p.fold + step]
            owner = h - step
            owner = jnp.where(owner < 0, owner + p.fold, owner)
            rows[:, rows_at(c * p.half + owner * p.mrows, p.mrows), :] = piece[:, 0 : p.mrows, :]
            if step == 0 and (p.cores_share or side == 0):
                start = c * p.frows if p.cores_share else 0
                turned[:, rows_at(start, p.frows), :] = piece[:, p.mrows :, :]

    def one_block(i):
        for part in range(2):
            base = part * p.half
            one[i, part * p.blk : (part + 1) * p.blk] = rows[i, base : base + p.blk]
            factor = rows[i, base + p.blk : base + 2 * p.blk]
            four[i, :, part * p.blk : (part + 1) * p.blk] = factor if part == 0 else -factor
            small[part, i] = rows[i, base + 2 * p.blk : base + 2 * p.blk + p.yrows]
        logs = turned[i]
        if p.fold > 1:
            logs = jnp.concatenate([logs] * p.fold, axis=0)
        filt[i] = jnp.exp(logs.T.astype(F32))

    each(p.nblk, one_block)


def iota(dims, axis):
    return lax.broadcasted_iota(jnp.int32, dims, axis)


def block_masks(p):
    d, nb, pairs = p.dim, p.nblk, p.pairs
    same = iota((d, d), 0) % TILE == iota((d, d), 1) // nb
    lane = iota((d, 2 * pairs), 1)
    block = iota((d, 2 * pairs), 0) // TILE
    keep_two = (lane < pairs) & (lane % nb == block)
    keep_three = (lane >= pairs) & ((lane - pairs) // nb == block)
    return same, keep_two, keep_three


def selectors(p, turned):
    d, nb, pairs = p.dim, p.nblk, p.pairs
    dims = (d, 2 * pairs) if turned else (2 * pairs, d)
    lane = iota(dims, 1 if turned else 0)
    block = iota(dims, 0 if turned else 1) % nb
    two = (lane < pairs) & (lane // nb == block)
    three = (lane >= pairs) & ((lane - pairs) % nb == block)
    return two.astype(BF16), three.astype(BF16)


def block_factor_kernel(p, small, two, three):
    same, keep_two, keep_three = block_masks(p)
    pick_two, pick_three = selectors(p, False)
    d = p.dim

    def one_group(g):
        parts = {}
        for part in range(2):
            entries = small[part, rows_at(g * TILE, TILE)]
            tiled = jnp.concatenate([entries] * p.nblk, axis=0)
            zero = jnp.zeros_like(tiled)
            for name, keep, pick in (("two", keep_two, pick_two), ("three", keep_three, pick_three)):
                spread = dot(jnp.where(keep, tiled, zero), pick, 1, 0)
                parts[name, part] = jnp.where(same, spread, 0.0).astype(BF16)
        two[g, :d, :d] = parts["two", 0]
        two[g, d:, d:] = parts["two", 0]
        two[g, :d, d:] = parts["two", 1]
        two[g, d:, :d] = -parts["two", 1]
        three[g, :d, :d] = parts["three", 0]
        three[g, d:, d:] = parts["three", 0]
        three[g, :d, d:] = -parts["three", 1]
        three[g, d:, :d] = parts["three", 1]

    each(p.kgroups, one_group)


def mixer_kernel(
    p, place, tokens_in, taps, one, four, two_far, three_far, filt,
    grad_x, keep, send, small_keep, small_send,
    tok, ups, val, mix, groups_a, groups_b, second, time_a, gate, grad_v, filter_grad, halves, fulls, small, *near,
):
    core = place[1]

    def factor(far, at, g):
        if not p.streamed:
            return far[g]
        pltpu.sync_copy(far.at[g], near[at])
        return near[at][...]

    blk, nb, d, w, cols = p.blk, p.nblk, p.dim, p.width, p.cols
    edge = 8

    def taps_of(branch, offset):
        return taps[3 * branch + offset : 3 * branch + offset + 1, :]

    zero_edge = jnp.zeros((edge, cols), F32)
    for ref in (tok, gate, grad_v):
        ref[0:edge] = zero_edge
        ref[edge + p.length : 2 * edge + p.length] = zero_edge

    def load(i):
        both = [tokens_in[h * nb + i] for h in range(p.fold)]
        t = jnp.concatenate([b[0:w] for b in both], axis=0) if p.fold > 1 else both[0][0:w]
        u = jnp.concatenate([b[w:] for b in both], axis=0) if p.fold > 1 else both[0][w:]
        tok[rows_at(edge + i * blk, blk) if isinstance(i, int) else pl.ds(pl.multiple_of(edge + i * blk, 8), blk)] = t.T.astype(F32)
        ups[rows_at(i * blk, blk)] = u.T

    each(nb, load)

    def window(ref, i, offset):
        return ref[pl.ds(edge + i * blk + offset, blk)]

    def spread(ref, i, value):
        for part in range(2):
            for g in range(p.kgroups):
                row = part * blk + g * TILE
                ref[g, rows_at((part * nb + i) * TILE, TILE)] = value[row : row + TILE]

    def first_stage(i):
        before, here, after = (window(tok, i, o) for o in (-1, 0, 1))
        values = taps_of(0, 0) * before + taps_of(0, 1) * here + taps_of(0, 2) * after
        gating = taps_of(1, 0) * before + taps_of(1, 1) * here + taps_of(1, 2) * after
        values = values.astype(BF16)
        val[rows_at(i * blk, blk)] = values
        up = ups[rows_at(i * blk, blk)].astype(F32)
        mix[rows_at(i * blk, blk)] = (up * gating.astype(BF16).astype(F32)).astype(BF16)
        spread(groups_a, i, dot(one[i], values, 1, 0).astype(BF16))

    each(nb, first_stage)

    def filter_of(g):
        f = filt[rows_at(g * d, d)]
        return f

    def forward_middle(g):
        f = filter_of(g)
        f2 = jnp.concatenate([f, f], axis=0)
        sec = dot(factor(two_far, 0, g), groups_a[g], 0, 0)
        second[g] = sec
        weighted = (f2 * sec).astype(BF16)
        groups_b[g] = weighted
        third = dot(factor(three_far, 1, g), weighted, 1, 0).astype(BF16)
        for part in range(2):
            for n in range(nb):
                row = (part * nb + n) * TILE
                time_a[n, rows_at(part * blk + g * TILE, TILE)] = third[row : row + TILE]

    each(p.kgroups, forward_middle)

    def last_factor(n):
        third = time_a[n]
        last = four[n]
        mixed = dot(last, third, 1, 0)
        at = rows_at(n * blk, blk)
        gate[pl.ds(edge + n * blk, blk)] = ups[at].astype(F32) * mixed
        grads = mix[at]
        back = dot(last, grads, 0, 0).astype(BF16)
        for part in range(2):
            for g in range(p.kgroups):
                row = part * blk + g * TILE
                groups_b[p.kgroups + g, rows_at((part * nb + n) * TILE, TILE)] = back[row : row + TILE]
        products = dot(grads, third, 1, 1)
        halves[0, n, blk : 2 * blk] = products[:, 0:blk].astype(BF16)
        halves[1, n, blk : 2 * blk] = (-products[:, blk:]).astype(BF16)

    each(nb, last_factor)

    same, keep_two, keep_three = block_masks(p)
    pick_two, pick_three = selectors(p, True)

    def folded(real, imag, pick, kept):
        out = []
        for value in (real, imag):
            value = jnp.where(same, value, 0.0).astype(BF16)
            wide = dot(value, pick, 1, 0)
            wide = jnp.where(kept, wide, 0.0)
            out.append(jnp.sum(wide.reshape(nb, TILE, 2 * p.pairs), axis=0))
        return out

    def backward_middle(g):
        f = filter_of(g)
        f2 = jnp.concatenate([f, f], axis=0)
        third_grad = groups_b[p.kgroups + g]
        weighted_grad = dot(factor(three_far, 1, g), third_grad, 0, 0)
        term = weighted_grad * second[g]
        filter_grad[rows_at(g * d, d)] = f * (term[:d] + term[d:])
        products = dot(third_grad, groups_b[g], 1, 1)
        three_real, three_imag = folded(
            products[:d, :d] + products[d:, d:], products[d:, :d] - products[:d, d:], pick_three, keep_three
        )
        second_grad = (f2 * weighted_grad).astype(BF16)
        products = dot(groups_a[g], second_grad, 1, 1)
        two_real, two_imag = folded(
            products[:d, :d] + products[d:, d:], products[:d, d:] - products[d:, :d], pick_two, keep_two
        )
        at = rows_at(g * TILE, TILE)
        small[0, at] = (two_real + three_real).astype(BF16)
        small[1, at] = (two_imag + three_imag).astype(BF16)
        back = dot(factor(two_far, 0, g), second_grad, 1, 0).astype(BF16)
        for part in range(2):
            for i in range(nb):
                row = (part * nb + i) * TILE
                time_a[i, rows_at(part * blk + g * TILE, TILE)] = back[row : row + TILE]

    each(p.kgroups, backward_middle)

    def first_factor(i):
        first_grad = time_a[i]
        grad_v[pl.ds(edge + i * blk, blk)] = dot(one[i], first_grad, 0, 0)
        products = dot(first_grad, val[rows_at(i * blk, blk)], 1, 1)
        for part in range(2):
            halves[part, i, 0:blk] = products[part * blk : (part + 1) * blk].astype(BF16)
        if p.half > 2 * blk:
            rest = jnp.zeros((p.half - 2 * blk, blk), BF16)
            for part in range(2):
                halves[part, i, 2 * blk :] = rest

    each(nb, first_factor)

    sums = [jnp.zeros((8, cols), F32) for _ in range(6)]

    def last_stage(i, sums):
        total = jnp.zeros((blk, cols), F32)
        sums = list(sums)
        for branch, ref in ((0, grad_v), (1, gate)):
            before, here, after = (window(ref, i, o) for o in (-1, 0, 1))
            total += taps_of(branch, 0) * after + taps_of(branch, 1) * here + taps_of(branch, 2) * before
            for offset in range(3):
                product = here * window(tok, i, offset - 1)
                sums[3 * branch + offset] += jnp.sum(product.reshape(blk // 8, 8, cols), axis=0)
        turned = total.astype(BF16).T
        terms = filter_grad[rows_at(i * blk, blk)].T
        term = terms[0:w]
        for h in range(1, p.fold):
            term = term + terms[h * w : (h + 1) * w]
        fulls[i, 0:w] = term.astype(BF16)
        if p.full > w + TILE:
            fulls[i, w + TILE :] = jnp.zeros((p.full - w - TILE, blk), BF16)
        for h in range(p.fold):
            grad_x[h * nb + i] = turned[h * w : (h + 1) * w]
        return tuple(sums)

    if nb <= 8:
        for i in range(nb):
            sums = last_stage(i, sums)
    else:
        sums = lax.fori_loop(0, nb, last_stage, tuple(sums))

    conv = jnp.concatenate([jnp.sum(s, axis=0, keepdims=True) for s in sums] + [jnp.zeros((2, cols), F32)], axis=0)
    term = conv[:, 0:w]
    for h in range(1, p.fold):
        term = term + conv[:, h * w : (h + 1) * w]
    if w < blk:
        term = jnp.concatenate([term, jnp.zeros((8, blk - w), F32)], axis=1)
    high = term.astype(BF16).astype(F32)
    conv_rows = jnp.concatenate([high, term - high], axis=0).astype(BF16)

    def hand_out(s):
        fulls[s, w : w + TILE] = conv_rows
        for ref, c in ((keep, core), (send, 1 - core)):
            for h in range(p.fold):
                ref[h, s, 0 : p.mrows] = halves[c, s, h * p.mrows : (h + 1) * p.mrows]
                ref[h, s, p.mrows :] = fulls[s, rows_at((c * p.fold + h) * p.orows, p.orows)]

    each(nb, hand_out)
    small_keep[...] = small[core]
    small_send[...] = small[1 - core]


def add_kernel(p, keep, got, small_keep, small_got, out):
    def one_target(s):
        extra = (small_keep[s].astype(F32) + small_got[s].astype(F32)).astype(BF16)
        for h in range(p.fold):
            q = h * p.seq + s
            out[q] = (keep[h, s].astype(F32) + got[h, s].astype(F32)).astype(BF16)
            first, last = 2 * p.blk - h * p.mrows, 2 * p.blk + p.yrows - h * p.mrows
            lo, hi = max(first, 0), min(last, p.mrows)
            if lo < hi:
                out[q, lo:hi] = extra[lo - first : hi - first]

    each(p.seq, one_target)


def sum_kernel(p, got, out):
    total = got[0, 0 : p.mrows].astype(F32)
    for q in range(1, p.members):
        total += got[q, 0 : p.mrows].astype(F32)
    out[0 : p.mrows] = total.astype(BF16)
    for q in range(p.members):
        at = p.mrows + q * p.orows
        out[at : at + p.orows] = got[q, p.mrows :]


def grad_x_kernel(p, got, out):
    rows = jnp.concatenate([got[q] for q in range(p.members)], axis=0)
    out[...] = rows.T


def finish_kernel(p, place, *refs):
    pieces, outs, (rows, fulls) = refs[: 2 * p.fold], refs[2 * p.fold : -2], refs[-2:]
    one, four, filt, conv_value, conv_gate, *small = outs
    h, core = place[0], place[1]
    for side in range(2):
        c = core if side == 0 else 1 - core
        for step in range(p.fold):
            piece = pieces[side * p.fold + step]
            owner = h - step
            owner = jnp.where(owner < 0, owner + p.fold, owner)
            rows[rows_at(c * p.half + owner * p.mrows, p.mrows)] = piece[0 : p.mrows]
            at = rows_at((c * p.fold + owner) * p.orows, p.orows)
            for q in range(p.members):
                fulls[q, at] = piece[p.mrows + q * p.orows : p.mrows + (q + 1) * p.orows]
    for part in range(2):
        base = part * p.half
        one[part] = rows[base : base + p.blk]
        four[part] = rows[base + p.blk : base + 2 * p.blk]
        entries = rows[base + 2 * p.blk : base + 2 * p.blk + p.yrows]
        if p.direct:
            entries = entries.T
            small[0][part] = entries[: p.pairs]
            small[1][part] = entries[p.pairs :]
        else:
            small[0][part] = entries
    turned = jnp.concatenate([fulls[q, 0 : p.width] for q in range(p.members)], axis=0)
    filt[...] = turned.T
    sums = fulls[:, p.width : p.width + TILE].astype(F32)
    sums = sums[:, :8] + sums[:, 8:]
    sums = jnp.concatenate([sums[q].T[: p.width] for q in range(p.members)], axis=0).T
    conv_value[...] = sums[0:3]
    conv_gate[...] = sums[3:6]


def shards(
    tokens, upstream, conv_value, conv_gate, mix_one, mix_two, mix_three, mix_four, filter_log
):
    p = Plan(lax.axis_size("dp"), lax.axis_size("seq"), tokens, mix_one, mix_two)
    dp_at, seq_at = lax.axis_index("dp"), lax.axis_index("seq")
    h_at = (dp_at // 2) % p.fold
    place = jnp.stack([h_at, dp_at % 2]).astype(jnp.int32)
    blk, pairs = p.blk, p.pairs

    def shuffle(array):
        return lax.all_to_all(
            array, ("dp", "seq"), 0, 0, tiled=True, axis_index_groups=p.group_lists
        )

    def swap(array):
        return lax.ppermute(array, "dp", p.across_cores())

    def gathered(array, rows):
        pieces = [array]
        for step in range(1, p.fold):
            pieces.append(lax.ppermute(rows(array), "dp", p.across_fold(step)))
        return pieces + [swap(piece) for piece in pieces]

    if p.direct:
        small = [f.transpose(0, 2, 3, 1).reshape(2, pairs, p.kloc) for f in (mix_two, mix_three)]
    else:
        small = [f.reshape(2, p.kloc, pairs) for f in (mix_two, mix_three)]
        small = [jnp.concatenate(small, axis=2).reshape(2, p.yrows, blk)]
    far = [
        filter_log.reshape(blk, p.channels),
        mix_one.reshape(2, blk, blk),
        mix_four.reshape(2, blk, blk),
        *small,
    ]
    message = call(
        functools.partial(factor_message_kernel, p),
        shape(p.seq, p.mrows + p.frows, blk),
        place,
        *far,
        scratch=[pltpu.VMEM(f.shape, BF16) for f in far]
        + [
            pltpu.VMEM((2 * p.half, blk), BF16),
            pltpu.VMEM((p.channels, blk), BF16),
            pltpu.SemaphoreType.DMA((len(far),)),
        ],
        smem=(0,),
        far=range(1, 1 + len(far)),
        limit=60,
        name="factor_message",
    )
    factors = lax.all_to_all(message, "seq", 0, 0, tiled=True)
    pieces = gathered(factors, lambda a: a[:, : p.mrows])

    message = call(
        functools.partial(token_message_kernel, p),
        shape(p.members, 2 * p.width, blk),
        tokens[0],
        upstream[0],
        name="token_message",
    )
    received = shuffle(message)
    pieces, received = lax.optimization_barrier((pieces, received))
    one, four, small, filt = call(
        functools.partial(prepare_kernel, p),
        [
            shape(p.nblk, 2 * blk, blk),
            shape(p.nblk, blk, 2 * blk),
            shape(2, p.nblk, p.yrows, blk),
            shape(p.nblk, blk, p.cols, dtype=F32),
        ],
        place,
        *pieces,
        scratch=[
            pltpu.VMEM((p.nblk, 2 * p.half, blk), BF16),
            pltpu.VMEM((p.nblk, p.width, blk), BF16),
        ],
        smem=(0,),
        name="prepare",
    )
    two, three = call(
        functools.partial(block_factor_kernel, p),
        [shape(p.kgroups, 2 * p.dim, 2 * p.dim)] * 2,
        small.reshape(2, blk, 2 * pairs),
        limit=48 if p.streamed else 20,
        name="block_factors",
    )

    start = (h_at * p.seq + seq_at) * p.width
    taps = jnp.concatenate([conv_value, conv_gate], axis=0)
    taps = lax.dynamic_slice_in_dim(taps, start, p.width, 1)
    taps = jnp.concatenate([taps] * p.fold, axis=1)

    padded = p.length + 16
    grad_x, keep, send, small_keep, small_send = call(
        functools.partial(mixer_kernel, p),
        [
            shape(p.members, p.width, blk),
            shape(p.fold, p.seq, p.share, blk),
            shape(p.fold, p.seq, p.share, blk),
            shape(blk, 2 * pairs),
            shape(blk, 2 * pairs),
        ],
        place,
        received,
        taps,
        one,
        four,
        two,
        three,
        filt.reshape(p.length, p.cols),
        scratch=[
            pltpu.VMEM((padded, p.cols), F32),
            pltpu.VMEM((p.length, p.cols), BF16),
            pltpu.VMEM((p.length, p.cols), BF16),
            pltpu.VMEM((p.length, p.cols), BF16),
            pltpu.VMEM((p.kgroups, 2 * p.dim, p.cols), BF16),
            pltpu.VMEM((2 * p.kgroups, 2 * p.dim, p.cols), BF16),
            pltpu.VMEM((p.kgroups, 2 * p.dim, p.cols), F32),
            pltpu.VMEM((p.nblk, 2 * blk, p.cols), BF16),
            pltpu.VMEM((padded, p.cols), F32),
            pltpu.VMEM((padded, p.cols), F32),
            pltpu.VMEM((p.length, p.cols), F32),
            pltpu.VMEM((2, p.nblk, p.half, blk), BF16),
            pltpu.VMEM((p.nblk, p.full, blk), BF16),
            pltpu.VMEM((2, blk, 2 * pairs), BF16),
        ]
        + [pltpu.VMEM((2 * p.dim, 2 * p.dim), BF16)] * (2 if p.streamed else 0),
        smem=(0,),
        far=(5, 6) if p.streamed else (),
        limit=60 if p.streamed else 20,
        name="mixer",
    )

    message = call(
        functools.partial(add_kernel, p),
        shape(p.members, p.share, blk),
        keep,
        swap(send),
        small_keep.reshape(p.seq, p.yrows, blk),
        swap(small_send).reshape(p.seq, p.yrows, blk),
        name="add_cores",
    )
    received = shuffle(message)
    received, grad_x = lax.optimization_barrier((received, grad_x))
    grad_x = shuffle(grad_x)
    sums = call(
        functools.partial(sum_kernel, p),
        shape(p.mrows + p.members * p.orows, blk),
        received,
        name="sum_sources",
    )
    if p.groups > 1:
        total = sums.astype(F32)
        for step in range(1, p.groups):
            total += lax.ppermute(sums, "dp", p.across_groups(step)).astype(F32)
        sums = total.astype(BF16)
    pieces = gathered(sums, lambda a: a)
    token_grad = call(
        functools.partial(grad_x_kernel, p), shape(blk, p.channels), grad_x, name="token_grad"
    )
    grad_one, grad_four, grad_filter, sum_value, sum_gate, *small = call(
        functools.partial(finish_kernel, p),
        [
            shape(2, blk, blk),
            shape(2, blk, blk),
            shape(blk, p.channels),
            shape(3, p.channels, dtype=F32),
            shape(3, p.channels, dtype=F32),
        ]
        + ([shape(2, pairs, p.kloc)] * 2 if p.direct else [shape(2, p.yrows, blk)]),
        place,
        *pieces,
        scratch=[
            pltpu.VMEM((2 * p.half, blk), BF16),
            pltpu.VMEM((p.members, p.full, blk), BF16),
        ],
        smem=(0,),
        name="finish",
    )
    if p.direct:
        small = [f.reshape(2, p.nblk, p.nblk, p.kloc).transpose(0, 3, 1, 2) for f in small]
    else:
        small = small[0].reshape(2, p.kloc, 2, p.nblk, p.nblk)
        small = [small[:, :, 0], small[:, :, 1]]
    return (
        token_grad[None],
        sum_value,
        sum_gate,
        grad_one.reshape(mix_one.shape),
        *small,
        grad_four.reshape(mix_four.shape),
        grad_filter.reshape(filter_log.shape),
    )


def solution(mesh):
    return jax.shard_map(
        shards,
        mesh=mesh,
        in_specs=(
            P("dp", "seq", None),
            P("dp", "seq", None),
            P(),
            P(),
            P(None, "seq", None, None),
            P(None, "seq", None, None),
            P(None, "seq", None, None),
            P(None, "seq", None, None),
            P("seq", None, None),
        ),
        out_specs=(
            P("dp", "seq", None),
            P(),
            P(),
            P(None, "seq", None, None),
            P(None, "seq", None, None),
            P(None, "seq", None, None),
            P(None, "seq", None, None),
            P("seq", None, None),
        ),
        check_vma=False,
    )
```

```python
import functools

import jax
import jax.numpy as jnp
from jax import lax
from jax.experimental import pallas as pl
from jax.experimental.pallas import tpu as pltpu
from jax.sharding import PartitionSpec as P

F32 = jnp.float32
BF16 = jnp.bfloat16
TILE = 16
VMEM = pl.BlockSpec(memory_space=pltpu.VMEM)
FAR = pl.BlockSpec(memory_space=pl.ANY)


class Plan:
    def __init__(self, dp, seq, tokens, mix_one, mix_two):
        self.dp, self.seq = dp, seq
        self.blk = mix_one.shape[-1]
        self.channels = tokens.shape[-1]
        assert tokens.shape[1] == self.blk and dp % 2 == 0
        self.nblk = seq
        self.kloc = mix_two.shape[1]
        half_dp = dp // 2
        self.fold = max(
            f
            for f in range(1, half_dp + 1)
            if half_dp % f == 0 and self.channels % (seq * f * TILE) == 0
        )
        self.groups = half_dp // self.fold
        self.members = self.fold * seq
        self.width = self.channels // self.members
        assert self.width <= 128
        self.cols = self.fold * self.width
        self.length = self.nblk * self.blk
        self.pairs = self.nblk * self.nblk
        self.yrows = self.kloc * 2 * self.pairs // self.blk
        self.direct = self.yrows == self.kloc
        self.streamed = self.nblk * TILE > self.blk
        self.kgroups = self.blk // TILE
        self.dim = self.nblk * TILE
        unit = TILE * self.fold
        self.half = -(-(2 * self.blk + self.yrows) // unit) * unit
        self.mrows = self.half // self.fold
        self.cores_share = self.width % (2 * TILE) == 0
        self.frows = self.width // 2 if self.cores_share else self.width
        self.full = -(-(self.width + TILE) // (2 * unit)) * 2 * unit
        self.orows = self.full // (2 * self.fold)
        self.share = self.mrows + self.orows
        self.group_lists = [
            [
                ((g * self.fold + h) * 2 + core) * seq + s
                for h in range(self.fold)
                for s in range(seq)
            ]
            for g in range(self.groups)
            for core in range(2)
        ]

    def across_cores(self):
        return [(d, d ^ 1) for d in range(self.dp)]

    def across_fold(self, step):
        moves = []
        for g in range(self.groups):
            for h in range(self.fold):
                for core in range(2):
                    source = (g * self.fold + h) * 2 + core
                    moves.append((source, (g * self.fold + (h + step) % self.fold) * 2 + core))
        return moves

    def across_groups(self, step):
        block = 2 * self.fold
        return [(d, (d + step * block) % self.dp) for d in range(self.dp)]


def each(count, body, unrolled=True):
    if count <= 8 and unrolled:
        for i in range(count):
            body(i)
    else:
        lax.fori_loop(0, count, lambda i, c: (body(i), c)[1], 0)


def rows_at(start, size):
    return pl.ds(start if isinstance(start, int) else pl.multiple_of(start, TILE), size)


def dot(a, b, ca, cb):
    return lax.dot_general(a, b, (((ca,), (cb,)), ((), ())), preferred_element_type=F32)


def call(kernel, out_shape, *args, scratch=(), far=(), limit=20, name=None):
    single = not isinstance(out_shape, (list, tuple))
    return pl.pallas_call(
        kernel,
        out_shape=out_shape,
        in_specs=[FAR if i in far else VMEM for i in range(len(args))],
        out_specs=VMEM if single else [VMEM] * len(out_shape),
        scratch_shapes=list(scratch),
        compiler_params=pltpu.CompilerParams(vmem_limit_bytes=limit * 2**20),
        name=name,
    )(*args)


def shape(*dims, dtype=BF16):
    return jax.ShapeDtypeStruct(dims, dtype)


def place(p):
    at = lax.axis_index("dp")
    return (at // 2) % p.fold, at % 2


def factor_message_kernel(p, *refs):
    count = 5 if p.direct else 4
    far, out, near, rows, turned, done = refs[:count], refs[count], refs[count + 1 : -3], *refs[-3:]
    h, core = place(p)
    part_width = p.seq * p.width
    sources = [far[0].at[:, pl.ds(pl.multiple_of(h * part_width, p.blk), part_width)]]
    sources += [f.at[core] for f in far[1:]]
    copies = [pltpu.make_async_copy(f, n, done.at[i]) for i, (f, n) in enumerate(zip(sources, near))]
    for copy in copies:
        copy.start()
    filt, one, four = near[:3]
    for copy in copies[1:]:
        copy.wait()
    rows[0 : p.blk] = one[...]
    rows[p.blk : 2 * p.blk] = four[...]
    if p.direct:
        small = jnp.concatenate([near[3][...], near[4][...]], axis=0).T
    else:
        small = near[3][...]
    rows[2 * p.blk : 2 * p.blk + p.yrows] = small
    pad = p.half - 2 * p.blk - p.yrows
    if pad:
        rows[p.half - pad :] = jnp.zeros((pad, p.blk), BF16)
    mine = rows[0 : p.mrows]
    for owner in range(1, p.fold):
        mine = jnp.where(h == owner, rows[owner * p.mrows : (owner + 1) * p.mrows], mine)
    copies[0].wait()
    turned[...] = filt[...].T

    def one_target(s):
        out[s, 0 : p.mrows] = mine
        logs = turned[rows_at(s * p.width, p.width)]
        if p.cores_share:
            logs = jnp.where(core == 0, logs[: p.frows], logs[p.frows :])
        out[s, p.mrows :] = logs

    each(p.seq, one_target)


def token_message_kernel(p, tokens, upstream, out):
    w = p.width
    token_rows = tokens[...].T
    upstream_rows = upstream[...].T
    for q in range(p.members):
        out[q, 0:w] = token_rows[q * w : (q + 1) * w]
        out[q, w : 2 * w] = upstream_rows[q * w : (q + 1) * w]


def shares_in_order(p, pieces):
    h, core = place(p)

    def share(c, owner, part):
        value = None
        for side in range(2):
            for step in range(p.fold):
                piece = part(pieces[side * p.fold + step], side, step)
                if value is None:
                    value = piece
                    continue
                here = core == (c if side == 0 else 1 - c)
                value = jnp.where(here & (h == (owner + step) % p.fold), piece, value)
        return value

    return share


def prepare_kernel(p, *refs):
    pieces, (one, four, small, filt) = refs[: 2 * p.fold], refs[2 * p.fold :]
    share = shares_in_order(p, pieces)
    _, core = place(p)

    def one_block(i):
        for part in range(2):
            rows = [share(part, owner, lambda ref, *_: ref[i, 0 : p.mrows]) for owner in range(p.fold)]
            rows = jnp.concatenate(rows, axis=0) if p.fold > 1 else rows[0]
            one[i, part * p.blk : (part + 1) * p.blk] = rows[0 : p.blk]
            factor = rows[p.blk : 2 * p.blk]
            four[i, :, part * p.blk : (part + 1) * p.blk] = factor if part == 0 else -factor
            small[part, i] = rows[2 * p.blk : 2 * p.blk + p.yrows]
        logs = pieces[0][i, p.mrows :]
        if p.cores_share:
            other = pieces[p.fold][i, p.mrows :]
            logs = [jnp.where(core == 0, logs, other), jnp.where(core == 0, other, logs)]
            logs = jnp.concatenate(logs, axis=0)
        if p.fold > 1:
            logs = jnp.concatenate([logs] * p.fold, axis=0)
        filt[i] = jnp.exp(logs.T.astype(F32))

    each(p.nblk, one_block)


def iota(dims, axis):
    return lax.broadcasted_iota(jnp.int32, dims, axis)


def block_masks(p):
    d, nb, pairs = p.dim, p.nblk, p.pairs
    same = iota((d, d), 0) % TILE == iota((d, d), 1) // nb
    lane = iota((d, 2 * pairs), 1)
    block = iota((d, 2 * pairs), 0) // TILE
    keep_two = (lane < pairs) & (lane % nb == block)
    keep_three = (lane >= pairs) & ((lane - pairs) // nb == block)
    return same, keep_two, keep_three


def selectors(p, turned):
    d, nb, pairs = p.dim, p.nblk, p.pairs
    dims = (d, 2 * pairs) if turned else (2 * pairs, d)
    lane = iota(dims, 1 if turned else 0)
    block = iota(dims, 0 if turned else 1) % nb
    two = (lane < pairs) & (lane // nb == block)
    three = (lane >= pairs) & ((lane - pairs) % nb == block)
    return two.astype(BF16), three.astype(BF16)


def block_factor_kernel(p, small, two, three):
    same, keep_two, keep_three = block_masks(p)
    pick_two, pick_three = selectors(p, False)
    d = p.dim

    def one_group(g):
        parts = {}
        for part in range(2):
            entries = small[part, rows_at(g * TILE, TILE)]
            tiled = jnp.concatenate([entries] * p.nblk, axis=0)
            zero = jnp.zeros_like(tiled)
            for name, keep, pick in (("two", keep_two, pick_two), ("three", keep_three, pick_three)):
                spread = dot(jnp.where(keep, tiled, zero), pick, 1, 0)
                parts[name, part] = jnp.where(same, spread, 0.0).astype(BF16)
        two[g, :d, :d] = parts["two", 0]
        two[g, d:, d:] = parts["two", 0]
        two[g, :d, d:] = parts["two", 1]
        two[g, d:, :d] = -parts["two", 1]
        three[g, :d, :d] = parts["three", 0]
        three[g, d:, d:] = parts["three", 0]
        three[g, :d, d:] = -parts["three", 1]
        three[g, d:, :d] = parts["three", 1]

    each(p.kgroups, one_group)


def mixer_kernel(
    p, tokens_in, taps, one, four, two_far, three_far, filt,
    grad_x, keep, send, *refs,
):
    _, core = place(p)
    small_out = None if p.direct else refs[:2]
    (tok, ups, val, mix, groups_a, groups_b, second, time_a, gate, grad_v, filter_grad,
     gradients, small, groups_d, diagonal, *near) = refs if p.direct else refs[2:]

    def hand_out(i, base, values):
        mine = jnp.where(core == 0, values[0], values[1])
        other = jnp.where(core == 0, values[1], values[0])
        last = base + values[0].shape[0]
        for h in range(p.fold):
            lo, hi = max(base, h * p.mrows), min(last, (h + 1) * p.mrows)
            if lo < hi:
                keep[h, i, lo - h * p.mrows : hi - h * p.mrows] = mine[lo - base : hi - base]
                send[h, i, lo - h * p.mrows : hi - h * p.mrows] = other[lo - base : hi - base]

    def factor(far, at, g):
        if not p.streamed:
            return far[g]
        pltpu.sync_copy(far.at[g], near[at])
        return near[at][...]

    blk, nb, d, w, cols = p.blk, p.nblk, p.dim, p.width, p.cols
    edge = 8

    def taps_of(branch, offset):
        return taps[3 * branch + offset : 3 * branch + offset + 1, :]

    zero_edge = jnp.zeros((edge, cols), F32)
    for ref in (tok, gate, grad_v):
        ref[0:edge] = zero_edge
        ref[edge + p.length : 2 * edge + p.length] = zero_edge

    def load(i):
        both = [tokens_in[h * nb + i] for h in range(p.fold)]
        t = jnp.concatenate([b[0:w] for b in both], axis=0) if p.fold > 1 else both[0][0:w]
        u = jnp.concatenate([b[w:] for b in both], axis=0) if p.fold > 1 else both[0][w:]
        tok[rows_at(edge + i * blk, blk) if isinstance(i, int) else pl.ds(pl.multiple_of(edge + i * blk, 8), blk)] = t.T.astype(F32)
        ups[rows_at(i * blk, blk)] = u.T

    each(nb, load)

    def window(ref, i, offset):
        return ref[pl.ds(edge + i * blk + offset, blk)]

    def spread(ref, i, value):
        for part in range(2):
            for g in range(p.kgroups):
                row = part * blk + g * TILE
                ref[g, rows_at((part * nb + i) * TILE, TILE)] = value[row : row + TILE]

    def first_stage(i):
        before, here, after = (window(tok, i, o) for o in (-1, 0, 1))
        values = taps_of(0, 0) * before + taps_of(0, 1) * here + taps_of(0, 2) * after
        gating = taps_of(1, 0) * before + taps_of(1, 1) * here + taps_of(1, 2) * after
        values = values.astype(BF16)
        val[rows_at(i * blk, blk)] = values
        up = ups[rows_at(i * blk, blk)].astype(F32)
        mix[rows_at(i * blk, blk)] = (up * gating.astype(BF16).astype(F32)).astype(BF16)
        spread(groups_a, i, dot(one[i], values, 1, 0).astype(BF16))

    each(nb, first_stage)

    def filter_of(g):
        f = filt[rows_at(g * d, d)]
        return f

    def forward_middle(g):
        f = filter_of(g)
        f2 = jnp.concatenate([f, f], axis=0)
        sec = dot(factor(two_far, 0, g), groups_a[g], 0, 0)
        second[g] = sec
        groups_b[g] = (f2 * sec).astype(BF16)

    def unspread(g, value):
        for part in range(2):
            for i in range(nb):
                row = (part * nb + i) * TILE
                time_a[i, rows_at(part * blk + g * TILE, TILE)] = value[row : row + TILE]

    def forward_last(g):
        unspread(g, dot(factor(three_far, 1, g), groups_b[g], 1, 0).astype(BF16))

    def each_group(*stages):
        if p.streamed:
            each(p.kgroups, lambda g: [stage(g) for stage in stages], unrolled=False)
        else:
            for stage in stages:
                each(p.kgroups, stage)

    each_group(forward_middle, forward_last)

    def last_factor(n):
        third = time_a[n]
        last = four[n]
        mixed = dot(last, third, 1, 0)
        at = rows_at(n * blk, blk)
        gate[pl.ds(edge + n * blk, blk)] = ups[at].astype(F32) * mixed
        grads = mix[at]
        back = dot(last, grads, 0, 0).astype(BF16)
        for part in range(2):
            for g in range(p.kgroups):
                row = part * blk + g * TILE
                groups_b[p.kgroups + g, rows_at((part * nb + n) * TILE, TILE)] = back[row : row + TILE]
        products = dot(grads, third, 1, 1)
        hand_out(n, blk, (products[:, 0:blk].astype(BF16), (-products[:, blk:]).astype(BF16)))

    each(nb, last_factor)

    same, keep_two, keep_three = block_masks(p)
    pick_two, pick_three = selectors(p, True)

    def backward_middle(g):
        f = filter_of(g)
        f2 = jnp.concatenate([f, f], axis=0)
        weighted_grad = dot(factor(three_far, 1, g), groups_b[p.kgroups + g], 0, 0)
        term = weighted_grad * second[g]
        filter_grad[rows_at(g * d, d)] = f * (term[:d] + term[d:])
        groups_d[g] = (f2 * weighted_grad).astype(BF16)

    def backward_last(g):
        unspread(g, dot(factor(two_far, 0, g), groups_d[g], 1, 0).astype(BF16))

    def group_products(g):
        at = rows_at(0 if p.streamed else g * d, d)
        three = dot(groups_b[p.kgroups + g], groups_b[g], 1, 1)
        two = dot(groups_a[g], groups_d[g], 1, 1)
        for kind, real, imag in (
            (0, two[:d, :d] + two[d:, d:], two[:d, d:] - two[d:, :d]),
            (1, three[:d, :d] + three[d:, d:], three[d:, :d] - three[:d, d:]),
        ):
            diagonal[kind, 0, at] = jnp.where(same, real, 0.0).astype(BF16)
            diagonal[kind, 1, at] = jnp.where(same, imag, 0.0).astype(BF16)

    def fold_products(g):
        at = rows_at(0 if p.streamed else g * d, d)
        for part in range(2):
            two = jnp.where(keep_two, dot(diagonal[0, part, at], pick_two, 1, 0), 0.0)
            three = jnp.where(keep_three, dot(diagonal[1, part, at], pick_three, 1, 0), 0.0)
            total = jnp.sum((two + three).reshape(nb, TILE, 2 * p.pairs), axis=0)
            small[part, rows_at(g * TILE, TILE)] = total.astype(BF16)
        if p.direct:
            at = rows_at(g * TILE, TILE)
            hand_out(g, 2 * blk, (small[0, at], small[1, at]))

    each_group(backward_middle, backward_last, group_products, fold_products)

    def first_factor(i):
        first_grad = time_a[i]
        grad_v[pl.ds(edge + i * blk, blk)] = dot(one[i], first_grad, 0, 0)
        products = dot(first_grad, val[rows_at(i * blk, blk)], 1, 1).astype(BF16)
        hand_out(i, 0, (products[:blk], products[blk:]))
        used = 2 * blk + (p.yrows if p.direct else 0)
        if p.half > used:
            rest = jnp.zeros((p.half - used, blk), BF16)
            hand_out(i, used, (rest, rest))

    each(nb, first_factor)

    sums = [jnp.zeros((8, cols), F32) for _ in range(6)]

    def last_stage(i, sums):
        total = jnp.zeros((blk, cols), F32)
        sums = list(sums)
        for branch, ref in ((0, grad_v), (1, gate)):
            before, here, after = (window(ref, i, o) for o in (-1, 0, 1))
            total += taps_of(branch, 0) * after + taps_of(branch, 1) * here + taps_of(branch, 2) * before
            for offset in range(3):
                product = here * window(tok, i, offset - 1)
                sums[3 * branch + offset] += jnp.sum(product.reshape(blk // 8, 8, cols), axis=0)
        grad_x[i] = total.astype(BF16)
        terms = filter_grad[rows_at(i * blk, blk)].T
        term = terms[0:w]
        for h in range(1, p.fold):
            term = term + terms[h * w : (h + 1) * w]
        gradients[i] = term.astype(BF16)
        return tuple(sums)

    if nb <= 8:
        for i in range(nb):
            sums = last_stage(i, sums)
    else:
        sums = lax.fori_loop(0, nb, last_stage, tuple(sums))

    conv = jnp.concatenate([jnp.sum(s, axis=0, keepdims=True) for s in sums] + [jnp.zeros((2, cols), F32)], axis=0)
    term = conv[:, 0:w]
    for h in range(1, p.fold):
        term = term + conv[:, h * w : (h + 1) * w]
    if w < blk:
        term = jnp.concatenate([term, jnp.zeros((8, blk - w), F32)], axis=1)
    high = term.astype(BF16).astype(F32)
    conv_rows = jnp.concatenate([high, term - high], axis=0).astype(BF16)

    ends = [conv_rows]
    if p.full > w + TILE:
        ends.append(jnp.zeros((p.full - w - TILE, blk), BF16))

    def last_rows(i):
        rows = jnp.concatenate([gradients[i], *ends], axis=0)
        middle = p.full // 2
        mine = jnp.where(core == 0, rows[:middle], rows[middle:])
        other = jnp.where(core == 0, rows[middle:], rows[:middle])
        for h in range(p.fold):
            at = slice(h * p.orows, (h + 1) * p.orows)
            keep[h, i, p.mrows :] = mine[at]
            send[h, i, p.mrows :] = other[at]

    each(nb, last_rows)
    if not p.direct:
        small_out[0][...] = jnp.where(core == 0, small[0], small[1])
        small_out[1][...] = jnp.where(core == 0, small[1], small[0])


def token_grad_message_kernel(p, grads, out):
    def one_target(i):
        turned = grads[i].T
        for h in range(p.fold):
            out[h * p.nblk + i] = turned[h * p.width : (h + 1) * p.width]

    each(p.nblk, one_target)


def add_kernel(p, keep, got, *refs):
    out = refs[-1]

    def one_target(s):
        for h in range(p.fold):
            q = h * p.seq + s
            out[q] = (keep[h, s].astype(F32) + got[h, s].astype(F32)).astype(BF16)
            first, last = 2 * p.blk - h * p.mrows, 2 * p.blk + p.yrows - h * p.mrows
            lo, hi = max(first, 0), min(last, p.mrows)
            if not p.direct and lo < hi:
                extra = (refs[0][s].astype(F32) + refs[1][s].astype(F32)).astype(BF16)
                out[q, lo:hi] = extra[lo - first : hi - first]

    each(p.seq, one_target)


def sum_kernel(p, got, out):
    total = got[0, 0 : p.mrows].astype(F32)
    for q in range(1, p.members):
        total += got[q, 0 : p.mrows].astype(F32)
    out[0 : p.mrows] = total.astype(BF16)
    for q in range(p.members):
        at = p.mrows + q * p.orows
        out[at : at + p.orows] = got[q, p.mrows :]


def grad_x_kernel(p, got, out):
    rows = jnp.concatenate([got[q] for q in range(p.members)], axis=0)
    out[...] = rows.T


def finish_kernel(p, *refs):
    pieces, outs = refs[: 2 * p.fold], refs[2 * p.fold :]
    one, four, filt, conv_value, conv_gate, *small = outs
    share = shares_in_order(p, pieces)
    for part in range(2):
        rows = [share(part, owner, lambda ref, *_: ref[0 : p.mrows]) for owner in range(p.fold)]
        rows = jnp.concatenate(rows, axis=0) if p.fold > 1 else rows[0]
        one[part] = rows[0 : p.blk]
        four[part] = rows[p.blk : 2 * p.blk]
        entries = rows[2 * p.blk : 2 * p.blk + p.yrows]
        if p.direct:
            entries = entries.T
            small[0][part] = entries[: p.pairs]
            small[1][part] = entries[p.pairs :]
        else:
            small[0][part] = entries
    turned, columns = [], []
    for q in range(p.members):
        first = p.mrows + q * p.orows
        rows = [
            share(c, owner, lambda ref, *_: ref[first : first + p.orows])
            for c in range(2)
            for owner in range(p.fold)
        ]
        rows = jnp.concatenate(rows, axis=0)
        turned.append(rows[0 : p.width])
        both = rows[p.width : p.width + TILE].astype(F32)
        columns.append((both[:8] + both[8:]).T[: p.width])
    filt[...] = jnp.concatenate(turned, axis=0).T
    sums = jnp.concatenate(columns, axis=0).T
    conv_value[...] = sums[0:3]
    conv_gate[...] = sums[3:6]


def shards(
    tokens, upstream, conv_value, conv_gate, mix_one, mix_two, mix_three, mix_four, filter_log
):
    p = Plan(lax.axis_size("dp"), lax.axis_size("seq"), tokens, mix_one, mix_two)
    dp_at, seq_at = lax.axis_index("dp"), lax.axis_index("seq")
    h_at = (dp_at // 2) % p.fold
    blk, pairs = p.blk, p.pairs

    def shuffle(array):
        return lax.all_to_all(
            array, ("dp", "seq"), 0, 0, tiled=True, axis_index_groups=p.group_lists
        )

    def swap(array):
        return lax.ppermute(array, "dp", p.across_cores())

    def gathered(array, rows):
        pieces = [array]
        for step in range(1, p.fold):
            pieces.append(lax.ppermute(rows(array), "dp", p.across_fold(step)))
        return pieces + [swap(piece) for piece in pieces]

    if p.direct:
        small = [f.transpose(0, 2, 3, 1).reshape(2, pairs, p.kloc) for f in (mix_two, mix_three)]
    else:
        small = [f.reshape(2, p.kloc, pairs) for f in (mix_two, mix_three)]
        small = [jnp.concatenate(small, axis=2).reshape(2, p.yrows, blk)]
    far = [
        filter_log.reshape(blk, p.channels),
        mix_one.reshape(2, blk, blk),
        mix_four.reshape(2, blk, blk),
        *small,
    ]
    message = call(
        functools.partial(factor_message_kernel, p),
        shape(p.seq, p.mrows + p.frows, blk),
        *far,
        scratch=[pltpu.VMEM((blk, p.channels // p.fold), BF16)]
        + [pltpu.VMEM(f.shape[1:], BF16) for f in far[1:]]
        + [
            pltpu.VMEM((p.half, blk), BF16),
            pltpu.VMEM((p.channels // p.fold, blk), BF16),
            pltpu.SemaphoreType.DMA((len(far),)),
        ],
        far=range(len(far)),
        limit=60,
        name="factor_message",
    )
    factors = lax.all_to_all(message, "seq", 0, 0, tiled=True)
    pieces = gathered(factors, lambda a: a[:, : p.mrows])

    message = call(
        functools.partial(token_message_kernel, p),
        shape(p.members, 2 * p.width, blk),
        tokens[0],
        upstream[0],
        name="token_message",
    )
    received = shuffle(message)
    pieces, received = lax.optimization_barrier((pieces, received))
    one, four, small, filt = call(
        functools.partial(prepare_kernel, p),
        [
            shape(p.nblk, 2 * blk, blk),
            shape(p.nblk, blk, 2 * blk),
            shape(2, p.nblk, p.yrows, blk),
            shape(p.nblk, blk, p.cols, dtype=F32),
        ],
        *pieces,
        name="prepare",
    )
    two, three = call(
        functools.partial(block_factor_kernel, p),
        [shape(p.kgroups, 2 * p.dim, 2 * p.dim)] * 2,
        small.reshape(2, blk, 2 * pairs),
        limit=48 if p.streamed else 20,
        name="block_factors",
    )

    start = (h_at * p.seq + seq_at) * p.width
    taps = jnp.concatenate([conv_value, conv_gate], axis=0)
    taps = lax.dynamic_slice_in_dim(taps, start, p.width, 1)
    taps = jnp.concatenate([taps] * p.fold, axis=1)

    padded = p.length + 16
    grad_x, keep, send, *small = call(
        functools.partial(mixer_kernel, p),
        [
            shape(p.nblk, blk, p.cols),
            shape(p.fold, p.seq, p.share, blk),
            shape(p.fold, p.seq, p.share, blk),
        ]
        + [shape(blk, 2 * pairs)] * (0 if p.direct else 2),
        received,
        taps,
        one,
        four,
        two,
        three,
        filt.reshape(p.length, p.cols),
        scratch=[
            pltpu.VMEM((padded, p.cols), F32),
            pltpu.VMEM((p.length, p.cols), BF16),
            pltpu.VMEM((p.length, p.cols), BF16),
            pltpu.VMEM((p.length, p.cols), BF16),
            pltpu.VMEM((p.kgroups, 2 * p.dim, p.cols), BF16),
            pltpu.VMEM((2 * p.kgroups, 2 * p.dim, p.cols), BF16),
            pltpu.VMEM((p.kgroups, 2 * p.dim, p.cols), F32),
            pltpu.VMEM((p.nblk, 2 * blk, p.cols), BF16),
            pltpu.VMEM((padded, p.cols), F32),
            pltpu.VMEM((padded, p.cols), F32),
            pltpu.VMEM((p.length, p.cols), F32),
            pltpu.VMEM((p.nblk, p.width, blk), BF16),
            pltpu.VMEM((2, blk, 2 * pairs), BF16),
            pltpu.VMEM((p.kgroups, 2 * p.dim, p.cols), BF16),
            pltpu.VMEM((2, 2, (1 if p.streamed else p.kgroups) * p.dim, p.dim), BF16),
        ]
        + [pltpu.VMEM((2 * p.dim, 2 * p.dim), BF16)] * (2 if p.streamed else 0),
        far=(4, 5) if p.streamed else (),
        limit=60 if p.streamed else 20,
        name="mixer",
    )

    message = call(
        functools.partial(add_kernel, p),
        shape(p.members, p.share, blk),
        keep,
        swap(send),
        *[f.reshape(p.seq, p.yrows, blk) for f in (small if p.direct else (small[0], swap(small[1])))],
        name="add_cores",
    )
    received = shuffle(message)
    grad_x = call(
        functools.partial(token_grad_message_kernel, p),
        shape(p.members, p.width, blk),
        grad_x,
        name="token_grad_message",
    )
    received, grad_x = lax.optimization_barrier((received, grad_x))
    grad_x = shuffle(grad_x)
    sums = call(
        functools.partial(sum_kernel, p),
        shape(p.mrows + p.members * p.orows, blk),
        received,
        name="sum_sources",
    )
    if p.groups > 1:
        total = sums.astype(F32)
        for step in range(1, p.groups):
            total += lax.ppermute(sums, "dp", p.across_groups(step)).astype(F32)
        sums = total.astype(BF16)
    pieces = gathered(sums, lambda a: a)
    token_grad = call(
        functools.partial(grad_x_kernel, p), shape(blk, p.channels), grad_x, name="token_grad"
    )
    grad_one, grad_four, grad_filter, sum_value, sum_gate, *small = call(
        functools.partial(finish_kernel, p),
        [
            shape(2, blk, blk),
            shape(2, blk, blk),
            shape(blk, p.channels),
            shape(3, p.channels, dtype=F32),
            shape(3, p.channels, dtype=F32),
        ]
        + ([shape(2, pairs, p.kloc)] * 2 if p.direct else [shape(2, p.yrows, blk)]),
        *pieces,
        name="finish",
    )
    if p.direct:
        small = [f.reshape(2, p.nblk, p.nblk, p.kloc).transpose(0, 3, 1, 2) for f in small]
    else:
        small = small[0].reshape(2, p.kloc, 2, p.nblk, p.nblk)
        small = [small[:, :, 0], small[:, :, 1]]
    return (
        token_grad[None],
        sum_value,
        sum_gate,
        grad_one.reshape(mix_one.shape),
        *small,
        grad_four.reshape(mix_four.shape),
        grad_filter.reshape(filter_log.shape),
    )


def solution(mesh):
    return jax.shard_map(
        shards,
        mesh=mesh,
        in_specs=(
            P("dp", "seq", None),
            P("dp", "seq", None),
            P(),
            P(),
            P(None, "seq", None, None),
            P(None, "seq", None, None),
            P(None, "seq", None, None),
            P(None, "seq", None, None),
            P("seq", None, None),
        ),
        out_specs=(
            P("dp", "seq", None),
            P(),
            P(),
            P(None, "seq", None, None),
            P(None, "seq", None, None),
            P(None, "seq", None, None),
            P(None, "seq", None, None),
            P("seq", None, None),
        ),
        check_vma=False,
    )
```

```python
import functools

import jax
import jax.numpy as jnp
from jax import lax
from jax.experimental import pallas as pl
from jax.experimental.pallas import tpu as pltpu
from jax.sharding import PartitionSpec as P

F32 = jnp.float32
BF16 = jnp.bfloat16
TILE = 16
VMEM = pl.BlockSpec(memory_space=pltpu.VMEM)
FAR = pl.BlockSpec(memory_space=pl.ANY)


class Plan:
    def __init__(self, dp, seq, tokens, mix_one, mix_two):
        self.dp, self.seq = dp, seq
        self.blk = mix_one.shape[-1]
        self.channels = tokens.shape[-1]
        assert tokens.shape[1] == self.blk and dp % 2 == 0
        self.nblk = seq
        self.kloc = mix_two.shape[1]
        half_dp = dp // 2
        self.fold = max(
            f
            for f in range(1, half_dp + 1)
            if half_dp % f == 0 and self.channels % (seq * f * TILE) == 0
        )
        self.groups = half_dp // self.fold
        self.members = self.fold * seq
        self.width = self.channels // self.members
        assert self.width <= 128
        self.cols = self.fold * self.width
        self.length = self.nblk * self.blk
        self.pairs = self.nblk * self.nblk
        self.yrows = self.kloc * 2 * self.pairs // self.blk
        self.direct = self.yrows == self.kloc
        self.streamed = self.nblk * TILE > self.blk
        self.kgroups = self.blk // TILE
        self.dim = self.nblk * TILE
        unit = TILE * self.fold
        self.half = -(-(2 * self.blk + self.yrows) // unit) * unit
        self.mrows = self.half // self.fold
        self.cores_share = self.width % (2 * TILE) == 0
        self.frows = self.width // 2 if self.cores_share else self.width
        self.full = -(-(self.width + TILE) // (2 * unit)) * 2 * unit
        self.orows = self.full // (2 * self.fold)
        self.share = self.mrows + self.orows
        self.group_lists = [
            [
                ((g * self.fold + h) * 2 + core) * seq + s
                for h in range(self.fold)
                for s in range(seq)
            ]
            for g in range(self.groups)
            for core in range(2)
        ]

    def across_cores(self):
        return [(d, d ^ 1) for d in range(self.dp)]

    def across_fold(self, step):
        moves = []
        for g in range(self.groups):
            for h in range(self.fold):
                for core in range(2):
                    source = (g * self.fold + h) * 2 + core
                    moves.append((source, (g * self.fold + (h + step) % self.fold) * 2 + core))
        return moves

    def across_groups(self, step):
        block = 2 * self.fold
        return [(d, (d + step * block) % self.dp) for d in range(self.dp)]


def each(count, body, unrolled=True):
    if count <= 8 and unrolled:
        for i in range(count):
            body(i)
    else:
        lax.fori_loop(0, count, lambda i, c: (body(i), c)[1], 0)


def rows_at(start, size):
    return pl.ds(start if isinstance(start, int) else pl.multiple_of(start, TILE), size)


def dot(a, b, ca, cb):
    return lax.dot_general(a, b, (((ca,), (cb,)), ((), ())), preferred_element_type=F32)


def call(kernel, out_shape, *args, scratch=(), far=(), limit=24, name=None):
    single = not isinstance(out_shape, (list, tuple))
    return pl.pallas_call(
        kernel,
        out_shape=out_shape,
        in_specs=[FAR if i in far else VMEM for i in range(len(args))],
        out_specs=VMEM if single else [VMEM] * len(out_shape),
        scratch_shapes=list(scratch),
        compiler_params=pltpu.CompilerParams(vmem_limit_bytes=limit * 2**20),
        name=name,
    )(*args)


def shape(*dims, dtype=BF16):
    return jax.ShapeDtypeStruct(dims, dtype)


def place(p):
    at = lax.axis_index("dp")
    return (at // 2) % p.fold, at % 2


def factor_message_kernel(p, *refs):
    count = 5 if p.direct else 4
    far, out, near, rows, turned, done = refs[:count], refs[count], refs[count + 1 : -3], *refs[-3:]
    h, core = place(p)
    part_width = p.seq * p.width
    sources = [far[0].at[:, pl.ds(pl.multiple_of(h * part_width, p.blk), part_width)]]
    sources += [f.at[core] for f in far[1:]]
    copies = [pltpu.make_async_copy(f, n, done.at[i]) for i, (f, n) in enumerate(zip(sources, near))]
    for copy in copies:
        copy.start()
    filt, one, four = near[:3]
    for copy in copies[1:]:
        copy.wait()
    rows[0 : p.blk] = one[...]
    rows[p.blk : 2 * p.blk] = four[...]
    if p.direct:
        small = jnp.concatenate([near[3][...], near[4][...]], axis=0).T
    else:
        small = near[3][...]
    rows[2 * p.blk : 2 * p.blk + p.yrows] = small
    pad = p.half - 2 * p.blk - p.yrows
    if pad:
        rows[p.half - pad :] = jnp.zeros((pad, p.blk), BF16)
    mine = rows[0 : p.mrows]
    for owner in range(1, p.fold):
        mine = jnp.where(h == owner, rows[owner * p.mrows : (owner + 1) * p.mrows], mine)
    copies[0].wait()
    turned[...] = filt[...].T

    def one_target(s):
        out[s, 0 : p.mrows] = mine
        logs = turned[rows_at(s * p.width, p.width)]
        if p.cores_share:
            logs = jnp.where(core == 0, logs[: p.frows], logs[p.frows :])
        out[s, p.mrows :] = logs

    each(p.seq, one_target)


def token_message_kernel(p, tokens, upstream, out):
    w = p.width
    token_rows = tokens[...].T
    upstream_rows = upstream[...].T
    for q in range(p.members):
        out[q, 0:w] = token_rows[q * w : (q + 1) * w]
        out[q, w : 2 * w] = upstream_rows[q * w : (q + 1) * w]


def shares_in_order(p, pieces):
    h, core = place(p)

    def share(c, owner, part):
        value = None
        for side in range(2):
            for step in range(p.fold):
                piece = part(pieces[side * p.fold + step], side, step)
                if value is None:
                    value = piece
                    continue
                here = core == (c if side == 0 else 1 - c)
                value = jnp.where(here & (h == (owner + step) % p.fold), piece, value)
        return value

    return share


def prepare_kernel(p, *refs):
    pieces, (one, four, small, filt) = refs[: 2 * p.fold], refs[2 * p.fold :]
    share = shares_in_order(p, pieces)
    _, core = place(p)

    def one_block(i):
        for part in range(2):
            rows = [share(part, owner, lambda ref, *_: ref[i, 0 : p.mrows]) for owner in range(p.fold)]
            rows = jnp.concatenate(rows, axis=0) if p.fold > 1 else rows[0]
            one[i, part * p.blk : (part + 1) * p.blk] = rows[0 : p.blk]
            factor = rows[p.blk : 2 * p.blk]
            four[i, :, part * p.blk : (part + 1) * p.blk] = factor if part == 0 else -factor
            small[part, i] = rows[2 * p.blk : 2 * p.blk + p.yrows]
        logs = pieces[0][i, p.mrows :]
        if p.cores_share:
            other = pieces[p.fold][i, p.mrows :]
            logs = [jnp.where(core == 0, logs, other), jnp.where(core == 0, other, logs)]
            logs = jnp.concatenate(logs, axis=0)
        if p.fold > 1:
            logs = jnp.concatenate([logs] * p.fold, axis=0)
        filt[i] = jnp.exp(logs.T.astype(F32))

    each(p.nblk, one_block)


def iota(dims, axis):
    return lax.broadcasted_iota(jnp.int32, dims, axis)


def block_masks(p):
    d, nb, pairs = p.dim, p.nblk, p.pairs
    same = iota((d, d), 0) % TILE == iota((d, d), 1) // nb
    lane = iota((d, 2 * pairs), 1)
    block = iota((d, 2 * pairs), 0) // TILE
    keep_two = (lane < pairs) & (lane % nb == block)
    keep_three = (lane >= pairs) & ((lane - pairs) // nb == block)
    return same, keep_two, keep_three


def selectors(p, turned):
    d, nb, pairs = p.dim, p.nblk, p.pairs
    dims = (d, 2 * pairs) if turned else (2 * pairs, d)
    lane = iota(dims, 1 if turned else 0)
    block = iota(dims, 0 if turned else 1) % nb
    two = (lane < pairs) & (lane // nb == block)
    three = (lane >= pairs) & ((lane - pairs) % nb == block)
    return two.astype(BF16), three.astype(BF16)


def block_factor_kernel(p, small, two, three):
    same, keep_two, keep_three = block_masks(p)
    pick_two, pick_three = selectors(p, False)
    d = p.dim

    def one_group(g):
        parts = {}
        for part in range(2):
            entries = small[part, rows_at(g * TILE, TILE)]
            tiled = jnp.concatenate([entries] * p.nblk, axis=0)
            zero = jnp.zeros_like(tiled)
            for name, keep, pick in (("two", keep_two, pick_two), ("three", keep_three, pick_three)):
                spread = dot(jnp.where(keep, tiled, zero), pick, 1, 0)
                parts[name, part] = jnp.where(same, spread, 0.0).astype(BF16)
        two[g, :d, :d] = parts["two", 0]
        two[g, d:, d:] = parts["two", 0]
        two[g, :d, d:] = parts["two", 1]
        two[g, d:, :d] = -parts["two", 1]
        three[g, :d, :d] = parts["three", 0]
        three[g, d:, d:] = parts["three", 0]
        three[g, :d, d:] = -parts["three", 1]
        three[g, d:, :d] = parts["three", 1]

    each(p.kgroups, one_group)


def mixer_kernel(
    p, tokens_in, taps, one, four, two_far, three_far, filt,
    grad_x, keep, send, *refs,
):
    _, core = place(p)
    small_out = None if p.direct else refs[:2]
    (tok, ups, val, mix, groups_a, groups_b, second, time_a, gate, grad_v, filter_grad,
     gradients, small, groups_d, diagonal, *near) = refs if p.direct else refs[2:]

    def hand_out(i, base, values):
        mine = jnp.where(core == 0, values[0], values[1])
        other = jnp.where(core == 0, values[1], values[0])
        last = base + values[0].shape[0]
        for h in range(p.fold):
            lo, hi = max(base, h * p.mrows), min(last, (h + 1) * p.mrows)
            if lo < hi:
                keep[h, i, lo - h * p.mrows : hi - h * p.mrows] = mine[lo - base : hi - base]
                send[h, i, lo - h * p.mrows : hi - h * p.mrows] = other[lo - base : hi - base]

    def factor(far, at, g):
        if not p.streamed:
            return far[g]
        pltpu.sync_copy(far.at[g], near[at])
        return near[at][...]

    blk, nb, d, w, cols = p.blk, p.nblk, p.dim, p.width, p.cols
    edge = 8

    def taps_of(branch, offset):
        return taps[3 * branch + offset : 3 * branch + offset + 1, :]

    zero_edge = jnp.zeros((edge, cols), F32)
    for ref in (tok, gate, grad_v):
        ref[0:edge] = zero_edge
        ref[edge + p.length : 2 * edge + p.length] = zero_edge

    def load(i):
        both = [tokens_in[h * nb + i] for h in range(p.fold)]
        t = jnp.concatenate([b[0:w] for b in both], axis=0) if p.fold > 1 else both[0][0:w]
        u = jnp.concatenate([b[w:] for b in both], axis=0) if p.fold > 1 else both[0][w:]
        tok[rows_at(edge + i * blk, blk) if isinstance(i, int) else pl.ds(pl.multiple_of(edge + i * blk, 8), blk)] = t.T.astype(F32)
        ups[rows_at(i * blk, blk)] = u.T

    each(nb, load)

    def window(ref, i, offset):
        return ref[pl.ds(edge + i * blk + offset, blk)]

    def spread(ref, i, value):
        for part in range(2):
            for g in range(p.kgroups):
                row = part * blk + g * TILE
                ref[g, rows_at((part * nb + i) * TILE, TILE)] = value[row : row + TILE]

    def first_stage(i):
        before, here, after = (window(tok, i, o) for o in (-1, 0, 1))
        values = taps_of(0, 0) * before + taps_of(0, 1) * here + taps_of(0, 2) * after
        gating = taps_of(1, 0) * before + taps_of(1, 1) * here + taps_of(1, 2) * after
        values = values.astype(BF16)
        val[rows_at(i * blk, blk)] = values
        up = ups[rows_at(i * blk, blk)].astype(F32)
        mix[rows_at(i * blk, blk)] = (up * gating.astype(BF16).astype(F32)).astype(BF16)
        spread(groups_a, i, dot(one[i], values, 1, 0).astype(BF16))

    each(nb, first_stage)

    def filter_of(g):
        f = filt[rows_at(g * d, d)]
        return f

    def forward_middle(g):
        f = filter_of(g)
        f2 = jnp.concatenate([f, f], axis=0)
        sec = dot(factor(two_far, 0, g), groups_a[g], 0, 0)
        second[g] = sec
        groups_b[g] = (f2 * sec).astype(BF16)

    def unspread(g, value):
        for part in range(2):
            for i in range(nb):
                row = (part * nb + i) * TILE
                time_a[i, rows_at(part * blk + g * TILE, TILE)] = value[row : row + TILE]

    def forward_last(g):
        unspread(g, dot(factor(three_far, 1, g), groups_b[g], 1, 0).astype(BF16))

    def each_group(*stages):
        if p.streamed:
            each(p.kgroups, lambda g: [stage(g) for stage in stages], unrolled=False)
        else:
            for stage in stages:
                each(p.kgroups, stage)

    each_group(forward_middle, forward_last)

    def last_factor(n):
        third = time_a[n]
        last = four[n]
        mixed = dot(last, third, 1, 0)
        at = rows_at(n * blk, blk)
        gate[pl.ds(edge + n * blk, blk)] = ups[at].astype(F32) * mixed
        grads = mix[at]
        back = dot(last, grads, 0, 0).astype(BF16)
        for part in range(2):
            for g in range(p.kgroups):
                row = part * blk + g * TILE
                groups_b[p.kgroups + g, rows_at((part * nb + n) * TILE, TILE)] = back[row : row + TILE]
        products = dot(grads, third, 1, 1)
        hand_out(n, blk, (products[:, 0:blk].astype(BF16), (-products[:, blk:]).astype(BF16)))

    each(nb, last_factor)

    same, keep_two, keep_three = block_masks(p)
    pick_two, pick_three = selectors(p, True)

    def backward_middle(g):
        f = filter_of(g)
        f2 = jnp.concatenate([f, f], axis=0)
        weighted_grad = dot(factor(three_far, 1, g), groups_b[p.kgroups + g], 0, 0)
        term = weighted_grad * second[g]
        filter_grad[rows_at(g * d, d)] = f * (term[:d] + term[d:])
        groups_d[g] = (f2 * weighted_grad).astype(BF16)

    def backward_last(g):
        unspread(g, dot(factor(two_far, 0, g), groups_d[g], 1, 0).astype(BF16))

    def group_products(g):
        at = rows_at(0 if p.streamed else g * d, d)
        three = dot(groups_b[p.kgroups + g], groups_b[g], 1, 1)
        two = dot(groups_a[g], groups_d[g], 1, 1)
        for kind, real, imag in (
            (0, two[:d, :d] + two[d:, d:], two[:d, d:] - two[d:, :d]),
            (1, three[:d, :d] + three[d:, d:], three[d:, :d] - three[:d, d:]),
        ):
            diagonal[kind, 0, at] = jnp.where(same, real, 0.0).astype(BF16)
            diagonal[kind, 1, at] = jnp.where(same, imag, 0.0).astype(BF16)

    def fold_products(g):
        at = rows_at(0 if p.streamed else g * d, d)
        for part in range(2):
            two = jnp.where(keep_two, dot(diagonal[0, part, at], pick_two, 1, 0), 0.0)
            three = jnp.where(keep_three, dot(diagonal[1, part, at], pick_three, 1, 0), 0.0)
            total = jnp.sum((two + three).reshape(nb, TILE, 2 * p.pairs), axis=0)
            small[part, rows_at(g * TILE, TILE)] = total.astype(BF16)
        if p.direct:
            at = rows_at(g * TILE, TILE)
            hand_out(g, 2 * blk, (small[0, at], small[1, at]))

    each_group(backward_middle, backward_last, group_products, fold_products)

    def first_factor(i):
        first_grad = time_a[i]
        grad_v[pl.ds(edge + i * blk, blk)] = dot(one[i], first_grad, 0, 0)
        products = dot(first_grad, val[rows_at(i * blk, blk)], 1, 1).astype(BF16)
        hand_out(i, 0, (products[:blk], products[blk:]))
        used = 2 * blk + (p.yrows if p.direct else 0)
        if p.half > used:
            rest = jnp.zeros((p.half - used, blk), BF16)
            hand_out(i, used, (rest, rest))

    each(nb, first_factor)

    sums = [jnp.zeros((8, cols), F32) for _ in range(6)]

    def last_stage(i, sums):
        total = jnp.zeros((blk, cols), F32)
        sums = list(sums)
        for branch, ref in ((0, grad_v), (1, gate)):
            before, here, after = (window(ref, i, o) for o in (-1, 0, 1))
            total += taps_of(branch, 0) * after + taps_of(branch, 1) * here + taps_of(branch, 2) * before
            for offset in range(3):
                product = here * window(tok, i, offset - 1)
                sums[3 * branch + offset] += jnp.sum(product.reshape(blk // 8, 8, cols), axis=0)
        grad_x[i] = total.astype(BF16)
        terms = filter_grad[rows_at(i * blk, blk)].T
        term = terms[0:w]
        for h in range(1, p.fold):
            term = term + terms[h * w : (h + 1) * w]
        gradients[i] = term.astype(BF16)
        return tuple(sums)

    if nb <= 8:
        for i in range(nb):
            sums = last_stage(i, sums)
    else:
        sums = lax.fori_loop(0, nb, last_stage, tuple(sums))

    conv = jnp.concatenate([jnp.sum(s, axis=0, keepdims=True) for s in sums] + [jnp.zeros((2, cols), F32)], axis=0)
    term = conv[:, 0:w]
    for h in range(1, p.fold):
        term = term + conv[:, h * w : (h + 1) * w]
    if w < blk:
        term = jnp.concatenate([term, jnp.zeros((8, blk - w), F32)], axis=1)
    high = term.astype(BF16).astype(F32)
    conv_rows = jnp.concatenate([high, term - high], axis=0).astype(BF16)

    ends = [conv_rows]
    if p.full > w + TILE:
        ends.append(jnp.zeros((p.full - w - TILE, blk), BF16))

    def last_rows(i):
        rows = jnp.concatenate([gradients[i], *ends], axis=0)
        middle = p.full // 2
        mine = jnp.where(core == 0, rows[:middle], rows[middle:])
        other = jnp.where(core == 0, rows[middle:], rows[:middle])
        for h in range(p.fold):
            at = slice(h * p.orows, (h + 1) * p.orows)
            keep[h, i, p.mrows :] = mine[at]
            send[h, i, p.mrows :] = other[at]

    each(nb, last_rows)
    if not p.direct:
        small_out[0][...] = jnp.where(core == 0, small[0], small[1])
        small_out[1][...] = jnp.where(core == 0, small[1], small[0])


def token_grad_message_kernel(p, grads, out):
    def one_target(i):
        turned = grads[i].T
        for h in range(p.fold):
            out[h * p.nblk + i] = turned[h * p.width : (h + 1) * p.width]

    each(p.nblk, one_target)


def pick(p, values, wanted):
    value = values[0]
    for i in range(1, len(values)):
        value = jnp.where(wanted == i, values[i], value)
    return value


def add_cores_kernel(p, grad_x, keep, got, *refs):
    count = 0 if p.direct else 2
    out, shares = refs[count], refs[count + 1 :]
    h, _ = place(p)

    def one_target(s):
        rows = []
        for owner in range(p.fold):
            q = owner * p.seq + s
            total = (keep[owner, s].astype(F32) + got[owner, s].astype(F32)).astype(BF16)
            out[q, 0 : p.width] = grad_x[q]
            out[q, p.width :] = total[p.mrows :]
            total = total[: p.mrows]
            first, last = 2 * p.blk - owner * p.mrows, 2 * p.blk + p.yrows - owner * p.mrows
            lo, hi = max(first, 0), min(last, p.mrows)
            if not p.direct and lo < hi:
                extra = (refs[0][s].astype(F32) + refs[1][s].astype(F32)).astype(BF16)
                parts = [total[:lo], extra[lo - first : hi - first], total[hi:]]
                total = jnp.concatenate([part for part in parts if part.shape[0]], axis=0)
            rows.append(total)
        for step in range(p.fold):
            shares[step][s] = pick(p, [rows[(i + step) % p.fold] for i in range(p.fold)], h)

    each(p.seq, one_target)


def add_fold_kernel(p, *refs):
    terms, out = refs[:-1], refs[-1]

    def one_target(s):
        total = terms[0][s].astype(F32)
        for term in terms[1:]:
            total += term[s].astype(F32)
        out[s] = total.astype(BF16)

    each(p.seq, one_target)


def sum_kernel(p, got, out):
    total = got[0].astype(F32)
    for q in range(1, p.seq):
        total += got[q].astype(F32)
    out[...] = total.astype(BF16)


def filter_rows_kernel(p, got, out):
    for q in range(p.members):
        out[q] = got[q, p.width :]


def token_grad_kernel(p, got, out):
    rows = jnp.concatenate([got[q, 0 : p.width] for q in range(p.members)], axis=0)
    out[...] = rows.T


def finish_factors_kernel(p, *refs):
    pieces, (one, four, *small) = refs[: 2 * p.fold], refs[2 * p.fold :]
    share = shares_in_order(p, pieces)
    for part in range(2):
        rows = [share(part, owner, lambda ref, *_: ref[...]) for owner in range(p.fold)]
        rows = jnp.concatenate(rows, axis=0) if p.fold > 1 else rows[0]
        one[part] = rows[0 : p.blk]
        four[part] = rows[p.blk : 2 * p.blk]
        entries = rows[2 * p.blk : 2 * p.blk + p.yrows]
        if p.direct:
            entries = entries.T
            small[0][part] = entries[: p.pairs]
            small[1][part] = entries[p.pairs :]
        else:
            small[0][part] = entries


def finish_filter_kernel(p, *refs):
    pieces, (filt, conv_value, conv_gate) = refs[: 2 * p.fold], refs[2 * p.fold :]
    share = shares_in_order(p, pieces)
    turned, columns = [], []
    for q in range(p.members):
        rows = [
            share(c, owner, lambda ref, *_: ref[q]) for c in range(2) for owner in range(p.fold)
        ]
        rows = jnp.concatenate(rows, axis=0)
        turned.append(rows[0 : p.width])
        both = rows[p.width : p.width + TILE].astype(F32)
        columns.append((both[:8] + both[8:]).T[: p.width])
    filt[...] = jnp.concatenate(turned, axis=0).T
    sums = jnp.concatenate(columns, axis=0).T
    conv_value[...] = sums[0:3]
    conv_gate[...] = sums[3:6]


def shards(
    tokens, upstream, conv_value, conv_gate, mix_one, mix_two, mix_three, mix_four, filter_log
):
    p = Plan(lax.axis_size("dp"), lax.axis_size("seq"), tokens, mix_one, mix_two)
    dp_at, seq_at = lax.axis_index("dp"), lax.axis_index("seq")
    h_at = (dp_at // 2) % p.fold
    blk, pairs = p.blk, p.pairs

    def shuffle(array):
        return lax.all_to_all(
            array, ("dp", "seq"), 0, 0, tiled=True, axis_index_groups=p.group_lists
        )

    def swap(array):
        return lax.ppermute(array, "dp", p.across_cores())

    def gathered(array, rows):
        pieces = [array]
        for step in range(1, p.fold):
            pieces.append(lax.ppermute(rows(array), "dp", p.across_fold(step)))
        return pieces + [swap(piece) for piece in pieces]

    if p.direct:
        small = [f.transpose(0, 2, 3, 1).reshape(2, pairs, p.kloc) for f in (mix_two, mix_three)]
    else:
        small = [f.reshape(2, p.kloc, pairs) for f in (mix_two, mix_three)]
        small = [jnp.concatenate(small, axis=2).reshape(2, p.yrows, blk)]
    far = [
        filter_log.reshape(blk, p.channels),
        mix_one.reshape(2, blk, blk),
        mix_four.reshape(2, blk, blk),
        *small,
    ]
    message = call(
        functools.partial(factor_message_kernel, p),
        shape(p.seq, p.mrows + p.frows, blk),
        *far,
        scratch=[pltpu.VMEM((blk, p.channels // p.fold), BF16)]
        + [pltpu.VMEM(f.shape[1:], BF16) for f in far[1:]]
        + [
            pltpu.VMEM((p.half, blk), BF16),
            pltpu.VMEM((p.channels // p.fold, blk), BF16),
            pltpu.SemaphoreType.DMA((len(far),)),
        ],
        far=range(len(far)),
        limit=60,
        name="factor_message",
    )
    factors = lax.all_to_all(message, "seq", 0, 0, tiled=True)
    pieces = gathered(factors, lambda a: a[:, : p.mrows])

    message = call(
        functools.partial(token_message_kernel, p),
        shape(p.members, 2 * p.width, blk),
        tokens[0],
        upstream[0],
        name="token_message",
    )
    received = shuffle(message)
    pieces, received = lax.optimization_barrier((pieces, received))
    one, four, small, filt = call(
        functools.partial(prepare_kernel, p),
        [
            shape(p.nblk, 2 * blk, blk),
            shape(p.nblk, blk, 2 * blk),
            shape(2, p.nblk, p.yrows, blk),
            shape(p.nblk, blk, p.cols, dtype=F32),
        ],
        *pieces,
        name="prepare",
    )
    two, three = call(
        functools.partial(block_factor_kernel, p),
        [shape(p.kgroups, 2 * p.dim, 2 * p.dim)] * 2,
        small.reshape(2, blk, 2 * pairs),
        limit=48 if p.streamed else 24,
        name="block_factors",
    )

    start = (h_at * p.seq + seq_at) * p.width
    taps = jnp.concatenate([conv_value, conv_gate], axis=0)
    taps = lax.dynamic_slice_in_dim(taps, start, p.width, 1)
    taps = jnp.concatenate([taps] * p.fold, axis=1)

    padded = p.length + 16
    grad_x, keep, send, *small = call(
        functools.partial(mixer_kernel, p),
        [
            shape(p.nblk, blk, p.cols),
            shape(p.fold, p.seq, p.share, blk),
            shape(p.fold, p.seq, p.share, blk),
        ]
        + [shape(blk, 2 * pairs)] * (0 if p.direct else 2),
        received,
        taps,
        one,
        four,
        two,
        three,
        filt.reshape(p.length, p.cols),
        scratch=[
            pltpu.VMEM((padded, p.cols), F32),
            pltpu.VMEM((p.length, p.cols), BF16),
            pltpu.VMEM((p.length, p.cols), BF16),
            pltpu.VMEM((p.length, p.cols), BF16),
            pltpu.VMEM((p.kgroups, 2 * p.dim, p.cols), BF16),
            pltpu.VMEM((2 * p.kgroups, 2 * p.dim, p.cols), BF16),
            pltpu.VMEM((p.kgroups, 2 * p.dim, p.cols), F32),
            pltpu.VMEM((p.nblk, 2 * blk, p.cols), BF16),
            pltpu.VMEM((padded, p.cols), F32),
            pltpu.VMEM((padded, p.cols), F32),
            pltpu.VMEM((p.length, p.cols), F32),
            pltpu.VMEM((p.nblk, p.width, blk), BF16),
            pltpu.VMEM((2, blk, 2 * pairs), BF16),
            pltpu.VMEM((p.kgroups, 2 * p.dim, p.cols), BF16),
            pltpu.VMEM((2, 2, (1 if p.streamed else p.kgroups) * p.dim, p.dim), BF16),
        ]
        + [pltpu.VMEM((2 * p.dim, 2 * p.dim), BF16)] * (2 if p.streamed else 0),
        far=(4, 5) if p.streamed else (),
        limit=60 if p.streamed else 24,
        name="mixer",
    )

    def summed_over_groups(array):
        if p.groups == 1:
            return array
        total = array.astype(F32)
        for step in range(1, p.groups):
            total += lax.ppermute(array, "dp", p.across_groups(step)).astype(F32)
        return total.astype(BF16)

    grad_x = call(
        functools.partial(token_grad_message_kernel, p),
        shape(p.members, p.width, blk),
        grad_x,
        name="token_grad_message",
    )
    message, *shares = call(
        functools.partial(add_cores_kernel, p),
        [shape(p.members, p.width + p.orows, blk)] + [shape(p.seq, p.mrows, blk)] * p.fold,
        grad_x,
        keep,
        swap(send),
        *[f.reshape(p.seq, p.yrows, blk) for f in (small if p.direct else (small[0], swap(small[1])))],
        name="add_cores",
    )
    received = shuffle(message)

    for step in range(1, p.fold):
        shares[step] = lax.ppermute(shares[step], "dp", p.across_fold(step))
    message = shares[0]
    if p.fold > 1:
        message = call(
            functools.partial(add_fold_kernel, p),
            shape(p.seq, p.mrows, blk),
            *shares,
            name="add_fold",
        )
    message, received = lax.optimization_barrier((message, received))
    factor_grads = lax.all_to_all(message, "seq", 0, 0, tiled=True)

    rows = call(
        functools.partial(filter_rows_kernel, p),
        shape(p.members, p.orows, blk),
        received,
        name="filter_rows",
    )
    rows = gathered(summed_over_groups(rows), lambda a: a)
    token_grad = call(
        functools.partial(token_grad_kernel, p), shape(blk, p.channels), received, name="token_grad"
    )
    grad_filter, sum_value, sum_gate = call(
        functools.partial(finish_filter_kernel, p),
        [
            shape(blk, p.channels),
            shape(3, p.channels, dtype=F32),
            shape(3, p.channels, dtype=F32),
        ],
        *rows,
        name="finish_filter",
    )
    factor_grads, token_grad, grad_filter, sum_value, sum_gate = lax.optimization_barrier(
        (factor_grads, token_grad, grad_filter, sum_value, sum_gate)
    )
    sums = call(
        functools.partial(sum_kernel, p), shape(p.mrows, blk), factor_grads, name="sum_sources"
    )
    grad_one, grad_four, *small = call(
        functools.partial(finish_factors_kernel, p),
        [shape(2, blk, blk)] * 2
        + ([shape(2, pairs, p.kloc)] * 2 if p.direct else [shape(2, p.yrows, blk)]),
        *gathered(summed_over_groups(sums), lambda a: a),
        name="finish_factors",
    )
    if p.direct:
        small = [f.reshape(2, p.nblk, p.nblk, p.kloc).transpose(0, 3, 1, 2) for f in small]
    else:
        small = small[0].reshape(2, p.kloc, 2, p.nblk, p.nblk)
        small = [small[:, :, 0], small[:, :, 1]]
    return (
        token_grad[None],
        sum_value,
        sum_gate,
        grad_one.reshape(mix_one.shape),
        *small,
        grad_four.reshape(mix_four.shape),
        grad_filter.reshape(filter_log.shape),
    )


def solution(mesh):
    return jax.shard_map(
        shards,
        mesh=mesh,
        in_specs=(
            P("dp", "seq", None),
            P("dp", "seq", None),
            P(),
            P(),
            P(None, "seq", None, None),
            P(None, "seq", None, None),
            P(None, "seq", None, None),
            P(None, "seq", None, None),
            P("seq", None, None),
        ),
        out_specs=(
            P("dp", "seq", None),
            P(),
            P(),
            P(None, "seq", None, None),
            P(None, "seq", None, None),
            P(None, "seq", None, None),
            P(None, "seq", None, None),
            P("seq", None, None),
        ),
        check_vma=False,
    )
```

```python
import functools

import jax
import jax.numpy as jnp
from jax import lax
from jax.experimental import pallas as pl
from jax.experimental.pallas import tpu as pltpu
from jax.sharding import PartitionSpec as P

F32 = jnp.float32
BF16 = jnp.bfloat16
TILE = 16
VMEM = pl.BlockSpec(memory_space=pltpu.VMEM)
FAR = pl.BlockSpec(memory_space=pl.ANY)


class Plan:
    def __init__(self, dp, seq, tokens, mix_one, mix_two):
        self.dp, self.seq = dp, seq
        self.blk = mix_one.shape[-1]
        self.channels = tokens.shape[-1]
        assert tokens.shape[1] == self.blk and dp % 2 == 0
        self.nblk = seq
        self.near = 2 if seq % 2 == 0 else 1
        self.layers = seq // self.near
        self.layer_groups = [list(range(y, seq, self.near)) for y in range(self.near)]
        self.kloc = mix_two.shape[1]
        half_dp = dp // 2
        self.fold = max(
            f
            for f in range(1, half_dp + 1)
            if half_dp % f == 0 and self.channels % (seq * f * TILE) == 0
        )
        self.groups = half_dp // self.fold
        self.members = self.fold * seq
        self.width = self.channels // self.members
        assert self.width <= 128
        self.cols = self.fold * self.width
        self.length = self.nblk * self.blk
        self.pairs = self.nblk * self.nblk
        self.yrows = self.kloc * 2 * self.pairs // self.blk
        self.direct = self.yrows == self.kloc
        self.streamed = self.nblk * TILE > self.blk
        self.kgroups = self.blk // TILE
        self.dim = self.nblk * TILE
        unit = TILE * self.fold
        self.half = -(-(2 * self.blk + self.yrows) // unit) * unit
        self.mrows = self.half // self.fold
        self.cores_share = self.width % (2 * TILE) == 0
        self.frows = self.width // 2 if self.cores_share else self.width
        self.full = -(-(self.width + TILE) // (2 * unit)) * 2 * unit
        self.orows = self.full // (2 * self.fold)
        self.share = self.mrows + self.orows
        self.group_lists = [
            [
                ((g * self.fold + h) * 2 + core) * seq + s
                for h in range(self.fold)
                for s in range(seq)
            ]
            for g in range(self.groups)
            for core in range(2)
        ]

    def across_cores(self):
        return [(d, d ^ 1) for d in range(self.dp)]

    def across_fold(self, step, side=0):
        moves = []
        for g in range(self.groups):
            for h in range(self.fold):
                for core in range(2):
                    source = (g * self.fold + h) * 2 + core
                    target = (g * self.fold + (h + step) % self.fold) * 2 + (core ^ side)
                    moves.append((source, target))
        return moves

    def across_plane(self, step, near_step, side=0):
        return [
            (source * self.seq + s, target * self.seq + s // self.near * self.near + (s + near_step) % self.near)
            for source, target in self.across_fold(step, side)
            for s in range(self.seq)
        ]

    def plane(self):
        return [(step, near_step) for step in range(self.fold) for near_step in range(self.near)]

    def across_groups(self, step):
        block = 2 * self.fold
        return [(d, (d + step * block) % self.dp) for d in range(self.dp)]


def each(count, body, unrolled=True):
    if count <= 8 and unrolled:
        for i in range(count):
            body(i)
    else:
        lax.fori_loop(0, count, lambda i, c: (body(i), c)[1], 0)


def rows_at(start, size):
    return pl.ds(start if isinstance(start, int) else pl.multiple_of(start, TILE), size)


def dot(a, b, ca, cb):
    return lax.dot_general(a, b, (((ca,), (cb,)), ((), ())), preferred_element_type=F32)


def call(kernel, out_shape, *args, scratch=(), far=(), limit=24, name=None):
    single = not isinstance(out_shape, (list, tuple))
    return pl.pallas_call(
        kernel,
        out_shape=out_shape,
        in_specs=[FAR if i in far else VMEM for i in range(len(args))],
        out_specs=VMEM if single else [VMEM] * len(out_shape),
        scratch_shapes=list(scratch),
        compiler_params=pltpu.CompilerParams(vmem_limit_bytes=limit * 2**20),
        name=name,
    )(*args)


def shape(*dims, dtype=BF16):
    return jax.ShapeDtypeStruct(dims, dtype)


def place(p):
    at = lax.axis_index("dp")
    return (at // 2) % p.fold, at % 2


def factor_message_kernel(p, *refs):
    count = 5 if p.direct else 4
    far, out, near, rows, turned, done = refs[:count], refs[count], refs[count + 1 : -3], *refs[-3:]
    h, core = place(p)
    part_width = p.seq * p.width
    sources = [far[0].at[:, pl.ds(pl.multiple_of(h * part_width, p.blk), part_width)]]
    sources += [f.at[core] for f in far[1:]]
    copies = [pltpu.make_async_copy(f, n, done.at[i]) for i, (f, n) in enumerate(zip(sources, near))]
    for copy in copies:
        copy.start()
    filt, one, four = near[:3]
    for copy in copies[1:]:
        copy.wait()
    rows[0 : p.blk] = one[...]
    rows[p.blk : 2 * p.blk] = four[...]
    if p.direct:
        small = jnp.concatenate([near[3][...], near[4][...]], axis=0).T
    else:
        small = near[3][...]
    rows[2 * p.blk : 2 * p.blk + p.yrows] = small
    pad = p.half - 2 * p.blk - p.yrows
    if pad:
        rows[p.half - pad :] = jnp.zeros((pad, p.blk), BF16)
    mine = rows[0 : p.mrows]
    for owner in range(1, p.fold):
        mine = jnp.where(h == owner, rows[owner * p.mrows : (owner + 1) * p.mrows], mine)
    copies[0].wait()
    turned[...] = filt[...].T

    def one_layer(z):
        out[z, 0 : p.mrows] = mine
        for near in range(p.near):
            logs = turned[rows_at((z * p.near + near) * p.width, p.width)]
            if p.cores_share:
                logs = jnp.where(core == 0, logs[: p.frows], logs[p.frows :])
            out[z, p.mrows + near * p.frows : p.mrows + (near + 1) * p.frows] = logs

    each(p.layers, one_layer)


def near_message_kernel(p, got, *outs):
    y = lax.axis_index("seq") % p.near

    def one_layer(z):
        logs = [got[z, p.mrows + i * p.frows : p.mrows + (i + 1) * p.frows] for i in range(p.near)]
        for step in range(p.near):
            outs[step][z, 0 : p.mrows] = got[z, 0 : p.mrows]
            outs[step][z, p.mrows :] = pick(p, [logs[(i + step) % p.near] for i in range(p.near)], y)

    each(p.layers, one_layer)


def token_message_kernel(p, tokens, upstream, out):
    w = p.width
    token_rows = tokens[...].T
    upstream_rows = upstream[...].T
    for q in range(p.members):
        out[q, 0:w] = token_rows[q * w : (q + 1) * w]
        out[q, w : 2 * w] = upstream_rows[q * w : (q + 1) * w]


def shares_in_order(p, pieces):
    h, core = place(p)

    def share(c, owner, part):
        value = None
        for side in range(2):
            for step in range(p.fold):
                piece = part(pieces[side * p.fold + step], side, step)
                if value is None:
                    value = piece
                    continue
                here = core == (c if side == 0 else 1 - c)
                value = jnp.where(here & (h == (owner + step) % p.fold), piece, value)
        return value

    return share


def prepare_kernel(p, *refs):
    count = 2 * len(p.plane())
    pieces, (one, four, small, filt) = refs[:count], refs[count:]
    _, core = place(p)
    y = lax.axis_index("seq") % p.near

    def one_layer(z):
        for near in range(p.near):
            i = z * p.near + near

            def from_near(part):
                return pick(p, [part(pieces[(near - at) % p.near :: p.near]) for at in range(p.near)], y)

            for side in range(2):
                rows = [
                    from_near(
                        lambda own: shares_in_order(p, own)(side, owner, lambda ref, *_: ref[z, 0 : p.mrows])
                    )
                    for owner in range(p.fold)
                ]
                rows = jnp.concatenate(rows, axis=0) if p.fold > 1 else rows[0]
                one[i, side * p.blk : (side + 1) * p.blk] = rows[0 : p.blk]
                factor = rows[p.blk : 2 * p.blk]
                four[i, :, side * p.blk : (side + 1) * p.blk] = factor if side == 0 else -factor
                small[side, i] = rows[2 * p.blk : 2 * p.blk + p.yrows]
            logs = from_near(lambda own: own[0][z, p.mrows :])
            if p.cores_share:
                other = from_near(lambda own: own[p.fold][z, p.mrows :])
                logs = [jnp.where(core == 0, logs, other), jnp.where(core == 0, other, logs)]
                logs = jnp.concatenate(logs, axis=0)
            if p.fold > 1:
                logs = jnp.concatenate([logs] * p.fold, axis=0)
            filt[i] = jnp.exp(logs.T.astype(F32))

    each(p.layers, one_layer)


def iota(dims, axis):
    return lax.broadcasted_iota(jnp.int32, dims, axis)


def block_masks(p):
    d, nb, pairs = p.dim, p.nblk, p.pairs
    same = iota((d, d), 0) % TILE == iota((d, d), 1) // nb
    lane = iota((d, 2 * pairs), 1)
    block = iota((d, 2 * pairs), 0) // TILE
    keep_two = (lane < pairs) & (lane % nb == block)
    keep_three = (lane >= pairs) & ((lane - pairs) // nb == block)
    return same, keep_two, keep_three


def selectors(p, turned):
    d, nb, pairs = p.dim, p.nblk, p.pairs
    dims = (d, 2 * pairs) if turned else (2 * pairs, d)
    lane = iota(dims, 1 if turned else 0)
    block = iota(dims, 0 if turned else 1) % nb
    two = (lane < pairs) & (lane // nb == block)
    three = (lane >= pairs) & ((lane - pairs) % nb == block)
    return two.astype(BF16), three.astype(BF16)


def block_factor_kernel(p, small, two, three):
    same, keep_two, keep_three = block_masks(p)
    pick_two, pick_three = selectors(p, False)
    d = p.dim

    def one_group(g):
        parts = {}
        for part in range(2):
            entries = small[part, rows_at(g * TILE, TILE)]
            tiled = jnp.concatenate([entries] * p.nblk, axis=0)
            zero = jnp.zeros_like(tiled)
            for name, keep, pick in (("two", keep_two, pick_two), ("three", keep_three, pick_three)):
                spread = dot(jnp.where(keep, tiled, zero), pick, 1, 0)
                parts[name, part] = jnp.where(same, spread, 0.0).astype(BF16)
        two[g, :d, :d] = parts["two", 0]
        two[g, d:, d:] = parts["two", 0]
        two[g, :d, d:] = parts["two", 1]
        two[g, d:, :d] = -parts["two", 1]
        three[g, :d, :d] = parts["three", 0]
        three[g, d:, d:] = parts["three", 0]
        three[g, :d, d:] = -parts["three", 1]
        three[g, d:, :d] = parts["three", 1]

    each(p.kgroups, one_group)


def mixer_kernel(
    p, tokens_in, taps, one, four, two_far, three_far, filt,
    grad_x, keep, send, *refs,
):
    _, core = place(p)
    small_out = None if p.direct else refs[:2]
    (tok, ups, val, mix, groups_a, groups_b, second, time_a, gate, grad_v, filter_grad,
     gradients, small, groups_d, diagonal, *near) = refs if p.direct else refs[2:]

    def hand_out(i, base, values):
        mine = jnp.where(core == 0, values[0], values[1])
        other = jnp.where(core == 0, values[1], values[0])
        last = base + values[0].shape[0]
        for h in range(p.fold):
            lo, hi = max(base, h * p.mrows), min(last, (h + 1) * p.mrows)
            if lo < hi:
                keep[h, i, lo - h * p.mrows : hi - h * p.mrows] = mine[lo - base : hi - base]
                send[h, i, lo - h * p.mrows : hi - h * p.mrows] = other[lo - base : hi - base]

    def factor(far, at, g):
        if not p.streamed:
            return far[g]
        pltpu.sync_copy(far.at[g], near[at])
        return near[at][...]

    blk, nb, d, w, cols = p.blk, p.nblk, p.dim, p.width, p.cols
    edge = 8

    def taps_of(branch, offset):
        return taps[3 * branch + offset : 3 * branch + offset + 1, :]

    zero_edge = jnp.zeros((edge, cols), F32)
    for ref in (tok, gate, grad_v):
        ref[0:edge] = zero_edge
        ref[edge + p.length : 2 * edge + p.length] = zero_edge

    def load(i):
        both = [tokens_in[h * nb + i] for h in range(p.fold)]
        t = jnp.concatenate([b[0:w] for b in both], axis=0) if p.fold > 1 else both[0][0:w]
        u = jnp.concatenate([b[w:] for b in both], axis=0) if p.fold > 1 else both[0][w:]
        tok[rows_at(edge + i * blk, blk) if isinstance(i, int) else pl.ds(pl.multiple_of(edge + i * blk, 8), blk)] = t.T.astype(F32)
        ups[rows_at(i * blk, blk)] = u.T

    each(nb, load)

    def window(ref, i, offset):
        return ref[pl.ds(edge + i * blk + offset, blk)]

    def spread(ref, i, value):
        for part in range(2):
            for g in range(p.kgroups):
                row = part * blk + g * TILE
                ref[g, rows_at((part * nb + i) * TILE, TILE)] = value[row : row + TILE]

    def first_stage(i):
        before, here, after = (window(tok, i, o) for o in (-1, 0, 1))
        values = taps_of(0, 0) * before + taps_of(0, 1) * here + taps_of(0, 2) * after
        gating = taps_of(1, 0) * before + taps_of(1, 1) * here + taps_of(1, 2) * after
        values = values.astype(BF16)
        val[rows_at(i * blk, blk)] = values
        up = ups[rows_at(i * blk, blk)].astype(F32)
        mix[rows_at(i * blk, blk)] = (up * gating.astype(BF16).astype(F32)).astype(BF16)
        spread(groups_a, i, dot(one[i], values, 1, 0).astype(BF16))

    each(nb, first_stage)

    def filter_of(g):
        f = filt[rows_at(g * d, d)]
        return f

    def forward_middle(g):
        f = filter_of(g)
        f2 = jnp.concatenate([f, f], axis=0)
        sec = dot(factor(two_far, 0, g), groups_a[g], 0, 0)
        second[g] = sec
        groups_b[g] = (f2 * sec).astype(BF16)

    def unspread(g, value):
        for part in range(2):
            for i in range(nb):
                row = (part * nb + i) * TILE
                time_a[i, rows_at(part * blk + g * TILE, TILE)] = value[row : row + TILE]

    def forward_last(g):
        unspread(g, dot(factor(three_far, 1, g), groups_b[g], 1, 0).astype(BF16))

    def each_group(*stages):
        if p.streamed:
            each(p.kgroups, lambda g: [stage(g) for stage in stages], unrolled=False)
        else:
            for stage in stages:
                each(p.kgroups, stage)

    each_group(forward_middle, forward_last)

    def last_factor(n):
        third = time_a[n]
        last = four[n]
        mixed = dot(last, third, 1, 0)
        at = rows_at(n * blk, blk)
        gate[pl.ds(edge + n * blk, blk)] = ups[at].astype(F32) * mixed
        grads = mix[at]
        back = dot(last, grads, 0, 0).astype(BF16)
        for part in range(2):
            for g in range(p.kgroups):
                row = part * blk + g * TILE
                groups_b[p.kgroups + g, rows_at((part * nb + n) * TILE, TILE)] = back[row : row + TILE]
        products = dot(grads, third, 1, 1)
        hand_out(n, blk, (products[:, 0:blk].astype(BF16), (-products[:, blk:]).astype(BF16)))

    each(nb, last_factor)

    same, keep_two, keep_three = block_masks(p)
    pick_two, pick_three = selectors(p, True)

    def backward_middle(g):
        f = filter_of(g)
        f2 = jnp.concatenate([f, f], axis=0)
        weighted_grad = dot(factor(three_far, 1, g), groups_b[p.kgroups + g], 0, 0)
        term = weighted_grad * second[g]
        filter_grad[rows_at(g * d, d)] = f * (term[:d] + term[d:])
        groups_d[g] = (f2 * weighted_grad).astype(BF16)

    def backward_last(g):
        unspread(g, dot(factor(two_far, 0, g), groups_d[g], 1, 0).astype(BF16))

    def group_products(g):
        at = rows_at(0 if p.streamed else g * d, d)
        three = dot(groups_b[p.kgroups + g], groups_b[g], 1, 1)
        two = dot(groups_a[g], groups_d[g], 1, 1)
        for kind, real, imag in (
            (0, two[:d, :d] + two[d:, d:], two[:d, d:] - two[d:, :d]),
            (1, three[:d, :d] + three[d:, d:], three[d:, :d] - three[:d, d:]),
        ):
            diagonal[kind, 0, at] = jnp.where(same, real, 0.0).astype(BF16)
            diagonal[kind, 1, at] = jnp.where(same, imag, 0.0).astype(BF16)

    def fold_products(g):
        at = rows_at(0 if p.streamed else g * d, d)
        for part in range(2):
            two = jnp.where(keep_two, dot(diagonal[0, part, at], pick_two, 1, 0), 0.0)
            three = jnp.where(keep_three, dot(diagonal[1, part, at], pick_three, 1, 0), 0.0)
            total = jnp.sum((two + three).reshape(nb, TILE, 2 * p.pairs), axis=0)
            small[part, rows_at(g * TILE, TILE)] = total.astype(BF16)
        if p.direct:
            at = rows_at(g * TILE, TILE)
            hand_out(g, 2 * blk, (small[0, at], small[1, at]))

    each_group(backward_middle, backward_last, group_products, fold_products)

    def first_factor(i):
        first_grad = time_a[i]
        grad_v[pl.ds(edge + i * blk, blk)] = dot(one[i], first_grad, 0, 0)
        products = dot(first_grad, val[rows_at(i * blk, blk)], 1, 1).astype(BF16)
        hand_out(i, 0, (products[:blk], products[blk:]))
        used = 2 * blk + (p.yrows if p.direct else 0)
        if p.half > used:
            rest = jnp.zeros((p.half - used, blk), BF16)
            hand_out(i, used, (rest, rest))

    each(nb, first_factor)

    sums = [jnp.zeros((8, cols), F32) for _ in range(6)]

    def last_stage(i, sums):
        total = jnp.zeros((blk, cols), F32)
        sums = list(sums)
        for branch, ref in ((0, grad_v), (1, gate)):
            before, here, after = (window(ref, i, o) for o in (-1, 0, 1))
            total += taps_of(branch, 0) * after + taps_of(branch, 1) * here + taps_of(branch, 2) * before
            for offset in range(3):
                product = here * window(tok, i, offset - 1)
                sums[3 * branch + offset] += jnp.sum(product.reshape(blk // 8, 8, cols), axis=0)
        grad_x[i] = total.astype(BF16)
        terms = filter_grad[rows_at(i * blk, blk)].T
        term = terms[0:w]
        for h in range(1, p.fold):
            term = term + terms[h * w : (h + 1) * w]
        gradients[i] = term.astype(BF16)
        return tuple(sums)

    if nb <= 8:
        for i in range(nb):
            sums = last_stage(i, sums)
    else:
        sums = lax.fori_loop(0, nb, last_stage, tuple(sums))

    conv = jnp.concatenate([jnp.sum(s, axis=0, keepdims=True) for s in sums] + [jnp.zeros((2, cols), F32)], axis=0)
    term = conv[:, 0:w]
    for h in range(1, p.fold):
        term = term + conv[:, h * w : (h + 1) * w]
    if w < blk:
        term = jnp.concatenate([term, jnp.zeros((8, blk - w), F32)], axis=1)
    high = term.astype(BF16).astype(F32)
    conv_rows = jnp.concatenate([high, term - high], axis=0).astype(BF16)

    ends = [conv_rows]
    if p.full > w + TILE:
        ends.append(jnp.zeros((p.full - w - TILE, blk), BF16))

    def last_rows(i):
        rows = jnp.concatenate([gradients[i], *ends], axis=0)
        middle = p.full // 2
        mine = jnp.where(core == 0, rows[:middle], rows[middle:])
        other = jnp.where(core == 0, rows[middle:], rows[:middle])
        for h in range(p.fold):
            at = slice(h * p.orows, (h + 1) * p.orows)
            keep[h, i, p.mrows :] = mine[at]
            send[h, i, p.mrows :] = other[at]

    each(nb, last_rows)
    if not p.direct:
        small_out[0][...] = jnp.where(core == 0, small[0], small[1])
        small_out[1][...] = jnp.where(core == 0, small[1], small[0])


def token_grad_message_kernel(p, grads, out):
    def one_target(i):
        turned = grads[i].T
        for h in range(p.fold):
            out[h * p.nblk + i] = turned[h * p.width : (h + 1) * p.width]

    each(p.nblk, one_target)


def pick(p, values, wanted):
    value = values[0]
    for i in range(1, len(values)):
        value = jnp.where(wanted == i, values[i], value)
    return value


def add_cores_kernel(p, grad_x, keep, got, *refs):
    count = 0 if p.direct else 2
    out, shares = refs[count], refs[count + 1 :]
    h, _ = place(p)
    y = lax.axis_index("seq") % p.near

    def one_layer(z):
        rows = {}
        for near in range(p.near):
            s = z * p.near + near
            for owner in range(p.fold):
                q = owner * p.seq + s
                total = (keep[owner, s].astype(F32) + got[owner, s].astype(F32)).astype(BF16)
                out[q, 0 : p.width] = grad_x[q]
                out[q, p.width :] = total[p.mrows :]
                total = total[: p.mrows]
                first, last = 2 * p.blk - owner * p.mrows, 2 * p.blk + p.yrows - owner * p.mrows
                lo, hi = max(first, 0), min(last, p.mrows)
                if not p.direct and lo < hi:
                    extra = (refs[0][s].astype(F32) + refs[1][s].astype(F32)).astype(BF16)
                    parts = [total[:lo], extra[lo - first : hi - first], total[hi:]]
                    total = jnp.concatenate([part for part in parts if part.shape[0]], axis=0)
                rows[owner, near] = total
        for share, (step, near_step) in zip(shares, p.plane()):
            by_near = [
                pick(p, [rows[(i + step) % p.fold, (near + near_step) % p.near] for i in range(p.fold)], h)
                for near in range(p.near)
            ]
            share[z] = pick(p, by_near, y)

    each(p.layers, one_layer)


def add_fold_kernel(p, *refs):
    terms, out = refs[:-1], refs[-1]

    def one_layer(z):
        total = terms[0][z].astype(F32)
        for term in terms[1:]:
            total += term[z].astype(F32)
        out[z] = total.astype(BF16)

    each(p.layers, one_layer)


def sum_kernel(p, got, out):
    total = got[0].astype(F32)
    for q in range(1, p.layers):
        total += got[q].astype(F32)
    out[...] = total.astype(BF16)


def filter_rows_kernel(p, got, out):
    for q in range(p.members):
        out[q] = got[q, p.width :]


def token_grad_kernel(p, got, out):
    rows = jnp.concatenate([got[q, 0 : p.width] for q in range(p.members)], axis=0)
    out[...] = rows.T


def finish_factors_kernel(p, *refs):
    pieces, (one, four, *small) = refs[: 2 * p.fold], refs[2 * p.fold :]
    share = shares_in_order(p, pieces)
    for part in range(2):
        rows = [share(part, owner, lambda ref, *_: ref[...]) for owner in range(p.fold)]
        rows = jnp.concatenate(rows, axis=0) if p.fold > 1 else rows[0]
        one[part] = rows[0 : p.blk]
        four[part] = rows[p.blk : 2 * p.blk]
        entries = rows[2 * p.blk : 2 * p.blk + p.yrows]
        if p.direct:
            entries = entries.T
            small[0][part] = entries[: p.pairs]
            small[1][part] = entries[p.pairs :]
        else:
            small[0][part] = entries


def finish_filter_kernel(p, *refs):
    pieces, (filt, conv_value, conv_gate) = refs[: 2 * p.fold], refs[2 * p.fold :]
    share = shares_in_order(p, pieces)
    turned, columns = [], []
    for q in range(p.members):
        rows = [
            share(c, owner, lambda ref, *_: ref[q]) for c in range(2) for owner in range(p.fold)
        ]
        rows = jnp.concatenate(rows, axis=0)
        turned.append(rows[0 : p.width])
        both = rows[p.width : p.width + TILE].astype(F32)
        columns.append((both[:8] + both[8:]).T[: p.width])
    filt[...] = jnp.concatenate(turned, axis=0).T
    sums = jnp.concatenate(columns, axis=0).T
    conv_value[...] = sums[0:3]
    conv_gate[...] = sums[3:6]


def shards(
    tokens, upstream, conv_value, conv_gate, mix_one, mix_two, mix_three, mix_four, filter_log
):
    p = Plan(lax.axis_size("dp"), lax.axis_size("seq"), tokens, mix_one, mix_two)
    dp_at, seq_at = lax.axis_index("dp"), lax.axis_index("seq")
    h_at = (dp_at // 2) % p.fold
    blk, pairs = p.blk, p.pairs

    def shuffle(array):
        return lax.all_to_all(
            array, ("dp", "seq"), 0, 0, tiled=True, axis_index_groups=p.group_lists
        )

    def across_layers(array):
        return lax.all_to_all(
            array, "seq", 0, 0, tiled=True, axis_index_groups=p.layer_groups
        )

    def swap(array):
        return lax.ppermute(array, "dp", p.across_cores())

    def gathered(array, rows):
        pieces = [array]
        for step in range(1, p.fold):
            pieces.append(lax.ppermute(rows(array), "dp", p.across_fold(step)))
        return pieces + [swap(piece) for piece in pieces]

    def gathered_at_once(array):
        return [
            lax.ppermute(array, "dp", p.across_fold(step, side)) if step or side else array
            for side in range(2)
            for step in range(p.fold)
        ]

    if p.direct:
        small = [f.transpose(0, 2, 3, 1).reshape(2, pairs, p.kloc) for f in (mix_two, mix_three)]
    else:
        small = [f.reshape(2, p.kloc, pairs) for f in (mix_two, mix_three)]
        small = [jnp.concatenate(small, axis=2).reshape(2, p.yrows, blk)]
    far = [
        filter_log.reshape(blk, p.channels),
        mix_one.reshape(2, blk, blk),
        mix_four.reshape(2, blk, blk),
        *small,
    ]
    message = call(
        functools.partial(factor_message_kernel, p),
        shape(p.layers, p.mrows + p.near * p.frows, blk),
        *far,
        scratch=[pltpu.VMEM((blk, p.channels // p.fold), BF16)]
        + [pltpu.VMEM(f.shape[1:], BF16) for f in far[1:]]
        + [
            pltpu.VMEM((p.half, blk), BF16),
            pltpu.VMEM((p.channels // p.fold, blk), BF16),
            pltpu.SemaphoreType.DMA((len(far),)),
        ],
        far=range(len(far)),
        limit=60,
        name="factor_message",
    )
    factors = across_layers(message)
    near_messages = [factors]
    if p.near > 1:
        near_messages = call(
            functools.partial(near_message_kernel, p),
            [shape(p.layers, p.mrows + p.frows, blk)] * p.near,
            factors,
            name="near_message",
        )
    pieces = [near_messages[0]]
    for step, near_step in p.plane()[1:]:
        piece = near_messages[near_step] if step == 0 else factors[:, : p.mrows]
        pieces.append(lax.ppermute(piece, ("dp", "seq"), p.across_plane(step, near_step)))
    pieces += [swap(piece) for piece in pieces]

    message = call(
        functools.partial(token_message_kernel, p),
        shape(p.members, 2 * p.width, blk),
        tokens[0],
        upstream[0],
        name="token_message",
    )
    received = shuffle(message)
    pieces, received = lax.optimization_barrier((pieces, received))
    one, four, small, filt = call(
        functools.partial(prepare_kernel, p),
        [
            shape(p.nblk, 2 * blk, blk),
            shape(p.nblk, blk, 2 * blk),
            shape(2, p.nblk, p.yrows, blk),
            shape(p.nblk, blk, p.cols, dtype=F32),
        ],
        *pieces,
        name="prepare",
    )
    two, three = call(
        functools.partial(block_factor_kernel, p),
        [shape(p.kgroups, 2 * p.dim, 2 * p.dim)] * 2,
        small.reshape(2, blk, 2 * pairs),
        limit=48 if p.streamed else 24,
        name="block_factors",
    )

    start = (h_at * p.seq + seq_at) * p.width
    taps = jnp.concatenate([conv_value, conv_gate], axis=0)
    taps = lax.dynamic_slice_in_dim(taps, start, p.width, 1)
    taps = jnp.concatenate([taps] * p.fold, axis=1)

    padded = p.length + 16
    grad_x, keep, send, *small = call(
        functools.partial(mixer_kernel, p),
        [
            shape(p.nblk, blk, p.cols),
            shape(p.fold, p.seq, p.share, blk),
            shape(p.fold, p.seq, p.share, blk),
        ]
        + [shape(blk, 2 * pairs)] * (0 if p.direct else 2),
        received,
        taps,
        one,
        four,
        two,
        three,
        filt.reshape(p.length, p.cols),
        scratch=[
            pltpu.VMEM((padded, p.cols), F32),
            pltpu.VMEM((p.length, p.cols), BF16),
            pltpu.VMEM((p.length, p.cols), BF16),
            pltpu.VMEM((p.length, p.cols), BF16),
            pltpu.VMEM((p.kgroups, 2 * p.dim, p.cols), BF16),
            pltpu.VMEM((2 * p.kgroups, 2 * p.dim, p.cols), BF16),
            pltpu.VMEM((p.kgroups, 2 * p.dim, p.cols), F32),
            pltpu.VMEM((p.nblk, 2 * blk, p.cols), BF16),
            pltpu.VMEM((padded, p.cols), F32),
            pltpu.VMEM((padded, p.cols), F32),
            pltpu.VMEM((p.length, p.cols), F32),
            pltpu.VMEM((p.nblk, p.width, blk), BF16),
            pltpu.VMEM((2, blk, 2 * pairs), BF16),
            pltpu.VMEM((p.kgroups, 2 * p.dim, p.cols), BF16),
            pltpu.VMEM((2, 2, (1 if p.streamed else p.kgroups) * p.dim, p.dim), BF16),
        ]
        + [pltpu.VMEM((2 * p.dim, 2 * p.dim), BF16)] * (2 if p.streamed else 0),
        far=(4, 5) if p.streamed else (),
        limit=60 if p.streamed else 24,
        name="mixer",
    )

    def summed_over_groups(array):
        if p.groups == 1:
            return array
        total = array.astype(F32)
        for step in range(1, p.groups):
            total += lax.ppermute(array, "dp", p.across_groups(step)).astype(F32)
        return total.astype(BF16)

    grad_x = call(
        functools.partial(token_grad_message_kernel, p),
        shape(p.members, p.width, blk),
        grad_x,
        name="token_grad_message",
    )
    message, *shares = call(
        functools.partial(add_cores_kernel, p),
        [shape(p.members, p.width + p.orows, blk)]
        + [shape(p.layers, p.mrows, blk)] * len(p.plane()),
        grad_x,
        keep,
        swap(send),
        *[f.reshape(p.seq, p.yrows, blk) for f in (small if p.direct else (small[0], swap(small[1])))],
        name="add_cores",
    )
    received = shuffle(message)

    message = shares[0]
    if len(shares) > 1:
        message = call(
            functools.partial(add_fold_kernel, p),
            shape(p.layers, p.mrows, blk),
            message,
            *[
                lax.ppermute(share, ("dp", "seq"), p.across_plane(*steps))
                for share, steps in zip(shares[1:], p.plane()[1:])
            ],
            name="add_fold",
        )
    message, received = lax.optimization_barrier((message, received))
    factor_grads = across_layers(message)

    rows = call(
        functools.partial(filter_rows_kernel, p),
        shape(p.members, p.orows, blk),
        received,
        name="filter_rows",
    )
    rows = gathered(summed_over_groups(rows), lambda a: a)
    token_grad = call(
        functools.partial(token_grad_kernel, p), shape(blk, p.channels), received, name="token_grad"
    )
    grad_filter, sum_value, sum_gate = call(
        functools.partial(finish_filter_kernel, p),
        [
            shape(blk, p.channels),
            shape(3, p.channels, dtype=F32),
            shape(3, p.channels, dtype=F32),
        ],
        *rows,
        name="finish_filter",
    )
    factor_grads, token_grad, grad_filter, sum_value, sum_gate = lax.optimization_barrier(
        (factor_grads, token_grad, grad_filter, sum_value, sum_gate)
    )
    sums = call(
        functools.partial(sum_kernel, p), shape(p.mrows, blk), factor_grads, name="sum_sources"
    )
    grad_one, grad_four, *small = call(
        functools.partial(finish_factors_kernel, p),
        [shape(2, blk, blk)] * 2
        + ([shape(2, pairs, p.kloc)] * 2 if p.direct else [shape(2, p.yrows, blk)]),
        *gathered_at_once(summed_over_groups(sums)),
        name="finish_factors",
    )
    if p.direct:
        small = [f.reshape(2, p.nblk, p.nblk, p.kloc).transpose(0, 3, 1, 2) for f in small]
    else:
        small = small[0].reshape(2, p.kloc, 2, p.nblk, p.nblk)
        small = [small[:, :, 0], small[:, :, 1]]
    return (
        token_grad[None],
        sum_value,
        sum_gate,
        grad_one.reshape(mix_one.shape),
        *small,
        grad_four.reshape(mix_four.shape),
        grad_filter.reshape(filter_log.shape),
    )


def solution(mesh):
    return jax.shard_map(
        shards,
        mesh=mesh,
        in_specs=(
            P("dp", "seq", None),
            P("dp", "seq", None),
            P(),
            P(),
            P(None, "seq", None, None),
            P(None, "seq", None, None),
            P(None, "seq", None, None),
            P(None, "seq", None, None),
            P("seq", None, None),
        ),
        out_specs=(
            P("dp", "seq", None),
            P(),
            P(),
            P(None, "seq", None, None),
            P(None, "seq", None, None),
            P(None, "seq", None, None),
            P(None, "seq", None, None),
            P("seq", None, None),
        ),
        check_vma=False,
    )
```

```python
import functools

import jax
import jax.numpy as jnp
from jax import lax
from jax.experimental import pallas as pl
from jax.experimental.pallas import tpu as pltpu
from jax.sharding import PartitionSpec as P

F32 = jnp.float32
BF16 = jnp.bfloat16
TILE = 16
VMEM = pl.BlockSpec(memory_space=pltpu.VMEM)
FAR = pl.BlockSpec(memory_space=pl.ANY)


class Plan:
    def __init__(self, dp, seq, tokens, mix_one, mix_two):
        self.dp, self.seq = dp, seq
        self.blk = mix_one.shape[-1]
        self.channels = tokens.shape[-1]
        assert tokens.shape[1] == self.blk and dp % 2 == 0
        self.nblk = seq
        self.near = 2 if seq % 2 == 0 else 1
        self.layers = seq // self.near
        self.layer_groups = [list(range(y, seq, self.near)) for y in range(self.near)]
        self.kloc = mix_two.shape[1]
        half_dp = dp // 2
        self.fold = max(
            f
            for f in range(1, half_dp + 1)
            if half_dp % f == 0 and self.channels % (seq * f * TILE) == 0
        )
        self.groups = half_dp // self.fold
        self.members = self.fold * seq
        self.width = self.channels // self.members
        assert self.width <= 128
        self.cols = self.fold * self.width
        self.length = self.nblk * self.blk
        self.pairs = self.nblk * self.nblk
        self.yrows = self.kloc * 2 * self.pairs // self.blk
        self.direct = self.yrows == self.kloc
        self.streamed = self.nblk * TILE > self.blk
        self.kgroups = self.blk // TILE
        self.dim = self.nblk * TILE
        unit = TILE * self.fold
        self.half = -(-(2 * self.blk + self.yrows) // unit) * unit
        self.mrows = self.half // self.fold
        self.cores_share = self.width % (2 * TILE) == 0
        self.frows = self.width // 2 if self.cores_share else self.width
        self.full = -(-(self.width + TILE) // (2 * unit)) * 2 * unit
        self.orows = self.full // (2 * self.fold)
        self.share = self.mrows + self.orows
        self.group_lists = [
            [
                ((g * self.fold + h) * 2 + core) * seq + s
                for h in range(self.fold)
                for s in range(seq)
            ]
            for g in range(self.groups)
            for core in range(2)
        ]

    def across_cores(self):
        return [(d, d ^ 1) for d in range(self.dp)]

    def across_fold(self, step, side=0):
        moves = []
        for g in range(self.groups):
            for h in range(self.fold):
                for core in range(2):
                    source = (g * self.fold + h) * 2 + core
                    target = (g * self.fold + (h + step) % self.fold) * 2 + (core ^ side)
                    moves.append((source, target))
        return moves

    def layer_partner(self, z, step):
        if self.layers & (self.layers - 1) == 0:
            return z ^ step
        return (step + self.layers - z) % self.layers

    def across_plane(self, step, near_step, side=0):
        return [
            (source * self.seq + s, target * self.seq + s // self.near * self.near + (s + near_step) % self.near)
            for source, target in self.across_fold(step, side)
            for s in range(self.seq)
        ]

    def plane(self):
        return [(step, near_step) for step in range(self.fold) for near_step in range(self.near)]

    def across_groups(self, step):
        block = 2 * self.fold
        return [(d, (d + step * block) % self.dp) for d in range(self.dp)]


def each(count, body, unrolled=True):
    if count <= 8 and unrolled:
        for i in range(count):
            body(i)
    else:
        lax.fori_loop(0, count, lambda i, c: (body(i), c)[1], 0)


def rows_at(start, size):
    return pl.ds(start if isinstance(start, int) else pl.multiple_of(start, TILE), size)


def dot(a, b, ca, cb):
    return lax.dot_general(a, b, (((ca,), (cb,)), ((), ())), preferred_element_type=F32)


def call(kernel, out_shape, *args, scratch=(), far=(), limit=24, name=None):
    single = not isinstance(out_shape, (list, tuple))
    return pl.pallas_call(
        kernel,
        out_shape=out_shape,
        in_specs=[FAR if i in far else VMEM for i in range(len(args))],
        out_specs=VMEM if single else [VMEM] * len(out_shape),
        scratch_shapes=list(scratch),
        compiler_params=pltpu.CompilerParams(vmem_limit_bytes=limit * 2**20),
        name=name,
    )(*args)


def shape(*dims, dtype=BF16):
    return jax.ShapeDtypeStruct(dims, dtype)


def place(p):
    at = lax.axis_index("dp")
    return (at // 2) % p.fold, at % 2


def factor_message_kernel(p, *refs):
    count = 5 if p.direct else 4
    far, outs, refs = refs[:count], refs[count : count + p.layers], refs[count + p.layers :]
    near, rows, turned, done = refs[:-3], *refs[-3:]
    h, core = place(p)
    part_width = p.seq * p.width
    sources = [far[0].at[:, pl.ds(pl.multiple_of(h * part_width, p.blk), part_width)]]
    sources += [f.at[core] for f in far[1:]]
    copies = [pltpu.make_async_copy(f, n, done.at[i]) for i, (f, n) in enumerate(zip(sources, near))]
    for copy in copies:
        copy.start()
    filt, one, four = near[:3]
    for copy in copies[1:]:
        copy.wait()
    rows[0 : p.blk] = one[...]
    rows[p.blk : 2 * p.blk] = four[...]
    if p.direct:
        small = jnp.concatenate([near[3][...], near[4][...]], axis=0).T
    else:
        small = near[3][...]
    rows[2 * p.blk : 2 * p.blk + p.yrows] = small
    pad = p.half - 2 * p.blk - p.yrows
    if pad:
        rows[p.half - pad :] = jnp.zeros((pad, p.blk), BF16)
    mine = rows[0 : p.mrows]
    for owner in range(1, p.fold):
        mine = jnp.where(h == owner, rows[owner * p.mrows : (owner + 1) * p.mrows], mine)
    copies[0].wait()
    turned[...] = filt[...].T

    z = lax.axis_index("seq") // p.near
    for near in range(p.near):
        logs = []
        for target in range(p.layers):
            at = (target * p.near + near) * p.width
            rows_here = turned[at : at + p.width]
            if p.cores_share:
                rows_here = jnp.where(core == 0, rows_here[: p.frows], rows_here[p.frows :])
            logs.append(rows_here)
        for step in range(p.layers):
            chosen = pick(p, [logs[p.layer_partner(at, step)] for at in range(p.layers)], z)
            outs[step][p.mrows + near * p.frows : p.mrows + (near + 1) * p.frows] = chosen
    for step in range(p.layers):
        outs[step][0 : p.mrows] = mine


def near_message_kernel(p, *refs):
    got, outs = refs[: p.layers], refs[p.layers :]
    y = lax.axis_index("seq") % p.near
    for z in range(p.layers):
        logs = [got[z][p.mrows + i * p.frows : p.mrows + (i + 1) * p.frows] for i in range(p.near)]
        for step in range(p.near):
            outs[step][z, 0 : p.mrows] = got[z][0 : p.mrows]
            outs[step][z, p.mrows :] = pick(p, [logs[(i + step) % p.near] for i in range(p.near)], y)


def token_message_kernel(p, tokens, upstream, out):
    w = p.width
    token_rows = tokens[...].T
    upstream_rows = upstream[...].T
    for q in range(p.members):
        out[q, 0:w] = token_rows[q * w : (q + 1) * w]
        out[q, w : 2 * w] = upstream_rows[q * w : (q + 1) * w]


def shares_in_order(p, pieces):
    h, core = place(p)

    def share(c, owner, part):
        value = None
        for side in range(2):
            for step in range(p.fold):
                piece = part(pieces[side * p.fold + step], side, step)
                if value is None:
                    value = piece
                    continue
                here = core == (c if side == 0 else 1 - c)
                value = jnp.where(here & (h == (owner + step) % p.fold), piece, value)
        return value

    return share


def prepare_kernel(p, *refs):
    count = 2 * len(p.plane())
    pieces, (one, four, small, filt) = refs[:count], refs[count:]
    h, core = place(p)
    y = lax.axis_index("seq") % p.near

    def from_near(z, near, side, step, rows):
        first = (side * p.fold + step) * p.near
        return pick(p, [pieces[first + (near - at) % p.near][z, rows] for at in range(p.near)], y)

    def half_rows(z, near):
        sides = []
        for side in range(2):
            steps = [from_near(z, near, side, step, slice(0, p.mrows)) for step in range(p.fold)]
            shares = [
                pick(p, [steps[(at - owner) % p.fold] for at in range(p.fold)], h)
                for owner in range(p.fold)
            ]
            sides.append(jnp.concatenate(shares, axis=0) if p.fold > 1 else shares[0])
        return [jnp.where(core == c, sides[0], sides[1]) for c in range(2)]

    def one_layer(z):
        for near in range(p.near):
            i = p.layer_partner(lax.axis_index("seq") // p.near, z) * p.near + near
            for side, rows in enumerate(half_rows(z, near)):
                one[i, side * p.blk : (side + 1) * p.blk] = rows[0 : p.blk]
                factor = rows[p.blk : 2 * p.blk]
                four[i, :, side * p.blk : (side + 1) * p.blk] = factor if side == 0 else -factor
                small[side, i] = rows[2 * p.blk : 2 * p.blk + p.yrows]
            logs = from_near(z, near, 0, 0, slice(p.mrows, p.mrows + p.frows))
            if p.cores_share:
                other = from_near(z, near, 1, 0, slice(p.mrows, p.mrows + p.frows))
                logs = [jnp.where(core == 0, logs, other), jnp.where(core == 0, other, logs)]
                logs = jnp.concatenate(logs, axis=0)
            if p.fold > 1:
                logs = jnp.concatenate([logs] * p.fold, axis=0)
            filt[i] = jnp.exp(logs.T.astype(F32))

    each(p.layers, one_layer)


def iota(dims, axis):
    return lax.broadcasted_iota(jnp.int32, dims, axis)


def block_masks(p):
    d, nb, pairs = p.dim, p.nblk, p.pairs
    same = iota((d, d), 0) % TILE == iota((d, d), 1) // nb
    lane = iota((d, 2 * pairs), 1)
    block = iota((d, 2 * pairs), 0) // TILE
    keep_two = (lane < pairs) & (lane % nb == block)
    keep_three = (lane >= pairs) & ((lane - pairs) // nb == block)
    return same, keep_two, keep_three


def selectors(p, turned):
    d, nb, pairs = p.dim, p.nblk, p.pairs
    dims = (d, 2 * pairs) if turned else (2 * pairs, d)
    lane = iota(dims, 1 if turned else 0)
    block = iota(dims, 0 if turned else 1) % nb
    two = (lane < pairs) & (lane // nb == block)
    three = (lane >= pairs) & ((lane - pairs) % nb == block)
    return two.astype(BF16), three.astype(BF16)


def block_factor_kernel(p, small, two, three):
    same, keep_two, keep_three = block_masks(p)
    pick_two, pick_three = selectors(p, False)
    d = p.dim

    def one_group(g):
        parts = {}
        for part in range(2):
            entries = small[part, rows_at(g * TILE, TILE)]
            tiled = jnp.concatenate([entries] * p.nblk, axis=0)
            zero = jnp.zeros_like(tiled)
            for name, keep, pick in (("two", keep_two, pick_two), ("three", keep_three, pick_three)):
                spread = dot(jnp.where(keep, tiled, zero), pick, 1, 0)
                parts[name, part] = jnp.where(same, spread, 0.0).astype(BF16)
        two[g, :d, :d] = parts["two", 0]
        two[g, d:, d:] = parts["two", 0]
        two[g, :d, d:] = parts["two", 1]
        two[g, d:, :d] = -parts["two", 1]
        three[g, :d, :d] = parts["three", 0]
        three[g, d:, d:] = parts["three", 0]
        three[g, :d, d:] = -parts["three", 1]
        three[g, d:, :d] = parts["three", 1]

    each(p.kgroups, one_group)


def mixer_kernel(
    p, tokens_in, taps, one, four, two_far, three_far, filt,
    grad_x, keep, send, *refs,
):
    _, core = place(p)
    small_out = None if p.direct else refs[:2]
    (tok, ups, val, mix, groups_a, groups_b, second, time_a, gate, grad_v, filter_grad,
     gradients, small, groups_d, diagonal, *near) = refs if p.direct else refs[2:]

    def hand_out(i, base, values):
        mine = jnp.where(core == 0, values[0], values[1])
        other = jnp.where(core == 0, values[1], values[0])
        last = base + values[0].shape[0]
        for h in range(p.fold):
            lo, hi = max(base, h * p.mrows), min(last, (h + 1) * p.mrows)
            if lo < hi:
                keep[h, i, lo - h * p.mrows : hi - h * p.mrows] = mine[lo - base : hi - base]
                send[h, i, lo - h * p.mrows : hi - h * p.mrows] = other[lo - base : hi - base]

    def factor(far, at, g):
        if not p.streamed:
            return far[g]
        pltpu.sync_copy(far.at[g], near[at])
        return near[at][...]

    blk, nb, d, w, cols = p.blk, p.nblk, p.dim, p.width, p.cols
    edge = 8

    def taps_of(branch, offset):
        return taps[3 * branch + offset : 3 * branch + offset + 1, :]

    zero_edge = jnp.zeros((edge, cols), F32)
    for ref in (tok, gate, grad_v):
        ref[0:edge] = zero_edge
        ref[edge + p.length : 2 * edge + p.length] = zero_edge

    def load(i):
        both = [tokens_in[h * nb + i] for h in range(p.fold)]
        t = jnp.concatenate([b[0:w] for b in both], axis=0) if p.fold > 1 else both[0][0:w]
        u = jnp.concatenate([b[w:] for b in both], axis=0) if p.fold > 1 else both[0][w:]
        tok[rows_at(edge + i * blk, blk) if isinstance(i, int) else pl.ds(pl.multiple_of(edge + i * blk, 8), blk)] = t.T.astype(F32)
        ups[rows_at(i * blk, blk)] = u.T

    each(nb, load)

    def window(ref, i, offset):
        return ref[pl.ds(edge + i * blk + offset, blk)]

    def spread(ref, i, value):
        for part in range(2):
            for g in range(p.kgroups):
                row = part * blk + g * TILE
                ref[g, rows_at((part * nb + i) * TILE, TILE)] = value[row : row + TILE]

    def first_stage(i):
        before, here, after = (window(tok, i, o) for o in (-1, 0, 1))
        values = taps_of(0, 0) * before + taps_of(0, 1) * here + taps_of(0, 2) * after
        gating = taps_of(1, 0) * before + taps_of(1, 1) * here + taps_of(1, 2) * after
        values = values.astype(BF16)
        val[rows_at(i * blk, blk)] = values
        up = ups[rows_at(i * blk, blk)].astype(F32)
        mix[rows_at(i * blk, blk)] = (up * gating.astype(BF16).astype(F32)).astype(BF16)
        spread(groups_a, i, dot(one[i], values, 1, 0).astype(BF16))

    each(nb, first_stage)

    def filter_of(g):
        f = filt[rows_at(g * d, d)]
        return f

    def forward_middle(g):
        f = filter_of(g)
        f2 = jnp.concatenate([f, f], axis=0)
        sec = dot(factor(two_far, 0, g), groups_a[g], 0, 0)
        second[g] = sec
        groups_b[g] = (f2 * sec).astype(BF16)

    def unspread(g, value):
        for part in range(2):
            for i in range(nb):
                row = (part * nb + i) * TILE
                time_a[i, rows_at(part * blk + g * TILE, TILE)] = value[row : row + TILE]

    def forward_last(g):
        unspread(g, dot(factor(three_far, 1, g), groups_b[g], 1, 0).astype(BF16))

    def each_group(*stages):
        if p.streamed:
            each(p.kgroups, lambda g: [stage(g) for stage in stages], unrolled=False)
        else:
            for stage in stages:
                each(p.kgroups, stage)

    each_group(forward_middle, forward_last)

    def last_factor(n):
        third = time_a[n]
        last = four[n]
        mixed = dot(last, third, 1, 0)
        at = rows_at(n * blk, blk)
        gate[pl.ds(edge + n * blk, blk)] = ups[at].astype(F32) * mixed
        grads = mix[at]
        back = dot(last, grads, 0, 0).astype(BF16)
        for part in range(2):
            for g in range(p.kgroups):
                row = part * blk + g * TILE
                groups_b[p.kgroups + g, rows_at((part * nb + n) * TILE, TILE)] = back[row : row + TILE]
        products = dot(grads, third, 1, 1)
        hand_out(n, blk, (products[:, 0:blk].astype(BF16), (-products[:, blk:]).astype(BF16)))

    each(nb, last_factor)

    same, keep_two, keep_three = block_masks(p)
    pick_two, pick_three = selectors(p, True)

    def backward_middle(g):
        f = filter_of(g)
        f2 = jnp.concatenate([f, f], axis=0)
        weighted_grad = dot(factor(three_far, 1, g), groups_b[p.kgroups + g], 0, 0)
        term = weighted_grad * second[g]
        filter_grad[rows_at(g * d, d)] = f * (term[:d] + term[d:])
        groups_d[g] = (f2 * weighted_grad).astype(BF16)

    def backward_last(g):
        unspread(g, dot(factor(two_far, 0, g), groups_d[g], 1, 0).astype(BF16))

    def group_products(g):
        at = rows_at(0 if p.streamed else g * d, d)
        three = dot(groups_b[p.kgroups + g], groups_b[g], 1, 1)
        two = dot(groups_a[g], groups_d[g], 1, 1)
        for kind, real, imag in (
            (0, two[:d, :d] + two[d:, d:], two[:d, d:] - two[d:, :d]),
            (1, three[:d, :d] + three[d:, d:], three[d:, :d] - three[:d, d:]),
        ):
            diagonal[kind, 0, at] = jnp.where(same, real, 0.0).astype(BF16)
            diagonal[kind, 1, at] = jnp.where(same, imag, 0.0).astype(BF16)

    def fold_products(g):
        at = rows_at(0 if p.streamed else g * d, d)
        for part in range(2):
            two = jnp.where(keep_two, dot(diagonal[0, part, at], pick_two, 1, 0), 0.0)
            three = jnp.where(keep_three, dot(diagonal[1, part, at], pick_three, 1, 0), 0.0)
            total = jnp.sum((two + three).reshape(nb, TILE, 2 * p.pairs), axis=0)
            small[part, rows_at(g * TILE, TILE)] = total.astype(BF16)
        if p.direct:
            at = rows_at(g * TILE, TILE)
            hand_out(g, 2 * blk, (small[0, at], small[1, at]))

    each_group(backward_middle, backward_last, group_products, fold_products)

    def first_factor(i):
        first_grad = time_a[i]
        grad_v[pl.ds(edge + i * blk, blk)] = dot(one[i], first_grad, 0, 0)
        products = dot(first_grad, val[rows_at(i * blk, blk)], 1, 1).astype(BF16)
        hand_out(i, 0, (products[:blk], products[blk:]))
        used = 2 * blk + (p.yrows if p.direct else 0)
        if p.half > used:
            rest = jnp.zeros((p.half - used, blk), BF16)
            hand_out(i, used, (rest, rest))

    each(nb, first_factor)

    sums = [jnp.zeros((8, cols), F32) for _ in range(6)]

    def last_stage(i, sums):
        total = jnp.zeros((blk, cols), F32)
        sums = list(sums)
        for branch, ref in ((0, grad_v), (1, gate)):
            before, here, after = (window(ref, i, o) for o in (-1, 0, 1))
            total += taps_of(branch, 0) * after + taps_of(branch, 1) * here + taps_of(branch, 2) * before
            for offset in range(3):
                product = here * window(tok, i, offset - 1)
                sums[3 * branch + offset] += jnp.sum(product.reshape(blk // 8, 8, cols), axis=0)
        grad_x[i] = total.astype(BF16)
        terms = filter_grad[rows_at(i * blk, blk)].T
        term = terms[0:w]
        for h in range(1, p.fold):
            term = term + terms[h * w : (h + 1) * w]
        gradients[i] = term.astype(BF16)
        return tuple(sums)

    if nb <= 8:
        for i in range(nb):
            sums = last_stage(i, sums)
    else:
        sums = lax.fori_loop(0, nb, last_stage, tuple(sums))

    conv = jnp.concatenate([jnp.sum(s, axis=0, keepdims=True) for s in sums] + [jnp.zeros((2, cols), F32)], axis=0)
    term = conv[:, 0:w]
    for h in range(1, p.fold):
        term = term + conv[:, h * w : (h + 1) * w]
    if w < blk:
        term = jnp.concatenate([term, jnp.zeros((8, blk - w), F32)], axis=1)
    high = term.astype(BF16).astype(F32)
    conv_rows = jnp.concatenate([high, term - high], axis=0).astype(BF16)

    ends = [conv_rows]
    if p.full > w + TILE:
        ends.append(jnp.zeros((p.full - w - TILE, blk), BF16))

    def last_rows(i):
        rows = jnp.concatenate([gradients[i], *ends], axis=0)
        middle = p.full // 2
        mine = jnp.where(core == 0, rows[:middle], rows[middle:])
        other = jnp.where(core == 0, rows[middle:], rows[:middle])
        for h in range(p.fold):
            at = slice(h * p.orows, (h + 1) * p.orows)
            keep[h, i, p.mrows :] = mine[at]
            send[h, i, p.mrows :] = other[at]

    each(nb, last_rows)
    if not p.direct:
        small_out[0][...] = jnp.where(core == 0, small[0], small[1])
        small_out[1][...] = jnp.where(core == 0, small[1], small[0])


def token_grad_message_kernel(p, grads, out):
    def one_target(i):
        turned = grads[i].T
        for h in range(p.fold):
            out[h * p.nblk + i] = turned[h * p.width : (h + 1) * p.width]

    each(p.nblk, one_target)


def pick(p, values, wanted):
    value = values[0]
    for i in range(1, len(values)):
        value = jnp.where(wanted == i, values[i], value)
    return value


def add_cores_kernel(p, grad_x, keep, got, *refs):
    count = 0 if p.direct else 2
    out, shares = refs[count], refs[count + 1 :]
    h, _ = place(p)
    y = lax.axis_index("seq") % p.near

    def one_layer(z):
        rows = {}
        for near in range(p.near):
            s = z * p.near + near
            for owner in range(p.fold):
                q = owner * p.seq + s
                total = (keep[owner, s].astype(F32) + got[owner, s].astype(F32)).astype(BF16)
                out[q, 0 : p.width] = grad_x[q]
                out[q, p.width :] = total[p.mrows :]
                total = total[: p.mrows]
                first, last = 2 * p.blk - owner * p.mrows, 2 * p.blk + p.yrows - owner * p.mrows
                lo, hi = max(first, 0), min(last, p.mrows)
                if not p.direct and lo < hi:
                    extra = (refs[0][s].astype(F32) + refs[1][s].astype(F32)).astype(BF16)
                    parts = [total[:lo], extra[lo - first : hi - first], total[hi:]]
                    total = jnp.concatenate([part for part in parts if part.shape[0]], axis=0)
                rows[owner, near] = total
        for share, (step, near_step) in zip(shares, p.plane()):
            by_near = [
                pick(p, [rows[(i + step) % p.fold, (near + near_step) % p.near] for i in range(p.fold)], h)
                for near in range(p.near)
            ]
            share[z] = pick(p, by_near, y)

    each(p.layers, one_layer)


def add_fold_kernel(p, *refs):
    terms, out = refs[:-1], refs[-1]

    def one_layer(z):
        total = terms[0][z].astype(F32)
        for term in terms[1:]:
            total += term[z].astype(F32)
        out[z] = total.astype(BF16)

    each(p.layers, one_layer)


def sum_kernel(p, got, out):
    total = got[0].astype(F32)
    for q in range(1, p.layers):
        total += got[q].astype(F32)
    out[...] = total.astype(BF16)


def filter_rows_kernel(p, got, out):
    for q in range(p.members):
        out[q] = got[q, p.width :]


def token_grad_kernel(p, got, out):
    rows = jnp.concatenate([got[q, 0 : p.width] for q in range(p.members)], axis=0)
    out[...] = rows.T


def finish_factors_kernel(p, *refs):
    pieces, (one, four, *small) = refs[: 2 * p.fold], refs[2 * p.fold :]
    share = shares_in_order(p, pieces)
    for part in range(2):
        rows = [share(part, owner, lambda ref, *_: ref[...]) for owner in range(p.fold)]
        rows = jnp.concatenate(rows, axis=0) if p.fold > 1 else rows[0]
        one[part] = rows[0 : p.blk]
        four[part] = rows[p.blk : 2 * p.blk]
        entries = rows[2 * p.blk : 2 * p.blk + p.yrows]
        if p.direct:
            entries = entries.T
            small[0][part] = entries[: p.pairs]
            small[1][part] = entries[p.pairs :]
        else:
            small[0][part] = entries


def finish_filter_kernel(p, *refs):
    pieces, (filt, conv_value, conv_gate) = refs[: 2 * p.fold], refs[2 * p.fold :]
    share = shares_in_order(p, pieces)
    turned, columns = [], []
    for q in range(p.members):
        rows = [
            share(c, owner, lambda ref, *_: ref[q]) for c in range(2) for owner in range(p.fold)
        ]
        rows = jnp.concatenate(rows, axis=0)
        turned.append(rows[0 : p.width])
        both = rows[p.width : p.width + TILE].astype(F32)
        columns.append((both[:8] + both[8:]).T[: p.width])
    filt[...] = jnp.concatenate(turned, axis=0).T
    sums = jnp.concatenate(columns, axis=0).T
    conv_value[...] = sums[0:3]
    conv_gate[...] = sums[3:6]


def shards(
    tokens, upstream, conv_value, conv_gate, mix_one, mix_two, mix_three, mix_four, filter_log
):
    p = Plan(lax.axis_size("dp"), lax.axis_size("seq"), tokens, mix_one, mix_two)
    dp_at, seq_at = lax.axis_index("dp"), lax.axis_index("seq")
    h_at = (dp_at // 2) % p.fold
    blk, pairs = p.blk, p.pairs

    def shuffle(array):
        return lax.all_to_all(
            array, ("dp", "seq"), 0, 0, tiled=True, axis_index_groups=p.group_lists
        )

    def across_layers(array):
        return lax.all_to_all(
            array, "seq", 0, 0, tiled=True, axis_index_groups=p.layer_groups
        )

    def swap(array):
        return lax.ppermute(array, "dp", p.across_cores())

    def gathered(array, rows):
        pieces = [array]
        for step in range(1, p.fold):
            pieces.append(lax.ppermute(rows(array), "dp", p.across_fold(step)))
        return pieces + [swap(piece) for piece in pieces]

    def gathered_at_once(array):
        return [
            lax.ppermute(array, "dp", p.across_fold(step, side)) if step or side else array
            for side in range(2)
            for step in range(p.fold)
        ]

    if p.direct:
        small = [f.transpose(0, 2, 3, 1).reshape(2, pairs, p.kloc) for f in (mix_two, mix_three)]
    else:
        small = [f.reshape(2, p.kloc, pairs) for f in (mix_two, mix_three)]
        small = [jnp.concatenate(small, axis=2).reshape(2, p.yrows, blk)]
    far = [
        filter_log.reshape(blk, p.channels),
        mix_one.reshape(2, blk, blk),
        mix_four.reshape(2, blk, blk),
        *small,
    ]
    message = call(
        functools.partial(factor_message_kernel, p),
        [shape(p.mrows + p.near * p.frows, blk)] * p.layers,
        *far,
        scratch=[pltpu.VMEM((blk, p.channels // p.fold), BF16)]
        + [pltpu.VMEM(f.shape[1:], BF16) for f in far[1:]]
        + [
            pltpu.VMEM((p.half, blk), BF16),
            pltpu.VMEM((p.channels // p.fold, blk), BF16),
            pltpu.SemaphoreType.DMA((len(far),)),
        ],
        far=range(len(far)),
        limit=60,
        name="factor_message",
    )
    factors = [message[0]]
    for step in range(1, p.layers):
        moves = [
            (s, p.layer_partner(s // p.near, step) * p.near + s % p.near) for s in range(p.seq)
        ]
        factors.append(lax.ppermute(message[step], "seq", moves))
    near_messages = call(
        functools.partial(near_message_kernel, p),
        [shape(p.layers, p.mrows + p.frows, blk)] * p.near,
        *factors,
        name="near_message",
    )
    pieces = [near_messages[0]]
    for step, near_step in p.plane()[1:]:
        piece = near_messages[near_step] if step == 0 else near_messages[0][:, : p.mrows]
        pieces.append(lax.ppermute(piece, ("dp", "seq"), p.across_plane(step, near_step)))
    pieces += [swap(piece) for piece in pieces]

    message = call(
        functools.partial(token_message_kernel, p),
        shape(p.members, 2 * p.width, blk),
        tokens[0],
        upstream[0],
        name="token_message",
    )
    message, factors = lax.optimization_barrier((message, factors))
    received = shuffle(message)
    pieces, received = lax.optimization_barrier((pieces, received))
    one, four, small, filt = call(
        functools.partial(prepare_kernel, p),
        [
            shape(p.nblk, 2 * blk, blk),
            shape(p.nblk, blk, 2 * blk),
            shape(2, p.nblk, p.yrows, blk),
            shape(p.nblk, blk, p.cols, dtype=F32),
        ],
        *pieces,
        name="prepare",
    )
    two, three = call(
        functools.partial(block_factor_kernel, p),
        [shape(p.kgroups, 2 * p.dim, 2 * p.dim)] * 2,
        small.reshape(2, blk, 2 * pairs),
        limit=48 if p.streamed else 24,
        name="block_factors",
    )

    start = (h_at * p.seq + seq_at) * p.width
    taps = jnp.concatenate([conv_value, conv_gate], axis=0)
    taps = lax.dynamic_slice_in_dim(taps, start, p.width, 1)
    taps = jnp.concatenate([taps] * p.fold, axis=1)

    padded = p.length + 16
    grad_x, keep, send, *small = call(
        functools.partial(mixer_kernel, p),
        [
            shape(p.nblk, blk, p.cols),
            shape(p.fold, p.seq, p.share, blk),
            shape(p.fold, p.seq, p.share, blk),
        ]
        + [shape(blk, 2 * pairs)] * (0 if p.direct else 2),
        received,
        taps,
        one,
        four,
        two,
        three,
        filt.reshape(p.length, p.cols),
        scratch=[
            pltpu.VMEM((padded, p.cols), F32),
            pltpu.VMEM((p.length, p.cols), BF16),
            pltpu.VMEM((p.length, p.cols), BF16),
            pltpu.VMEM((p.length, p.cols), BF16),
            pltpu.VMEM((p.kgroups, 2 * p.dim, p.cols), BF16),
            pltpu.VMEM((2 * p.kgroups, 2 * p.dim, p.cols), BF16),
            pltpu.VMEM((p.kgroups, 2 * p.dim, p.cols), F32),
            pltpu.VMEM((p.nblk, 2 * blk, p.cols), BF16),
            pltpu.VMEM((padded, p.cols), F32),
            pltpu.VMEM((padded, p.cols), F32),
            pltpu.VMEM((p.length, p.cols), F32),
            pltpu.VMEM((p.nblk, p.width, blk), BF16),
            pltpu.VMEM((2, blk, 2 * pairs), BF16),
            pltpu.VMEM((p.kgroups, 2 * p.dim, p.cols), BF16),
            pltpu.VMEM((2, 2, (1 if p.streamed else p.kgroups) * p.dim, p.dim), BF16),
        ]
        + [pltpu.VMEM((2 * p.dim, 2 * p.dim), BF16)] * (2 if p.streamed else 0),
        far=(4, 5) if p.streamed else (),
        limit=60 if p.streamed else 24,
        name="mixer",
    )

    def summed_over_groups(array):
        if p.groups == 1:
            return array
        total = array.astype(F32)
        for step in range(1, p.groups):
            total += lax.ppermute(array, "dp", p.across_groups(step)).astype(F32)
        return total.astype(BF16)

    grad_x = call(
        functools.partial(token_grad_message_kernel, p),
        shape(p.members, p.width, blk),
        grad_x,
        name="token_grad_message",
    )
    message, *shares = call(
        functools.partial(add_cores_kernel, p),
        [shape(p.members, p.width + p.orows, blk)]
        + [shape(p.layers, p.mrows, blk)] * len(p.plane()),
        grad_x,
        keep,
        swap(send),
        *[f.reshape(p.seq, p.yrows, blk) for f in (small if p.direct else (small[0], swap(small[1])))],
        name="add_cores",
    )
    received = shuffle(message)

    message = shares[0]
    if len(shares) > 1:
        message = call(
            functools.partial(add_fold_kernel, p),
            shape(p.layers, p.mrows, blk),
            message,
            *[
                lax.ppermute(share, ("dp", "seq"), p.across_plane(*steps))
                for share, steps in zip(shares[1:], p.plane()[1:])
            ],
            name="add_fold",
        )
    message, received = lax.optimization_barrier((message, received))
    factor_grads = across_layers(message)

    rows = call(
        functools.partial(filter_rows_kernel, p),
        shape(p.members, p.orows, blk),
        received,
        name="filter_rows",
    )
    rows = gathered(summed_over_groups(rows), lambda a: a)
    token_grad = call(
        functools.partial(token_grad_kernel, p), shape(blk, p.channels), received, name="token_grad"
    )
    grad_filter, sum_value, sum_gate = call(
        functools.partial(finish_filter_kernel, p),
        [
            shape(blk, p.channels),
            shape(3, p.channels, dtype=F32),
            shape(3, p.channels, dtype=F32),
        ],
        *rows,
        name="finish_filter",
    )
    factor_grads, token_grad, grad_filter, sum_value, sum_gate = lax.optimization_barrier(
        (factor_grads, token_grad, grad_filter, sum_value, sum_gate)
    )
    sums = call(
        functools.partial(sum_kernel, p), shape(p.mrows, blk), factor_grads, name="sum_sources"
    )
    grad_one, grad_four, *small = call(
        functools.partial(finish_factors_kernel, p),
        [shape(2, blk, blk)] * 2
        + ([shape(2, pairs, p.kloc)] * 2 if p.direct else [shape(2, p.yrows, blk)]),
        *gathered_at_once(summed_over_groups(sums)),
        name="finish_factors",
    )
    if p.direct:
        small = [f.reshape(2, p.nblk, p.nblk, p.kloc).transpose(0, 3, 1, 2) for f in small]
    else:
        small = small[0].reshape(2, p.kloc, 2, p.nblk, p.nblk)
        small = [small[:, :, 0], small[:, :, 1]]
    return (
        token_grad[None],
        sum_value,
        sum_gate,
        grad_one.reshape(mix_one.shape),
        *small,
        grad_four.reshape(mix_four.shape),
        grad_filter.reshape(filter_log.shape),
    )


def solution(mesh):
    return jax.shard_map(
        shards,
        mesh=mesh,
        in_specs=(
            P("dp", "seq", None),
            P("dp", "seq", None),
            P(),
            P(),
            P(None, "seq", None, None),
            P(None, "seq", None, None),
            P(None, "seq", None, None),
            P(None, "seq", None, None),
            P("seq", None, None),
        ),
        out_specs=(
            P("dp", "seq", None),
            P(),
            P(),
            P(None, "seq", None, None),
            P(None, "seq", None, None),
            P(None, "seq", None, None),
            P(None, "seq", None, None),
            P("seq", None, None),
        ),
        check_vma=False,
    )
```

```python
import functools

import jax
import jax.numpy as jnp
from jax import lax
from jax.experimental import pallas as pl
from jax.experimental.pallas import tpu as pltpu
from jax.sharding import PartitionSpec as P

F32 = jnp.float32
BF16 = jnp.bfloat16
TILE = 16
VMEM = pl.BlockSpec(memory_space=pltpu.VMEM)
FAR = pl.BlockSpec(memory_space=pl.ANY)


class Plan:
    def __init__(self, dp, seq, tokens, mix_one, mix_two):
        self.dp, self.seq = dp, seq
        self.blk = mix_one.shape[-1]
        self.channels = tokens.shape[-1]
        assert tokens.shape[1] == self.blk and dp % 2 == 0
        self.nblk = seq
        self.near = 2 if seq % 2 == 0 else 1
        self.layers = seq // self.near
        self.kloc = mix_two.shape[1]
        half_dp = dp // 2
        self.fold = max(
            f
            for f in range(1, half_dp + 1)
            if half_dp % f == 0 and self.channels % (seq * f * TILE) == 0
        )
        self.groups = half_dp // self.fold
        self.members = self.fold * seq
        self.width = self.channels // self.members
        assert self.width <= 128
        self.cols = self.fold * self.width
        self.length = self.nblk * self.blk
        self.pairs = self.nblk * self.nblk
        self.yrows = self.kloc * 2 * self.pairs // self.blk
        self.direct = self.yrows == self.kloc
        self.streamed = self.nblk * TILE > self.blk
        self.kgroups = self.blk // TILE
        self.dim = self.nblk * TILE
        unit = TILE * self.fold
        self.half = -(-(2 * self.blk + self.yrows) // unit) * unit
        self.mrows = self.half // self.fold
        self.cores_share = self.width % (2 * TILE) == 0
        self.frows = self.width // 2 if self.cores_share else self.width
        self.full = -(-(self.width + TILE) // (2 * unit)) * 2 * unit
        self.orows = self.full // (2 * self.fold)
        self.share = self.mrows + self.orows
        self.group_lists = [
            [
                ((g * self.fold + h) * 2 + core) * seq + s
                for h in range(self.fold)
                for s in range(seq)
            ]
            for g in range(self.groups)
            for core in range(2)
        ]

    def across_cores(self):
        return [(d, d ^ 1) for d in range(self.dp)]

    def across_fold(self, step, side=0):
        moves = []
        for g in range(self.groups):
            for h in range(self.fold):
                for core in range(2):
                    source = (g * self.fold + h) * 2 + core
                    target = (g * self.fold + (h + step) % self.fold) * 2 + (core ^ side)
                    moves.append((source, target))
        return moves

    def layer_partner(self, z, step):
        if self.layers & (self.layers - 1) == 0:
            return z ^ step
        return (step + self.layers - z) % self.layers

    def across_plane(self, step, near_step, side=0):
        return [
            (source * self.seq + s, target * self.seq + s // self.near * self.near + (s + near_step) % self.near)
            for source, target in self.across_fold(step, side)
            for s in range(self.seq)
        ]

    def plane(self):
        return [(step, near_step) for step in range(self.fold) for near_step in range(self.near)]

    def across_groups(self, step):
        block = 2 * self.fold
        return [(d, (d + step * block) % self.dp) for d in range(self.dp)]


def each(count, body, unrolled=True):
    if count <= 8 and unrolled:
        for i in range(count):
            body(i)
    else:
        lax.fori_loop(0, count, lambda i, c: (body(i), c)[1], 0)


def rows_at(start, size):
    return pl.ds(start if isinstance(start, int) else pl.multiple_of(start, TILE), size)


def dot(a, b, ca, cb):
    return lax.dot_general(a, b, (((ca,), (cb,)), ((), ())), preferred_element_type=F32)


def call(kernel, out_shape, *args, scratch=(), far=(), limit=24, name=None):
    single = not isinstance(out_shape, (list, tuple))
    return pl.pallas_call(
        kernel,
        out_shape=out_shape,
        in_specs=[FAR if i in far else VMEM for i in range(len(args))],
        out_specs=VMEM if single else [VMEM] * len(out_shape),
        scratch_shapes=list(scratch),
        compiler_params=pltpu.CompilerParams(vmem_limit_bytes=limit * 2**20),
        name=name,
    )(*args)


def shape(*dims, dtype=BF16):
    return jax.ShapeDtypeStruct(dims, dtype)


def place(p):
    at = lax.axis_index("dp")
    return (at // 2) % p.fold, at % 2


def factor_message_kernel(p, *refs):
    count = 5 if p.direct else 4
    far, outs, refs = refs[:count], refs[count : count + p.layers], refs[count + p.layers :]
    near, rows, turned, done = refs[:-3], *refs[-3:]
    h, core = place(p)
    part_width = p.seq * p.width
    sources = [far[0].at[:, pl.ds(pl.multiple_of(h * part_width, p.blk), part_width)]]
    sources += [f.at[core] for f in far[1:]]
    copies = [pltpu.make_async_copy(f, n, done.at[i]) for i, (f, n) in enumerate(zip(sources, near))]
    for copy in copies:
        copy.start()
    filt, one, four = near[:3]
    for copy in copies[1:]:
        copy.wait()
    rows[0 : p.blk] = one[...]
    rows[p.blk : 2 * p.blk] = four[...]
    if p.direct:
        small = jnp.concatenate([near[3][...], near[4][...]], axis=0).T
    else:
        small = near[3][...]
    rows[2 * p.blk : 2 * p.blk + p.yrows] = small
    pad = p.half - 2 * p.blk - p.yrows
    if pad:
        rows[p.half - pad :] = jnp.zeros((pad, p.blk), BF16)
    mine = rows[0 : p.mrows]
    for owner in range(1, p.fold):
        mine = jnp.where(h == owner, rows[owner * p.mrows : (owner + 1) * p.mrows], mine)
    copies[0].wait()
    turned[...] = filt[...].T

    z = lax.axis_index("seq") // p.near
    for near in range(p.near):
        logs = []
        for target in range(p.layers):
            at = (target * p.near + near) * p.width
            rows_here = turned[at : at + p.width]
            if p.cores_share:
                rows_here = jnp.where(core == 0, rows_here[: p.frows], rows_here[p.frows :])
            logs.append(rows_here)
        for step in range(p.layers):
            chosen = pick(p, [logs[p.layer_partner(at, step)] for at in range(p.layers)], z)
            outs[step][p.mrows + near * p.frows : p.mrows + (near + 1) * p.frows] = chosen
    for step in range(p.layers):
        outs[step][0 : p.mrows] = mine


def near_message_kernel(p, *refs):
    got, outs = refs[: p.layers], refs[p.layers :]
    y = lax.axis_index("seq") % p.near
    for z in range(p.layers):
        logs = [got[z][p.mrows + i * p.frows : p.mrows + (i + 1) * p.frows] for i in range(p.near)]
        for step in range(p.near):
            outs[step][z, 0 : p.mrows] = got[z][0 : p.mrows]
            outs[step][z, p.mrows :] = pick(p, [logs[(i + step) % p.near] for i in range(p.near)], y)


def token_message_kernel(p, tokens, upstream, out):
    w = p.width
    token_rows = tokens[...].T
    upstream_rows = upstream[...].T
    for q in range(p.members):
        out[q, 0:w] = token_rows[q * w : (q + 1) * w]
        out[q, w : 2 * w] = upstream_rows[q * w : (q + 1) * w]


def shares_in_order(p, pieces):
    h, core = place(p)

    def share(c, owner, part):
        value = None
        for side in range(2):
            for step in range(p.fold):
                piece = part(pieces[side * p.fold + step], side, step)
                if value is None:
                    value = piece
                    continue
                here = core == (c if side == 0 else 1 - c)
                value = jnp.where(here & (h == (owner + step) % p.fold), piece, value)
        return value

    return share


def prepare_kernel(p, *refs):
    count = 2 * len(p.plane())
    pieces, (one, four, small, filt) = refs[:count], refs[count:]
    h, core = place(p)
    y = lax.axis_index("seq") % p.near

    def from_near(z, near, side, step, rows):
        first = (side * p.fold + step) * p.near
        return pick(p, [pieces[first + (near - at) % p.near][z, rows] for at in range(p.near)], y)

    def half_rows(z, near):
        sides = []
        for side in range(2):
            steps = [from_near(z, near, side, step, slice(0, p.mrows)) for step in range(p.fold)]
            shares = [
                pick(p, [steps[(at - owner) % p.fold] for at in range(p.fold)], h)
                for owner in range(p.fold)
            ]
            sides.append(jnp.concatenate(shares, axis=0) if p.fold > 1 else shares[0])
        return [jnp.where(core == c, sides[0], sides[1]) for c in range(2)]

    def one_layer(z):
        for near in range(p.near):
            i = p.layer_partner(lax.axis_index("seq") // p.near, z) * p.near + near
            for side, rows in enumerate(half_rows(z, near)):
                one[i, side * p.blk : (side + 1) * p.blk] = rows[0 : p.blk]
                factor = rows[p.blk : 2 * p.blk]
                four[i, :, side * p.blk : (side + 1) * p.blk] = factor if side == 0 else -factor
                small[side, i] = rows[2 * p.blk : 2 * p.blk + p.yrows]
            logs = from_near(z, near, 0, 0, slice(p.mrows, p.mrows + p.frows))
            if p.cores_share:
                other = from_near(z, near, 1, 0, slice(p.mrows, p.mrows + p.frows))
                logs = [jnp.where(core == 0, logs, other), jnp.where(core == 0, other, logs)]
                logs = jnp.concatenate(logs, axis=0)
            if p.fold > 1:
                logs = jnp.concatenate([logs] * p.fold, axis=0)
            filt[i] = jnp.exp(logs.T.astype(F32))

    each(p.layers, one_layer)


def iota(dims, axis):
    return lax.broadcasted_iota(jnp.int32, dims, axis)


def block_masks(p):
    d, nb, pairs = p.dim, p.nblk, p.pairs
    same = iota((d, d), 0) % TILE == iota((d, d), 1) // nb
    lane = iota((d, 2 * pairs), 1)
    block = iota((d, 2 * pairs), 0) // TILE
    keep_two = (lane < pairs) & (lane % nb == block)
    keep_three = (lane >= pairs) & ((lane - pairs) // nb == block)
    return same, keep_two, keep_three


def selectors(p, turned):
    d, nb, pairs = p.dim, p.nblk, p.pairs
    dims = (d, 2 * pairs) if turned else (2 * pairs, d)
    lane = iota(dims, 1 if turned else 0)
    block = iota(dims, 0 if turned else 1) % nb
    two = (lane < pairs) & (lane // nb == block)
    three = (lane >= pairs) & ((lane - pairs) % nb == block)
    return two.astype(BF16), three.astype(BF16)


def block_factor_kernel(p, small, two, three):
    same, keep_two, keep_three = block_masks(p)
    pick_two, pick_three = selectors(p, False)
    d = p.dim

    def one_group(g):
        parts = {}
        for part in range(2):
            entries = small[part, rows_at(g * TILE, TILE)]
            tiled = jnp.concatenate([entries] * p.nblk, axis=0)
            zero = jnp.zeros_like(tiled)
            for name, keep, pick in (("two", keep_two, pick_two), ("three", keep_three, pick_three)):
                spread = dot(jnp.where(keep, tiled, zero), pick, 1, 0)
                parts[name, part] = jnp.where(same, spread, 0.0).astype(BF16)
        two[g, :d, :d] = parts["two", 0]
        two[g, d:, d:] = parts["two", 0]
        two[g, :d, d:] = parts["two", 1]
        two[g, d:, :d] = -parts["two", 1]
        three[g, :d, :d] = parts["three", 0]
        three[g, d:, d:] = parts["three", 0]
        three[g, :d, d:] = -parts["three", 1]
        three[g, d:, :d] = parts["three", 1]

    each(p.kgroups, one_group)


def mixer_kernel(
    p, tokens_in, taps, one, four, two_far, three_far, filt,
    grad_x, keep, send, *refs,
):
    _, core = place(p)
    small_out = None if p.direct else refs[:2]
    (tok, ups, val, mix, groups_a, groups_b, second, time_a, gate, grad_v, filter_grad,
     gradients, small, groups_d, diagonal, *near) = refs if p.direct else refs[2:]

    def hand_out(i, base, values):
        mine = jnp.where(core == 0, values[0], values[1])
        other = jnp.where(core == 0, values[1], values[0])
        last = base + values[0].shape[0]
        for h in range(p.fold):
            lo, hi = max(base, h * p.mrows), min(last, (h + 1) * p.mrows)
            if lo < hi:
                keep[h, i, lo - h * p.mrows : hi - h * p.mrows] = mine[lo - base : hi - base]
                send[h, i, lo - h * p.mrows : hi - h * p.mrows] = other[lo - base : hi - base]

    def factor(far, at, g):
        if not p.streamed:
            return far[g]
        pltpu.sync_copy(far.at[g], near[at])
        return near[at][...]

    blk, nb, d, w, cols = p.blk, p.nblk, p.dim, p.width, p.cols
    edge = 8

    def taps_of(branch, offset):
        return taps[3 * branch + offset : 3 * branch + offset + 1, :]

    zero_edge = jnp.zeros((edge, cols), F32)
    for ref in (tok, gate, grad_v):
        ref[0:edge] = zero_edge
        ref[edge + p.length : 2 * edge + p.length] = zero_edge

    def load(i):
        both = [tokens_in[h * nb + i] for h in range(p.fold)]
        t = jnp.concatenate([b[0:w] for b in both], axis=0) if p.fold > 1 else both[0][0:w]
        u = jnp.concatenate([b[w:] for b in both], axis=0) if p.fold > 1 else both[0][w:]
        tok[rows_at(edge + i * blk, blk) if isinstance(i, int) else pl.ds(pl.multiple_of(edge + i * blk, 8), blk)] = t.T.astype(F32)
        ups[rows_at(i * blk, blk)] = u.T

    each(nb, load)

    def window(ref, i, offset):
        return ref[pl.ds(edge + i * blk + offset, blk)]

    def spread(ref, i, value):
        for part in range(2):
            for g in range(p.kgroups):
                row = part * blk + g * TILE
                ref[g, rows_at((part * nb + i) * TILE, TILE)] = value[row : row + TILE]

    def first_stage(i):
        before, here, after = (window(tok, i, o) for o in (-1, 0, 1))
        values = taps_of(0, 0) * before + taps_of(0, 1) * here + taps_of(0, 2) * after
        gating = taps_of(1, 0) * before + taps_of(1, 1) * here + taps_of(1, 2) * after
        values = values.astype(BF16)
        val[rows_at(i * blk, blk)] = values
        up = ups[rows_at(i * blk, blk)].astype(F32)
        mix[rows_at(i * blk, blk)] = (up * gating.astype(BF16).astype(F32)).astype(BF16)
        spread(groups_a, i, dot(one[i], values, 1, 0).astype(BF16))

    each(nb, first_stage)

    def filter_of(g):
        f = filt[rows_at(g * d, d)]
        return f

    def forward_middle(g):
        f = filter_of(g)
        f2 = jnp.concatenate([f, f], axis=0)
        sec = dot(factor(two_far, 0, g), groups_a[g], 0, 0)
        second[g] = sec
        groups_b[g] = (f2 * sec).astype(BF16)

    def unspread(g, value):
        for part in range(2):
            for i in range(nb):
                row = (part * nb + i) * TILE
                time_a[i, rows_at(part * blk + g * TILE, TILE)] = value[row : row + TILE]

    def forward_last(g):
        unspread(g, dot(factor(three_far, 1, g), groups_b[g], 1, 0).astype(BF16))

    def each_group(*stages):
        if p.streamed:
            each(p.kgroups, lambda g: [stage(g) for stage in stages], unrolled=False)
        else:
            for stage in stages:
                each(p.kgroups, stage)

    each_group(forward_middle, forward_last)

    def last_factor(n):
        third = time_a[n]
        last = four[n]
        mixed = dot(last, third, 1, 0)
        at = rows_at(n * blk, blk)
        gate[pl.ds(edge + n * blk, blk)] = ups[at].astype(F32) * mixed
        grads = mix[at]
        back = dot(last, grads, 0, 0).astype(BF16)
        for part in range(2):
            for g in range(p.kgroups):
                row = part * blk + g * TILE
                groups_b[p.kgroups + g, rows_at((part * nb + n) * TILE, TILE)] = back[row : row + TILE]
        products = dot(grads, third, 1, 1)
        hand_out(n, blk, (products[:, 0:blk].astype(BF16), (-products[:, blk:]).astype(BF16)))

    each(nb, last_factor)

    same, keep_two, keep_three = block_masks(p)
    pick_two, pick_three = selectors(p, True)

    def backward_middle(g):
        f = filter_of(g)
        f2 = jnp.concatenate([f, f], axis=0)
        weighted_grad = dot(factor(three_far, 1, g), groups_b[p.kgroups + g], 0, 0)
        term = weighted_grad * second[g]
        filter_grad[rows_at(g * d, d)] = f * (term[:d] + term[d:])
        groups_d[g] = (f2 * weighted_grad).astype(BF16)

    def backward_last(g):
        unspread(g, dot(factor(two_far, 0, g), groups_d[g], 1, 0).astype(BF16))

    def group_products(g):
        at = rows_at(0 if p.streamed else g * d, d)
        three = dot(groups_b[p.kgroups + g], groups_b[g], 1, 1)
        two = dot(groups_a[g], groups_d[g], 1, 1)
        for kind, real, imag in (
            (0, two[:d, :d] + two[d:, d:], two[:d, d:] - two[d:, :d]),
            (1, three[:d, :d] + three[d:, d:], three[d:, :d] - three[:d, d:]),
        ):
            diagonal[kind, 0, at] = jnp.where(same, real, 0.0).astype(BF16)
            diagonal[kind, 1, at] = jnp.where(same, imag, 0.0).astype(BF16)

    def fold_products(g):
        at = rows_at(0 if p.streamed else g * d, d)
        for part in range(2):
            two = jnp.where(keep_two, dot(diagonal[0, part, at], pick_two, 1, 0), 0.0)
            three = jnp.where(keep_three, dot(diagonal[1, part, at], pick_three, 1, 0), 0.0)
            total = jnp.sum((two + three).reshape(nb, TILE, 2 * p.pairs), axis=0)
            small[part, rows_at(g * TILE, TILE)] = total.astype(BF16)
        if p.direct:
            at = rows_at(g * TILE, TILE)
            hand_out(g, 2 * blk, (small[0, at], small[1, at]))

    each_group(backward_middle, backward_last, group_products, fold_products)

    def first_factor(i):
        first_grad = time_a[i]
        grad_v[pl.ds(edge + i * blk, blk)] = dot(one[i], first_grad, 0, 0)
        products = dot(first_grad, val[rows_at(i * blk, blk)], 1, 1).astype(BF16)
        hand_out(i, 0, (products[:blk], products[blk:]))
        used = 2 * blk + (p.yrows if p.direct else 0)
        if p.half > used:
            rest = jnp.zeros((p.half - used, blk), BF16)
            hand_out(i, used, (rest, rest))

    each(nb, first_factor)

    sums = [jnp.zeros((8, cols), F32) for _ in range(6)]

    def last_stage(i, sums):
        total = jnp.zeros((blk, cols), F32)
        sums = list(sums)
        for branch, ref in ((0, grad_v), (1, gate)):
            before, here, after = (window(ref, i, o) for o in (-1, 0, 1))
            total += taps_of(branch, 0) * after + taps_of(branch, 1) * here + taps_of(branch, 2) * before
            for offset in range(3):
                product = here * window(tok, i, offset - 1)
                sums[3 * branch + offset] += jnp.sum(product.reshape(blk // 8, 8, cols), axis=0)
        grad_x[i] = total.astype(BF16)
        terms = filter_grad[rows_at(i * blk, blk)].T
        term = terms[0:w]
        for h in range(1, p.fold):
            term = term + terms[h * w : (h + 1) * w]
        gradients[i] = term.astype(BF16)
        return tuple(sums)

    if nb <= 8:
        for i in range(nb):
            sums = last_stage(i, sums)
    else:
        sums = lax.fori_loop(0, nb, last_stage, tuple(sums))

    conv = jnp.concatenate([jnp.sum(s, axis=0, keepdims=True) for s in sums] + [jnp.zeros((2, cols), F32)], axis=0)
    term = conv[:, 0:w]
    for h in range(1, p.fold):
        term = term + conv[:, h * w : (h + 1) * w]
    if w < blk:
        term = jnp.concatenate([term, jnp.zeros((8, blk - w), F32)], axis=1)
    high = term.astype(BF16).astype(F32)
    conv_rows = jnp.concatenate([high, term - high], axis=0).astype(BF16)

    ends = [conv_rows]
    if p.full > w + TILE:
        ends.append(jnp.zeros((p.full - w - TILE, blk), BF16))

    def last_rows(i):
        rows = jnp.concatenate([gradients[i], *ends], axis=0)
        middle = p.full // 2
        mine = jnp.where(core == 0, rows[:middle], rows[middle:])
        other = jnp.where(core == 0, rows[middle:], rows[:middle])
        for h in range(p.fold):
            at = slice(h * p.orows, (h + 1) * p.orows)
            keep[h, i, p.mrows :] = mine[at]
            send[h, i, p.mrows :] = other[at]

    each(nb, last_rows)
    if not p.direct:
        small_out[0][...] = jnp.where(core == 0, small[0], small[1])
        small_out[1][...] = jnp.where(core == 0, small[1], small[0])


def token_grad_message_kernel(p, grads, out):
    def one_target(i):
        turned = grads[i].T
        for h in range(p.fold):
            out[h * p.nblk + i] = turned[h * p.width : (h + 1) * p.width]

    each(p.nblk, one_target)


def pick(p, values, wanted):
    value = values[0]
    for i in range(1, len(values)):
        value = jnp.where(wanted == i, values[i], value)
    return value


def add_cores_kernel(p, grad_x, keep, got, *refs):
    count = 0 if p.direct else 2
    out, shares = refs[count], refs[count + 1 :]
    h, _ = place(p)
    y = lax.axis_index("seq") % p.near

    def one_layer(z):
        rows = {}
        for near in range(p.near):
            s = z * p.near + near
            for owner in range(p.fold):
                q = owner * p.seq + s
                total = (keep[owner, s].astype(F32) + got[owner, s].astype(F32)).astype(BF16)
                out[q, 0 : p.width] = grad_x[q]
                out[q, p.width :] = total[p.mrows :]
                total = total[: p.mrows]
                first, last = 2 * p.blk - owner * p.mrows, 2 * p.blk + p.yrows - owner * p.mrows
                lo, hi = max(first, 0), min(last, p.mrows)
                if not p.direct and lo < hi:
                    extra = (refs[0][s].astype(F32) + refs[1][s].astype(F32)).astype(BF16)
                    parts = [total[:lo], extra[lo - first : hi - first], total[hi:]]
                    total = jnp.concatenate([part for part in parts if part.shape[0]], axis=0)
                rows[owner, near] = total
        for share, (step, near_step) in zip(shares, p.plane()):
            by_near = [
                pick(p, [rows[(i + step) % p.fold, (near + near_step) % p.near] for i in range(p.fold)], h)
                for near in range(p.near)
            ]
            share[z] = pick(p, by_near, y)

    each(p.layers, one_layer)


def add_fold_kernel(p, *refs):
    count = len(p.plane())
    terms, outs = refs[:count], refs[count:]
    z = lax.axis_index("seq") // p.near
    totals = []
    for layer in range(p.layers):
        total = terms[0][layer].astype(F32)
        for term in terms[1:]:
            total += term[layer].astype(F32)
        totals.append(total.astype(BF16))
    for step in range(p.layers):
        outs[step][...] = pick(p, [totals[p.layer_partner(at, step)] for at in range(p.layers)], z)


def sum_kernel(p, *refs):
    terms, out = refs[:-1], refs[-1]
    total = terms[0][...].astype(F32)
    for term in terms[1:]:
        total += term[...].astype(F32)
    out[...] = total.astype(BF16)


def filter_rows_kernel(p, got, out):
    for q in range(p.members):
        out[q] = got[q, p.width :]


def token_grad_kernel(p, got, out):
    rows = jnp.concatenate([got[q, 0 : p.width] for q in range(p.members)], axis=0)
    out[...] = rows.T


def finish_factors_kernel(p, *refs):
    pieces, (one, four, *small) = refs[: 2 * p.fold], refs[2 * p.fold :]
    share = shares_in_order(p, pieces)
    for part in range(2):
        rows = [share(part, owner, lambda ref, *_: ref[...]) for owner in range(p.fold)]
        rows = jnp.concatenate(rows, axis=0) if p.fold > 1 else rows[0]
        one[part] = rows[0 : p.blk]
        four[part] = rows[p.blk : 2 * p.blk]
        entries = rows[2 * p.blk : 2 * p.blk + p.yrows]
        if p.direct:
            entries = entries.T
            small[0][part] = entries[: p.pairs]
            small[1][part] = entries[p.pairs :]
        else:
            small[0][part] = entries


def finish_filter_kernel(p, *refs):
    pieces, (filt, conv_value, conv_gate) = refs[: 2 * p.fold], refs[2 * p.fold :]
    share = shares_in_order(p, pieces)
    turned, columns = [], []
    for q in range(p.members):
        rows = [
            share(c, owner, lambda ref, *_: ref[q]) for c in range(2) for owner in range(p.fold)
        ]
        rows = jnp.concatenate(rows, axis=0)
        turned.append(rows[0 : p.width])
        both = rows[p.width : p.width + TILE].astype(F32)
        columns.append((both[:8] + both[8:]).T[: p.width])
    filt[...] = jnp.concatenate(turned, axis=0).T
    sums = jnp.concatenate(columns, axis=0).T
    conv_value[...] = sums[0:3]
    conv_gate[...] = sums[3:6]


def shards(
    tokens, upstream, conv_value, conv_gate, mix_one, mix_two, mix_three, mix_four, filter_log
):
    p = Plan(lax.axis_size("dp"), lax.axis_size("seq"), tokens, mix_one, mix_two)
    dp_at, seq_at = lax.axis_index("dp"), lax.axis_index("seq")
    h_at = (dp_at // 2) % p.fold
    blk, pairs = p.blk, p.pairs

    def shuffle(array):
        return lax.all_to_all(
            array, ("dp", "seq"), 0, 0, tiled=True, axis_index_groups=p.group_lists
        )

    def across_layers(pieces):
        got = [pieces[0]]
        for step in range(1, p.layers):
            moves = [
                (s, p.layer_partner(s // p.near, step) * p.near + s % p.near) for s in range(p.seq)
            ]
            got.append(lax.ppermute(pieces[step], "seq", moves))
        return got

    def swap(array):
        return lax.ppermute(array, "dp", p.across_cores())

    def gathered(array, rows):
        pieces = [array]
        for step in range(1, p.fold):
            pieces.append(lax.ppermute(rows(array), "dp", p.across_fold(step)))
        return pieces + [swap(piece) for piece in pieces]

    def gathered_at_once(array):
        return [
            lax.ppermute(array, "dp", p.across_fold(step, side)) if step or side else array
            for side in range(2)
            for step in range(p.fold)
        ]

    if p.direct:
        small = [f.transpose(0, 2, 3, 1).reshape(2, pairs, p.kloc) for f in (mix_two, mix_three)]
    else:
        small = [f.reshape(2, p.kloc, pairs) for f in (mix_two, mix_three)]
        small = [jnp.concatenate(small, axis=2).reshape(2, p.yrows, blk)]
    far = [
        filter_log.reshape(blk, p.channels),
        mix_one.reshape(2, blk, blk),
        mix_four.reshape(2, blk, blk),
        *small,
    ]
    message = call(
        functools.partial(factor_message_kernel, p),
        [shape(p.mrows + p.near * p.frows, blk)] * p.layers,
        *far,
        scratch=[pltpu.VMEM((blk, p.channels // p.fold), BF16)]
        + [pltpu.VMEM(f.shape[1:], BF16) for f in far[1:]]
        + [
            pltpu.VMEM((p.half, blk), BF16),
            pltpu.VMEM((p.channels // p.fold, blk), BF16),
            pltpu.SemaphoreType.DMA((len(far),)),
        ],
        far=range(len(far)),
        limit=60,
        name="factor_message",
    )
    factors = across_layers(message)
    near_messages = call(
        functools.partial(near_message_kernel, p),
        [shape(p.layers, p.mrows + p.frows, blk)] * p.near,
        *factors,
        name="near_message",
    )
    pieces = [near_messages[0]]
    for step, near_step in p.plane()[1:]:
        piece = near_messages[near_step] if step == 0 else near_messages[0][:, : p.mrows]
        pieces.append(lax.ppermute(piece, ("dp", "seq"), p.across_plane(step, near_step)))
    pieces += [swap(piece) for piece in pieces]

    message = call(
        functools.partial(token_message_kernel, p),
        shape(p.members, 2 * p.width, blk),
        tokens[0],
        upstream[0],
        name="token_message",
    )
    message, factors = lax.optimization_barrier((message, factors))
    received = shuffle(message)
    pieces, received = lax.optimization_barrier((pieces, received))
    one, four, small, filt = call(
        functools.partial(prepare_kernel, p),
        [
            shape(p.nblk, 2 * blk, blk),
            shape(p.nblk, blk, 2 * blk),
            shape(2, p.nblk, p.yrows, blk),
            shape(p.nblk, blk, p.cols, dtype=F32),
        ],
        *pieces,
        name="prepare",
    )
    two, three = call(
        functools.partial(block_factor_kernel, p),
        [shape(p.kgroups, 2 * p.dim, 2 * p.dim)] * 2,
        small.reshape(2, blk, 2 * pairs),
        limit=48 if p.streamed else 24,
        name="block_factors",
    )

    start = (h_at * p.seq + seq_at) * p.width
    taps = jnp.concatenate([conv_value, conv_gate], axis=0)
    taps = lax.dynamic_slice_in_dim(taps, start, p.width, 1)
    taps = jnp.concatenate([taps] * p.fold, axis=1)

    padded = p.length + 16
    grad_x, keep, send, *small = call(
        functools.partial(mixer_kernel, p),
        [
            shape(p.nblk, blk, p.cols),
            shape(p.fold, p.seq, p.share, blk),
            shape(p.fold, p.seq, p.share, blk),
        ]
        + [shape(blk, 2 * pairs)] * (0 if p.direct else 2),
        received,
        taps,
        one,
        four,
        two,
        three,
        filt.reshape(p.length, p.cols),
        scratch=[
            pltpu.VMEM((padded, p.cols), F32),
            pltpu.VMEM((p.length, p.cols), BF16),
            pltpu.VMEM((p.length, p.cols), BF16),
            pltpu.VMEM((p.length, p.cols), BF16),
            pltpu.VMEM((p.kgroups, 2 * p.dim, p.cols), BF16),
            pltpu.VMEM((2 * p.kgroups, 2 * p.dim, p.cols), BF16),
            pltpu.VMEM((p.kgroups, 2 * p.dim, p.cols), F32),
            pltpu.VMEM((p.nblk, 2 * blk, p.cols), BF16),
            pltpu.VMEM((padded, p.cols), F32),
            pltpu.VMEM((padded, p.cols), F32),
            pltpu.VMEM((p.length, p.cols), F32),
            pltpu.VMEM((p.nblk, p.width, blk), BF16),
            pltpu.VMEM((2, blk, 2 * pairs), BF16),
            pltpu.VMEM((p.kgroups, 2 * p.dim, p.cols), BF16),
            pltpu.VMEM((2, 2, (1 if p.streamed else p.kgroups) * p.dim, p.dim), BF16),
        ]
        + [pltpu.VMEM((2 * p.dim, 2 * p.dim), BF16)] * (2 if p.streamed else 0),
        far=(4, 5) if p.streamed else (),
        limit=60 if p.streamed else 24,
        name="mixer",
    )

    def summed_over_groups(array):
        if p.groups == 1:
            return array
        total = array.astype(F32)
        for step in range(1, p.groups):
            total += lax.ppermute(array, "dp", p.across_groups(step)).astype(F32)
        return total.astype(BF16)

    grad_x = call(
        functools.partial(token_grad_message_kernel, p),
        shape(p.members, p.width, blk),
        grad_x,
        name="token_grad_message",
    )
    message, *shares = call(
        functools.partial(add_cores_kernel, p),
        [shape(p.members, p.width + p.orows, blk)]
        + [shape(p.layers, p.mrows, blk)] * len(p.plane()),
        grad_x,
        keep,
        swap(send),
        *[f.reshape(p.seq, p.yrows, blk) for f in (small if p.direct else (small[0], swap(small[1])))],
        name="add_cores",
    )
    received = shuffle(message)

    message = call(
        functools.partial(add_fold_kernel, p),
        [shape(p.mrows, blk)] * p.layers,
        shares[0],
        *[
            lax.ppermute(share, ("dp", "seq"), p.across_plane(*steps))
            for share, steps in zip(shares[1:], p.plane()[1:])
        ],
        name="add_fold",
    )
    message, received = lax.optimization_barrier((message, received))
    factor_grads = across_layers(message)

    rows = call(
        functools.partial(filter_rows_kernel, p),
        shape(p.members, p.orows, blk),
        received,
        name="filter_rows",
    )
    rows = gathered_at_once(summed_over_groups(rows))
    token_grad = call(
        functools.partial(token_grad_kernel, p), shape(blk, p.channels), received, name="token_grad"
    )
    grad_filter, sum_value, sum_gate = call(
        functools.partial(finish_filter_kernel, p),
        [
            shape(blk, p.channels),
            shape(3, p.channels, dtype=F32),
            shape(3, p.channels, dtype=F32),
        ],
        *rows,
        name="finish_filter",
    )
    factor_grads, token_grad, grad_filter, sum_value, sum_gate = lax.optimization_barrier(
        (factor_grads, token_grad, grad_filter, sum_value, sum_gate)
    )
    sums = call(
        functools.partial(sum_kernel, p), shape(p.mrows, blk), *factor_grads, name="sum_sources"
    )
    grad_one, grad_four, *small = call(
        functools.partial(finish_factors_kernel, p),
        [shape(2, blk, blk)] * 2
        + ([shape(2, pairs, p.kloc)] * 2 if p.direct else [shape(2, p.yrows, blk)]),
        *gathered_at_once(summed_over_groups(sums)),
        name="finish_factors",
    )
    if p.direct:
        small = [f.reshape(2, p.nblk, p.nblk, p.kloc).transpose(0, 3, 1, 2) for f in small]
    else:
        small = small[0].reshape(2, p.kloc, 2, p.nblk, p.nblk)
        small = [small[:, :, 0], small[:, :, 1]]
    return (
        token_grad[None],
        sum_value,
        sum_gate,
        grad_one.reshape(mix_one.shape),
        *small,
        grad_four.reshape(mix_four.shape),
        grad_filter.reshape(filter_log.shape),
    )


def solution(mesh):
    return jax.shard_map(
        shards,
        mesh=mesh,
        in_specs=(
            P("dp", "seq", None),
            P("dp", "seq", None),
            P(),
            P(),
            P(None, "seq", None, None),
            P(None, "seq", None, None),
            P(None, "seq", None, None),
            P(None, "seq", None, None),
            P("seq", None, None),
        ),
        out_specs=(
            P("dp", "seq", None),
            P(),
            P(),
            P(None, "seq", None, None),
            P(None, "seq", None, None),
            P(None, "seq", None, None),
            P(None, "seq", None, None),
            P("seq", None, None),
        ),
        check_vma=False,
    )
```
